128 devices in a mesh: gx: 8 (over x_lo, z), gy: 4 (over x_hi, core), gz: 4 (over y).
Axes of the slice: x: 4 (x_hi: 2, x_lo: 2; x = x_hi * 2 + x_lo), y: 4, z: 4, core: 2. Of those that a mesh axis runs over, the one named last changes fastest.
Arguments:
- implicit_source: float32 [2, 64, 128, 512], P(None, 'gz', 'gx', 'gy'), may hold values from -6 to 6
- capacity: float32 [2, 64, 128, 512], P(None, 'gz', 'gx', 'gy'), may hold values from 0.02 to 0.5
- transfer_coefficient: float32 [64, 128, 512], P('gz', 'gx', 'gy'), may hold values from 0.05 to 2
- observed_state_vector: float32 [2, 64, 128, 512], P(None, 'gz', 'gx', 'gy'), may hold values from -6 to 6
- soil_class: int32 [64, 128, 512], P('gz', 'gx', 'gy'), may hold values from 0 to 11
- conductivity: float32 [2, 12], replicated, may hold values from 0.2 to 4
- filter_rates: float32 [3, 2, 12], replicated, may hold values from 0.004 to 0.5
Outputs:
- predicted_state: float32 [2, 64, 128, 512], P(None, 'gz', 'gx', 'gy')
- analysis: float32 [2, 64, 128, 512], P(None, 'gz', 'gx', 'gy')
The draws below stay inside these ranges and needn't reach their ends.
All inputs are finite; a program needn't handle non-finite values.
Results may differ from the reference program's by a relative error of at most 0.00002.
Values sent between devices are 32-bit elements; how exact they have to be, the bound alone decides.
No kernel may reach another device: no remote copies, remote signals or barrier semaphores. Data moves between devices by JAX's collectives and lax.ppermute only.
A program may use at most 64 MiB of HBM per device.

```python
import math
import jax
import jax.numpy as jnp
from jax import lax

JACOBI_PASSES = 8
CLASSES = 12
NX = 128
NY = 512
NZ = 64


def touch_ends(values, stream_key, least, high):
    shape = values.shape
    spot = [jax.random.randint(jax.random.fold_in(stream_key, axis), (), 0, shape[axis]) for axis in range(len(shape))]
    values = values.at[tuple(spot)].set(least)
    longest = shape.index(max(shape))
    spot[longest] = (spot[longest] + 1) % shape[longest]
    return values.at[tuple(spot)].set(high)


def block_scale(rng, shape, cuts, smallest, largest):
    def one(axis_at, shards_of):
        steps = jax.random.uniform(jax.random.fold_in(jax.random.fold_in(rng, 6), axis_at), (shards_of,), jnp.float32, smallest / len(cuts), largest / len(cuts))
        return jnp.repeat(jnp.exp(steps), shape[axis_at] // shards_of).reshape((-1,) + (1,) * (len(shape) - axis_at - 1))

    level = one(*cuts[0])
    for cut in cuts[1:]:
        level = level * one(*cut)
    return level


def normal_values(stream_key, dims, deviation, most, cuts=(), kind=jnp.bfloat16):
    values = jax.random.normal(stream_key, dims, jnp.float32) * deviation
    if len(cuts) > 0:
        values = block_scale(stream_key, dims, cuts, -0.22, 0.18) * values
    return jnp.clip(values, min=-most, max=most).astype(kind)


def setup_inputs(seed: int = 0) -> dict:
    key_list = jax.random.split(jax.random.key(seed), 8)
    implicit_source = normal_values(key_list[0], (2, NZ, NX, NY), 1.0, 6.0, ((1, 4), (2, 8), (3, 4)), jnp.float32)
    capacity = jnp.clip(jnp.exp(math.log(0.5) - 3.218876 * jax.random.uniform(key_list[1], (2, NZ, NX, NY), jnp.float32) ** block_scale(key_list[1], (2, NZ, NX, NY), ((1, 4), (2, 8), (3, 4)), -0.2, 0.2)), 0.02, 0.5)
    transfer_coefficient = jnp.clip(jnp.exp(math.log(2.0) - 3.6888794 * jax.random.uniform(key_list[2], (NZ, NX, NY), jnp.float32) ** block_scale(key_list[2], (NZ, NX, NY), ((0, 4), (1, 8), (2, 4)), -0.2, 0.2)), 0.05, 2.0)
    observed_state_vector = normal_values(key_list[3], (2, NZ, NX, NY), 1.0, 6.0, ((1, 4), (2, 8), (3, 4)), jnp.float32)
    soil_class = touch_ends(jax.random.randint(key_list[4], (NZ, NX, NY), 0, CLASSES), jax.random.fold_in(key_list[4], 1), 0, CLASSES - 1).astype(jnp.int32)
    conductivity = jnp.clip(jnp.exp(jax.random.uniform(key_list[5], (2, CLASSES), jnp.float32, math.log(0.2), math.log(4.0))), 0.2, 4.0)
    filter_rates = jnp.clip(jnp.exp(jax.random.uniform(key_list[6], (3, 2, CLASSES), jnp.float32, math.log(0.004), math.log(0.5))), 0.004, 0.5)
    return {"implicit_source": implicit_source, "capacity": capacity, "transfer_coefficient": transfer_coefficient, "observed_state_vector": observed_state_vector, "soil_class": soil_class, "conductivity": conductivity, "filter_rates": filter_rates}


def neighbour_total(values):
    bordered_grid = jnp.pad(values, ((0, 0), (1, 1), (1, 1), (1, 1)))
    summed = bordered_grid[:, 2:, 1:-1, 1:-1] + bordered_grid[:, :-2, 1:-1, 1:-1]
    summed = summed + bordered_grid[:, 1:-1, 2:, 1:-1] + bordered_grid[:, 1:-1, :-2, 1:-1]
    summed = summed + bordered_grid[:, 1:-1, 1:-1, 2:] + bordered_grid[:, 1:-1, 1:-1, :-2]
    return summed


def compose(earlier, latter):
    return (earlier[0] * latter[0], latter[0] * earlier[1] + latter[1])


def smoothing(values, weight_table, axis_dim):
    retain = 1.0 - weight_table
    for backward in (False, True):
        for order_step in range(4):
            values = lax.associative_scan(compose, (retain, weight_table * values), reverse=backward, axis=axis_dim)[1]
    return values


def reference(implicit_source, capacity, transfer_coefficient, observed_state_vector, soil_class, conductivity, filter_rates):
    hydraulic_transmissivity = conductivity[:, soil_class]
    principal_coefficients = capacity + 6.0 * hydraulic_transmissivity + transfer_coefficient[None]
    predicted_state = jnp.zeros_like(implicit_source)
    for repeat in range(JACOBI_PASSES):
        predicted_state = (implicit_source + hydraulic_transmissivity * neighbour_total(predicted_state) + transfer_coefficient[None] * predicted_state[::-1]) / principal_coefficients
    wetness_correction = observed_state_vector - predicted_state
    wetness_correction = smoothing(wetness_correction, filter_rates[0][:, soil_class], 2)
    wetness_correction = smoothing(wetness_correction, filter_rates[1][:, soil_class], 3)
    wetness_correction = smoothing(wetness_correction, filter_rates[2][:, soil_class], 1)
    return (predicted_state, wetness_correction)
```

```python
import jax
import jax.numpy as jnp
from jax import lax
from jax.experimental import pallas as pl
from jax.experimental.pallas import tpu as pltpu
from jax.sharding import PartitionSpec as P

SWEEPS = 8
DEEP = SWEEPS - 1
NEAR = DEEP - 1
CLASSES = 12
STEPS = 16
PLANES = STEPS + 2 * DEEP
F32 = jnp.float32
VMEM = pl.BlockSpec(memory_space=pltpu.VMEM)
SMEM = pl.BlockSpec(memory_space=pltpu.SMEM)


def call(body, outs, specs, scratch=(), flops=1000000):
    return pl.pallas_call(
        body,
        out_shape=[jax.ShapeDtypeStruct(shape, F32) for shape in outs],
        in_specs=specs,
        out_specs=[VMEM] * len(outs),
        scratch_shapes=[pltpu.VMEM(shape, F32) for shape in scratch],
        compiler_params=pltpu.CompilerParams(vmem_limit_bytes=40 * 1024 * 1024),
        cost_estimate=pl.CostEstimate(flops=flops, bytes_accessed=1000000, transcendentals=0),
    )


def picked(table, row, classes):
    value = jnp.full(classes.shape, table[row, 0], F32)
    for entry in range(1, CLASSES):
        value = jnp.where(classes == entry, table[row, entry], value)
    return value


def lanes(shape):
    return lax.broadcasted_iota(jnp.int32, shape, len(shape) - 1)


def first_mask(lane):
    return (lane % 14 < 7) & (lane < 84)


def last_mask(lane):
    return ((lane % 14 >= 7) & (lane < 70)) | (lane >= 121)


def coefficients_kernel(source, capacity, transfer, classes, conductivity, units, to_low, to_high, edges):
    def layer(z, _):
        transfer_z = transfer[z]
        classes_z = classes[z]
        lane = lanes(classes_z.shape)
        packed = jnp.zeros(classes_z.shape, F32)
        for f in range(2):
            conduct = picked(conductivity, f, classes_z)
            inverse = 1.0 / (capacity[f, z] + 6.0 * conduct + transfer_z)
            for unit, value in (
                (f, source[f, z] * inverse),
                (2 + f, conduct * inverse),
                (4 + f, transfer_z * inverse),
            ):
                units[unit, z] = value
                turned = pltpu.roll(value, 14 * unit, 1) if unit else value
                packed = jnp.where((lane - 14 * unit + 7 + 128) % 128 < 14, turned, packed)
        edges[z] = packed
        return 0

    lax.fori_loop(0, STEPS, layer, 0)

    def pair(z, _):
        upper, lower = (edges[z], edges[z + 8])
        lane = lanes(upper.shape)
        to_low[z] = jnp.where(first_mask(lane), upper, pltpu.roll(lower, 121, 1))
        to_high[z] = jnp.where(last_mask(lane), upper, pltpu.roll(lower, 7, 1))
        return 0

    lax.fori_loop(0, 8, pair, 0)


def face_rows():
    offset, rows = (0, [])
    for unit in range(7):
        count = DEEP if unit < 2 else NEAR
        rows.append((unit, offset, count))
        offset += count
    return rows, offset


def corner_rows():
    offset, rows = (0, [])
    for unit in range(7):
        for d in range(NEAR):
            count = NEAR - d if unit < 2 else NEAR - d - 1
            if count > 0:
                rows.append((unit, d, offset, count))
                offset += count
    return rows, -(-offset // 8) * 8


def halo_kernel(place, units, from_high, from_low, strips, z_low, z_high, x_low, x_high, ll, lh, hl, hh):
    has_low = place[1] > 0
    has_high = place[1] < place[4] - 1

    def pair(z, _):
        high = jnp.where(has_high, from_high[z], 0.0)
        low = jnp.where(has_low, from_low[z], 0.0)
        first = first_mask(lanes(high.shape))
        strips[z] = jnp.where(first, high, low)
        strips[z + 8] = jnp.where(first, pltpu.roll(high, 7, 1), pltpu.roll(low, 121, 1))
        return 0

    lax.fori_loop(0, 8, pair, 0)

    def read(unit, z, start, count):
        return strips[z, pl.ds(start, count)] if unit == 6 else units[unit, z, pl.ds(start, count)]

    for out, side in ((z_low, 0), (z_high, 1)):
        for d in range(DEEP):
            z = STEPS - 1 - d if side else d
            for unit in range(7):
                if d < NEAR:
                    out[unit * NEAR + d] = read(unit, z, 0, STEPS)
                elif unit < 2:
                    out[7 * NEAR + unit] = read(unit, z, 0, STEPS)

    def layer(z, _):
        for out, side in ((x_low, 0), (x_high, 1)):
            for unit, offset, count in face_rows()[0]:
                out[z, pl.ds(offset, count)] = read(unit, z, STEPS - count if side else 0, count)
        return 0

    lax.fori_loop(0, STEPS, layer, 0)
    for out, z_side, x_side in ((ll, 0, 0), (lh, 0, 1), (hl, 1, 0), (hh, 1, 1)):
        for unit, d, offset, count in corner_rows()[0]:
            z = STEPS - 1 - d if z_side else d
            out[pl.ds(offset, count)] = read(unit, z, STEPS - count if x_side else 0, count)


def forward(read_value, read_weight, state, write, count=4):
    for i in range(STEPS):
        for g in range(count):
            weight = read_weight(i, g)
            value = read_value(i, g)
            keep = 1.0 - weight
            for k in range(4):
                value = keep * state[g][k] + weight * value
                state[g][k] = value
            write(i, g, value)
    return state


def backward(read_value, read_weight, state, write, count=4):
    return forward(
        lambda i, g: read_value(STEPS - 1 - i, g),
        lambda i, g: read_weight(STEPS - 1 - i, g),
        state,
        lambda i, g, value: write(STEPS - 1 - i, g, value),
        count,
    )


def zeros(count=4):
    return [[jnp.zeros((8, 128), F32) for _ in range(4)] for _ in range(count)]


PAIRS = [(a, b) for a in range(4) for b in range(a, 4)]


def block_maps(read_weight, g):
    def step(i, carry):
        chain, sums = (list(carry[:4]), list(carry[4:]))
        weight = read_weight(i, g)
        keep = 1.0 - weight
        for k in range(1, 4):
            chain[k] = chain[k] + weight * chain[k - 1]
        scaled = [weight * value for value in chain]
        chain = [keep * value for value in chain]
        sums = [total + scaled[a] * chain[b] for total, (a, b) in zip(sums, PAIRS)]
        return tuple(chain + sums)

    zero = jnp.zeros((8, 128), F32)
    return lax.fori_loop(0, STEPS, step, (zero + 1.0,) + (zero,) * 13, unroll=4)


def pass_map(maps, state):
    return [sum(maps[k - m] * state[m] for m in range(k + 1)) for k in range(4)]


def coupling(maps, a, b):
    return maps[4 + PAIRS.index((min(a, b), max(a, b)))]


def couple(maps, state):
    return [sum(coupling(maps, k, 3 - m) * state[m] for m in range(4)) for k in range(4)]


def plus(left, right):
    return [a + b for a, b in zip(left, right)]


def chained(maps, ends, low, high):
    count = len(maps)
    lows = [low]
    for s in range(count):
        lows.append(plus(pass_map(maps[s], lows[s]), ends[s][:4]))
    highs = [high]
    for s in reversed(range(count)):
        highs.insert(0, plus(plus(pass_map(maps[s], highs[0]), couple(maps[s], lows[s])), ends[s][4:]))
    return lows, highs


def merged_maps(maps):
    chain, total = (list(maps[0][:4]), list(maps[0][4:]))
    for s in range(1, len(maps)):
        part = maps[s]
        half = [
            [sum(chain[i] * coupling(part, a - i, b) for i in range(a + 1)) for b in range(4)]
            for a in range(4)
        ]
        total = [
            value + sum(chain[j] * half[a][b - j] for j in range(b + 1))
            for value, (a, b) in zip(total, PAIRS)
        ]
        chain = [sum(part[k - m] * chain[m] for m in range(k + 1)) for k in range(4)]
    return chain + total


def maps_kernel(classes, rates, _, wx, wy, wz, mx, my, my_all, mz, by_x, turned):
    def by_layer(z, _):
        here = classes[z]
        for f in range(2):
            wz[f, z] = picked(rates, 4 + f, here)
        return 0

    lax.fori_loop(0, STEPS, by_layer, 0)

    def by_row(z, _):
        by_x[pl.ds(z, STEPS, stride=STEPS), :] = classes[z].astype(F32)
        return 0

    lax.fori_loop(0, STEPS, by_row, 0)

    def x_weights(i, _):
        here = by_x[pl.ds(pl.multiple_of(i * STEPS, 8), STEPS)]
        for f in range(2):
            wx[f, i] = picked(rates, f, here)
        return 0

    lax.fori_loop(0, STEPS, x_weights, 0)
    for h in range(2):
        turned[h] = by_x[128 * h : 128 * h + 128].T

    def y_weights(i, _):
        rows = pl.ds(pl.multiple_of(i * 8, 8), 8)
        for h in range(2):
            here = turned[h, rows]
            for f in range(2):
                wy[2 * f + h, rows] = picked(rates, 2 + f, here)
        return 0

    lax.fori_loop(0, STEPS, y_weights, 0)
    for g in range(4):
        part = pl.ds(8 * (g % 2), 8)
        for v, value in enumerate(block_maps(lambda i, g: wx[g // 2, i, part], g)):
            mx[v, pl.ds(8 * g, 8)] = value
        for v, value in enumerate(block_maps(lambda i, g: wz[g // 2, i, part], g)):
            mz[v, pl.ds(8 * g, 8)] = value
        for v, value in enumerate(block_maps(lambda i, g: wy[g, pl.ds(i, 8, stride=STEPS)], g)):
            my[v, pl.ds(8 * g, 8)] = value
    blocks = [[my[v, pl.ds(s, 4, stride=8)] for v in range(14)] for s in range(8)]
    for v, value in enumerate(merged_maps(blocks)):
        my_all[pl.ds(4 * v, 4)] = value


def sweep_kernel(
    place, units, strips, z_from_high, z_from_low, x_from_high, x_from_low, hh, hl, lh, ll, observed, wx, mx,
    predicted, increment, message,
    grid, side, even, odd, passed, ends,
):
    inside = slice(8, 8 + STEPS)
    has = {
        "x_low": place[0] > 0,
        "x_high": place[0] < place[3] - 1,
        "z_low": place[2] > 0,
        "z_high": place[2] < place[5] - 1,
    }

    def own(z, _):
        for unit in range(6):
            grid[unit, z + DEEP, inside] = units[unit, z]
        grid[6, z + DEEP, inside] = strips[z]
        for ref, name in ((x_from_high, "x_high"), (x_from_low, "x_low")):
            for unit, offset, count in face_rows()[0]:
                start = 8 + STEPS if name == "x_high" else 8 - count
                value = jnp.where(has[name], ref[z, pl.ds(offset, count)], 0.0)
                grid[unit, z + DEEP, pl.ds(start, count)] = value
        return 0

    lax.fori_loop(0, STEPS, own, 0)
    for ref, name in ((z_from_high, "z_high"), (z_from_low, "z_low")):
        for d in range(DEEP):
            z = DEEP + STEPS + d if name == "z_high" else DEEP - 1 - d
            for unit in range(7):
                if d < NEAR:
                    grid[unit, z, inside] = jnp.where(has[name], ref[unit * NEAR + d], 0.0)
                elif unit < 2:
                    grid[unit, z, inside] = jnp.where(has[name], ref[7 * NEAR + unit], 0.0)
    for ref, z_name, x_name in ((hh, "z_high", "x_high"), (hl, "z_high", "x_low"), (lh, "z_low", "x_high"), (ll, "z_low", "x_low")):
        valid = has[z_name] & has[x_name]
        for unit, d, offset, count in corner_rows()[0]:
            z = DEEP + STEPS + d if z_name == "z_high" else DEEP - 1 - d
            start = 8 + STEPS if x_name == "x_high" else 8 - count
            grid[unit, z, pl.ds(start, count)] = jnp.where(valid, ref[pl.ds(offset, count)], 0.0)

    def unpack(z, _):
        packed = grid[6, z]
        for unit in range(6):
            side[unit, z] = pltpu.roll(packed, 128 - 14 * unit, 1) if unit else packed
        return 0

    lax.fori_loop(0, PLANES, unpack, 0)

    def sweep(main_from, side_from, write):
        def layer(z, _):
            main = [main_from(f, z) for f in range(2)]
            edge = [side_from(f, z) for f in range(2)]
            lane = lanes(main[0].shape)
            new_main, new_edge = ([], [])
            for f in range(2):
                below = (pltpu.roll(main[f], 1, 1), pltpu.roll(edge[f], 1, 1))
                above = (pltpu.roll(main[f], 127, 1), pltpu.roll(edge[f], 127, 1))
                for i, (here, source) in enumerate(((main[f], main_from), (edge[f], side_from))):
                    total = source(f, z - 1) + source(f, z + 1)
                    total = total + (pltpu.roll(here, 1, 0) + pltpu.roll(here, 31, 0))
                    total = total + jnp.where(lane == 0, below[1 - i], below[i])
                    total = total + jnp.where(lane == 127, above[1 - i], above[i])
                    ref = side if i else grid
                    other = edge[1 - f] if i else main[1 - f]
                    new = ref[f, z] + ref[2 + f, z] * total + ref[4 + f, z] * other
                    (new_edge if i else new_main).append(new)
            write(z, new_main, new_edge)
            return 0

        return layer

    buffers = (even, odd)
    for s in range(2, SWEEPS + 1):
        reach = SWEEPS - s
        if s == 2:
            main_from, side_from = (lambda f, z: grid[f, z], lambda f, z: side[f, z])
        else:
            old = buffers[s % 2]
            main_from = lambda f, z, old=old: old[f, z]
            side_from = lambda f, z, old=old: old[2 + f, z]
        if s < SWEEPS:
            new = buffers[(s + 1) % 2]

            def write(z, new_main, new_edge, new=new):
                for f in range(2):
                    new[f, z] = new_main[f]
                    new[2 + f, z] = new_edge[f]
        else:

            def write(z, new_main, new_edge):
                for f in range(2):
                    value = new_main[f][inside]
                    predicted[f, z - DEEP] = value
                    change = observed[f, z - DEEP] - value
                    increment[f, pl.ds(z - DEEP, STEPS, stride=STEPS), :] = change

        lax.fori_loop(DEEP - reach, DEEP + STEPS + reach, sweep(main_from, side_from, write), 0)

    def weight(i, g):
        return wx[g // 2, i, pl.ds(8 * (g % 2), 8)]

    def put(i, g, value):
        passed[i, pl.ds(8 * g, 8)] = value

    def value(i, g):
        return increment[g // 2, pl.ds(STEPS * i + 8 * (g % 2), 8)]

    low = forward(value, weight, zeros(), put)
    high = backward(lambda i, g: passed[i, pl.ds(8 * g, 8)], weight, zeros(), lambda i, g, value: None)
    for g in range(4):
        for k in range(4):
            ends[k, pl.ds(8 * g, 8)] = low[g][k]
            ends[4 + k, pl.ds(8 * g, 8)] = high[g][k]
    for j in range(8):
        for v in range(22):
            rows = pl.ds(4 * j, 4)
            message[j, pl.ds(4 * v, 4)] = ends[v, rows] if v < 8 else mx[v - 8, rows]


def solve_kernel(gathered, inflow):
    parts = [[gathered[s, pl.ds(4 * v, 4)] for v in range(22)] for s in range(8)]
    zero = [jnp.zeros((4, 128), F32)] * 4
    lows, highs = chained([p[8:] for p in parts], [p[:8] for p in parts], zero, zero)
    for s in range(8):
        for k in range(4):
            inflow[s, pl.ds(4 * k, 4)] = lows[s][k]
            inflow[s, pl.ds(16 + 4 * k, 4)] = highs[s + 1][k]


def y_value(ref):
    return lambda i, g: ref[g, pl.ds(i, 8, stride=STEPS)]


def x_finish_kernel(increment, wx, inflow, wy, my, my_all, lines, ends, message, passed, start):
    for k in range(8):
        for j in range(8):
            start[k, pl.ds(4 * j, 4)] = inflow[j, pl.ds(4 * k, 4)]

    def weight(i, g):
        return wx[g // 2, i, pl.ds(8 * (g % 2), 8)]

    def value(i, g):
        return increment[g // 2, pl.ds(STEPS * i + 8 * (g % 2), 8)]

    def put(i, g, value):
        passed[g // 2, pl.ds(STEPS * i + 8 * (g % 2), 8)] = value

    def passed_value(i, g):
        return passed[g // 2, pl.ds(STEPS * i + 8 * (g % 2), 8)]

    low = [[start[k, pl.ds(8 * g, 8)] for k in range(4)] for g in range(4)]
    high = [[start[4 + k, pl.ds(8 * g, 8)] for k in range(4)] for g in range(4)]
    forward(value, weight, low, put)
    backward(passed_value, weight, high, put)
    for f in range(2):
        for h in range(2):
            lines[2 * f + h] = passed[f, pl.ds(128 * h, 128)].T

    def y_put(i, g, value):
        passed[g // 2, pl.ds(128 * (g % 2) + 8 * i, 8)] = value

    def y_passed(i, g):
        return passed[g // 2, pl.ds(128 * (g % 2) + 8 * i, 8)]

    low = forward(y_value(lines), y_value(wy), zeros(), y_put)
    high = backward(y_passed, y_value(wy), zeros(), lambda i, g, value: None)
    for g in range(4):
        for k in range(4):
            ends[k, pl.ds(8 * g, 8)] = low[g][k]
            ends[4 + k, pl.ds(8 * g, 8)] = high[g][k]
    maps = [[my[v, pl.ds(s, 4, stride=8)] for v in range(14)] for s in range(8)]
    block_ends = [[ends[v, pl.ds(s, 4, stride=8)] for v in range(8)] for s in range(8)]
    zero = [jnp.zeros((4, 128), F32)] * 4
    lows, highs = chained(maps, block_ends, zero, zero)
    for k in range(4):
        message[pl.ds(4 * k, 4)] = lows[8][k]
        message[pl.ds(16 + 4 * k, 4)] = highs[0][k]
    message[pl.ds(32, 56)] = my_all[...]


def own_inflow(position, count, maps, ends, zero):
    def keep(valid, state):
        return [jnp.where(valid, value, 0.0) for value in state]

    low = zero
    for s in range(count - 1, 0, -1):
        low = keep(position >= s, plus(pass_map(maps(s), low), ends(s)[:4]))
    right = [plus(pass_map(maps(0), low), ends(0)[:4])]
    for d in range(1, count - 1):
        right.append(plus(pass_map(maps(count - d), right[-1]), ends(count - d)[:4]))
    high = zero
    for d in range(count - 1, 0, -1):
        s = count - d
        state = plus(plus(pass_map(maps(s), high), couple(maps(s), right[d - 1])), ends(s)[4:])
        high = keep(position + d < count, state)
    return low, high


def y_finish_kernel(
    place, lines, wy, my, block_ends, own, back_1, back_2, back_3, wz, unsmoothed, message, passed, start, done, by_row
):
    refs = (own, back_1, back_2, back_3)
    low, high = own_inflow(
        place[1],
        4,
        lambda s: [refs[s][pl.ds(32 + 4 * v, 4)] for v in range(14)],
        lambda s: [refs[s][pl.ds(4 * v, 4)] for v in range(8)],
        [jnp.zeros((4, 128), F32)] * 4,
    )
    maps = [[my[v, pl.ds(s, 4, stride=8)] for v in range(14)] for s in range(8)]
    blocks = [[block_ends[v, pl.ds(s, 4, stride=8)] for v in range(8)] for s in range(8)]
    lows, highs = chained(maps, blocks, low, high)
    for s in range(8):
        for k in range(4):
            start[k, pl.ds(s, 4, stride=8), :] = lows[s][k]
            start[4 + k, pl.ds(s, 4, stride=8), :] = highs[s + 1][k]

    def put(i, g, value):
        passed[g // 2, pl.ds(128 * (g % 2) + 8 * i, 8)] = value

    def passed_value(i, g):
        return passed[g // 2, pl.ds(128 * (g % 2) + 8 * i, 8)]

    def put_line(i, g, value):
        done[g, pl.ds(i, 8, stride=STEPS), :] = value

    low = [[start[k, pl.ds(8 * g, 8)] for k in range(4)] for g in range(4)]
    high = [[start[4 + k, pl.ds(8 * g, 8)] for k in range(4)] for g in range(4)]
    forward(y_value(lines), y_value(wy), low, put)
    backward(passed_value, y_value(wy), high, put_line)
    for g in range(4):
        by_row[g // 2, pl.ds(128 * (g % 2), 128)] = done[g].T

    def value(i, g):
        return by_row[g // 2, pl.ds(i + 128 * (g % 2), 8, stride=STEPS)]

    def weight(i, g):
        return wz[g // 2, i, pl.ds(8 * (g % 2), 8)]

    for i in range(STEPS):
        for g in range(4):
            unsmoothed[g // 2, i, pl.ds(8 * (g % 2), 8)] = value(i, g)

    low = forward(value, weight, zeros(), put)
    high = backward(passed_value, weight, zeros(), lambda i, g, value: None)
    for g in range(4):
        for k in range(4):
            message[k, pl.ds(8 * g, 8)] = low[g][k]
            message[4 + k, pl.ds(8 * g, 8)] = high[g][k]


def z_finish_kernel(
    place, unsmoothed, wz, maps_0, maps_1, maps_2, maps_3, ends_0, ends_1, ends_2, ends_3, smoothed, passed
):
    maps = (maps_0, maps_1, maps_2, maps_3)
    ends = (ends_0, ends_1, ends_2, ends_3)
    lows, highs = ([], [])
    for g in range(4):
        rows = pl.ds(8 * g, 8)
        low, high = own_inflow(
            place[2],
            4,
            lambda s: [maps[s][v, rows] for v in range(14)],
            lambda s: [ends[s][v, rows] for v in range(8)],
            [jnp.zeros((8, 128), F32)] * 4,
        )
        lows.append(low)
        highs.append(high)

    def value(i, g):
        return unsmoothed[g // 2, i, pl.ds(8 * (g % 2), 8)]

    def weight(i, g):
        return wz[g // 2, i, pl.ds(8 * (g % 2), 8)]

    def put(i, g, value):
        passed[g // 2, i, pl.ds(8 * (g % 2), 8)] = value

    def put_last(i, g, value):
        smoothed[g // 2, i, pl.ds(8 * (g % 2), 8)] = value

    forward(value, weight, lows, put)
    backward(lambda i, g: passed[g // 2, i, pl.ds(8 * (g % 2), 8)], weight, highs, put_last)


def turned_by(value, axis, step):
    count = lax.axis_size(axis)
    return lax.ppermute(value, axis, [(i, (i + step) % count) for i in range(count)])


def turned_both(value, x_step, z_step):
    nx, nz = (lax.axis_size("gx"), lax.axis_size("gz"))
    moves = [
        (x * nz + z, (x + x_step) % nx * nz + (z + z_step) % nz) for x in range(nx) for z in range(nz)
    ]
    return lax.ppermute(value, ("gx", "gz"), moves)


def local(source, capacity, transfer, observed, classes, conductivity, filter_rates):
    axes = ("gx", "gy", "gz")
    place = jnp.stack([lax.axis_index(a) for a in axes] + [jnp.int32(lax.axis_size(a)) for a in axes])
    rates = filter_rates.reshape(6, CLASSES)
    plane = (STEPS, STEPS, 128)
    units, to_low, to_high, _ = call(
        coefficients_kernel, [(6,) + plane, (8, STEPS, 128), (8, STEPS, 128), plane], [VMEM] * 4 + [SMEM]
    )(source, capacity, transfer, classes, conductivity)
    from_high = turned_by(to_low, "gy", -1)
    from_low = turned_by(to_high, "gy", 1)

    z_face = (7 * NEAR + 2, STEPS, 128)
    x_face = (STEPS, face_rows()[1], 128)
    corner = (corner_rows()[1], 128)
    strips, z_low, z_high, x_low, x_high, ll, lh, hl, hh = call(
        halo_kernel, [plane, z_face, z_face, x_face, x_face] + [corner] * 4, [SMEM] + [VMEM] * 3
    )(place, units, from_high, from_low)
    z_from_high = turned_by(z_low, "gz", -1)
    z_from_low = turned_by(z_high, "gz", 1)
    x_from_high = turned_by(x_low, "gx", -1)
    x_from_low = turned_by(x_high, "gx", 1)
    from_hh = turned_both(ll, -1, -1)
    from_hl = turned_both(lh, 1, -1)
    from_lh = turned_both(hl, -1, 1)
    from_ll = turned_both(hh, 1, 1)

    rows = (32, 128)
    wx, wy, wz, mx, my, my_all, mz, _, _ = call(
        maps_kernel,
        [(2,) + plane, (4, 128, 128), (2,) + plane, (14,) + rows, (14,) + rows, (56, 128), (14,) + rows,
         (256, 128), (2, 128, 128)],
        [VMEM, SMEM, VMEM],
    )(classes, rates, ll)
    z_maps = [mz] + [turned_by(mz, "gz", s) for s in (1, 2, 3)]

    padded = (PLANES, 32, 128)
    predicted, increment, message = call(
        sweep_kernel,
        [(2,) + plane, (2, 256, 128), (8, 88, 128)],
        [SMEM] + [VMEM] * 13,
        [(7,) + padded, (6,) + padded, (4,) + padded, (4,) + padded, (STEPS,) + rows, (8,) + rows],
        flops=100000000,
    )(place, units, strips, z_from_high, z_from_low, x_from_high, x_from_low, from_hh, from_hl, from_lh, from_ll,
      observed, wx, mx)
    gathered = lax.all_to_all(message, "gx", 0, 0, tiled=True)
    inflow, = call(solve_kernel, [(8, 32, 128)], [VMEM])(gathered)
    inflow = lax.all_to_all(inflow, "gx", 0, 0, tiled=True)
    lines, block_ends, y_ends = call(
        x_finish_kernel,
        [(4, 128, 128), (8,) + rows, (88, 128)],
        [VMEM] * 6,
        [(2, 256, 128), (8,) + rows],
    )(increment, wx, inflow, wy, my, my_all)
    y_all = [y_ends] + [turned_by(y_ends, "gy", s) for s in (1, 2, 3)]
    unsmoothed, z_ends = call(
        y_finish_kernel,
        [(2,) + plane, (8,) + rows],
        [SMEM] + [VMEM] * 9,
        [(2, 256, 128), (8,) + rows, (4, 128, 128), (2, 256, 128)],
    )(place, lines, wy, my, block_ends, *y_all, wz)
    z_all = [z_ends] + [turned_by(z_ends, "gz", s) for s in (1, 2, 3)]
    smoothed, = call(z_finish_kernel, [(2,) + plane], [SMEM] + [VMEM] * 10, [(2,) + plane])(
        place, unsmoothed, wz, *z_maps, *z_all
    )
    return (predicted, smoothed)


def solution(mesh):
    cells = P(None, "gz", "gx", "gy")
    return jax.shard_map(
        local,
        mesh=mesh,
        in_specs=(cells, cells, P("gz", "gx", "gy"), cells, P("gz", "gx", "gy"), P(), P()),
        out_specs=(cells, cells),
        check_vma=False,
    )
```

```python
import jax
import jax.numpy as jnp
from jax import lax
from jax.experimental import pallas as pl
from jax.experimental.pallas import tpu as pltpu
from jax.sharding import PartitionSpec as P

SWEEPS = 8
DEEP = SWEEPS - 1
NEAR = DEEP - 1
CLASSES = 12
STEPS = 16
PLANES = STEPS + 2 * DEEP
F32 = jnp.float32
VMEM = pl.BlockSpec(memory_space=pltpu.VMEM)
SMEM = pl.BlockSpec(memory_space=pltpu.SMEM)
HBM = pl.BlockSpec(memory_space=pltpu.HBM)


def call(body, outs, specs, scratch=(), flops=1000000, limit=4, copies=0):
    return pl.pallas_call(
        body,
        out_shape=[shape if hasattr(shape, "dtype") else jax.ShapeDtypeStruct(shape, F32) for shape in outs],
        in_specs=specs,
        out_specs=[VMEM] * len(outs),
        scratch_shapes=[
            pltpu.VMEM(shape, F32) for shape in scratch
        ]
        + [pltpu.SemaphoreType.DMA((copies,))] * (copies > 0),
        compiler_params=pltpu.CompilerParams(vmem_limit_bytes=limit * 1024 * 1024),
        cost_estimate=pl.CostEstimate(flops=flops, bytes_accessed=1000000, transcendentals=0),
    )


def picked(table, row, classes):
    value = jnp.full(classes.shape, table[row, 0], F32)
    for entry in range(1, CLASSES):
        value = jnp.where(classes == entry, table[row, entry], value)
    return value


def lanes(shape):
    return lax.broadcasted_iota(jnp.int32, shape, len(shape) - 1)


def first_mask(lane):
    return (lane % 14 < 7) & (lane < 84)


def last_mask(lane):
    return ((lane % 14 >= 7) & (lane < 70)) | (lane >= 121)


def by_pairs(place, axis, low, high):
    is_even = place[axis] % 2 == 0
    return jnp.where(is_even, high, low), jnp.where(is_even, low, high)


def sides(place, axis, even, odd):
    high, low = by_pairs(place, axis, odd, even)
    return (
        jnp.where(place[axis] > 0, low, 0.0),
        jnp.where(place[axis] < place[axis + 3] - 1, high, 0.0),
    )


def brought(pairs, sems):
    copies = [pltpu.make_async_copy(a, b, sems.at[i]) for i, (a, b) in enumerate(pairs)]
    for copy in copies:
        copy.start()
    for copy in copies:
        copy.wait()


def coefficients_kernel(
    place, source_in, capacity_in, transfer_in, classes_in, conductivity,
    units, even, odd, classes,
    edges, source, capacity, transfer, sems,
):
    brought(((source_in, source), (capacity_in, capacity), (transfer_in, transfer), (classes_in, classes)), sems)

    def layer(z, _):
        transfer_z = transfer[z]
        classes_z = classes[z]
        lane = lanes(classes_z.shape)
        packed = jnp.zeros(classes_z.shape, F32)
        for f in range(2):
            conduct = picked(conductivity, f, classes_z)
            inverse = 1.0 / (capacity[f, z] + 6.0 * conduct + transfer_z)
            for unit, value in (
                (f, source[f, z] * inverse),
                (2 + f, conduct * inverse),
                (4 + f, transfer_z * inverse),
            ):
                units[unit, z] = value
                turned = pltpu.roll(value, 14 * unit, 1) if unit else value
                packed = jnp.where((lane - 14 * unit + 7 + 128) % 128 < 14, turned, packed)
        edges[z] = packed
        return 0

    lax.fori_loop(0, STEPS, layer, 0, unroll=4)

    def pair(z, _):
        upper, lower = (edges[z], edges[z + 8])
        lane = lanes(upper.shape)
        to_low = jnp.where(first_mask(lane), upper, pltpu.roll(lower, 121, 1))
        to_high = jnp.where(last_mask(lane), upper, pltpu.roll(lower, 7, 1))
        even[z], odd[z] = by_pairs(place, 1, to_low, to_high)
        return 0

    lax.fori_loop(0, 8, pair, 0, unroll=4)


def face_rows():
    offset, rows = (0, [])
    for unit in range(7):
        count = DEEP if unit < 2 else NEAR
        rows.append((unit, offset, count))
        offset += count
    return rows, offset


def corner_rows():
    offset, rows = (0, [])
    for unit in range(7):
        for d in range(NEAR):
            count = NEAR - d if unit < 2 else NEAR - d - 1
            if count > 0:
                rows.append((unit, d, offset, count))
                offset += count
    return rows, -(-offset // 8) * 8


def halo_kernel(place, units, y_even, y_odd, strips, z_even, z_odd, x_even, x_odd):
    def pair(z, _):
        low, high = sides(place, 1, y_even[z], y_odd[z])
        first = first_mask(lanes(high.shape))
        strips[z] = jnp.where(first, high, low)
        strips[z + 8] = jnp.where(first, pltpu.roll(high, 7, 1), pltpu.roll(low, 121, 1))
        return 0

    lax.fori_loop(0, 8, pair, 0, unroll=4)

    def read(unit, z, start, count):
        return strips[z, pl.ds(start, count)] if unit == 6 else units[unit, z, pl.ds(start, count)]

    for d in range(DEEP):
        for unit in range(7 if d < NEAR else 2):
            at = unit * NEAR + d if d < NEAR else 7 * NEAR + unit
            z_even[at], z_odd[at] = by_pairs(
                place, 2, read(unit, d, 0, STEPS), read(unit, STEPS - 1 - d, 0, STEPS)
            )

    def layer(z, _):
        for unit, offset, count in face_rows()[0]:
            even, odd = by_pairs(place, 0, read(unit, z, 0, count), read(unit, z, STEPS - count, count))
            x_even[z, pl.ds(offset, count)] = even
            x_odd[z, pl.ds(offset, count)] = odd
        return 0

    lax.fori_loop(0, STEPS, layer, 0, unroll=2)


def corner_kernel(place, x_even, x_odd, even, odd):
    spans = {unit: (offset, count) for unit, offset, count in face_rows()[0]}
    for unit, d, offset, count in corner_rows()[0]:
        first, span = spans[unit]
        ends = []
        for z in (d, STEPS - 1 - d):
            low = sides(place, 0, x_even[z, pl.ds(first + span - count, count)], x_odd[z, pl.ds(first + span - count, count)])[0]
            high = sides(place, 0, x_even[z, pl.ds(first, count)], x_odd[z, pl.ds(first, count)])[1]
            ends.append((low, high))
        for x_side in range(2):
            to_even, to_odd = by_pairs(place, 2, ends[0][x_side], ends[1][x_side])
            even[x_side, pl.ds(offset, count)] = to_even
            odd[x_side, pl.ds(offset, count)] = to_odd


def forward(read_value, read_weight, state, write, count=4):
    for i in range(STEPS):
        for g in range(count):
            weight = read_weight(i, g)
            value = read_value(i, g)
            keep = 1.0 - weight
            for k in range(4):
                value = keep * state[g][k] + weight * value
                state[g][k] = value
            write(i, g, value)
    return state


def backward(read_value, read_weight, state, write, count=4):
    return forward(
        lambda i, g: read_value(STEPS - 1 - i, g),
        lambda i, g: read_weight(STEPS - 1 - i, g),
        state,
        lambda i, g, value: write(STEPS - 1 - i, g, value),
        count,
    )


def zeros(count=4):
    return [[jnp.zeros((8, 128), F32) for _ in range(4)] for _ in range(count)]


PAIRS = [(a, b) for a in range(4) for b in range(a, 4)]


def block_maps(read_weights):
    def step(i, carries):
        out = []
        for read_weight, carry in zip(read_weights, carries):
            chain, sums = (list(carry[:4]), list(carry[4:]))
            weight = read_weight(i)
            keep = 1.0 - weight
            for k in range(1, 4):
                chain[k] = chain[k] + weight * chain[k - 1]
            scaled = [weight * value for value in chain]
            chain = [keep * value for value in chain]
            sums = [total + scaled[a] * chain[b] for total, (a, b) in zip(sums, PAIRS)]
            out.append(tuple(chain + sums))
        return tuple(out)

    zero = jnp.zeros((8, 128), F32)
    start = (zero + 1.0,) + (zero,) * 13
    return lax.fori_loop(0, STEPS, step, (start,) * len(read_weights), unroll=4)


def pass_map(maps, state):
    return [sum(maps[k - m] * state[m] for m in range(k + 1)) for k in range(4)]


def coupling(maps, a, b):
    return maps[4 + PAIRS.index((min(a, b), max(a, b)))]


def couple(maps, state):
    return [sum(coupling(maps, k, 3 - m) * state[m] for m in range(4)) for k in range(4)]


def plus(left, right):
    return [a + b for a, b in zip(left, right)]


def chained(maps, ends, low, high):
    count = len(maps)
    lows = [low]
    for s in range(count):
        lows.append(plus(pass_map(maps[s], lows[s]), ends[s][:4]))
    highs = [high]
    for s in reversed(range(count)):
        highs.insert(0, plus(plus(pass_map(maps[s], highs[0]), couple(maps[s], lows[s])), ends[s][4:]))
    return lows, highs


def merged_maps(maps):
    chain, total = (list(maps[0][:4]), list(maps[0][4:]))
    for s in range(1, len(maps)):
        part = maps[s]
        half = [
            [sum(chain[i] * coupling(part, a - i, b) for i in range(a + 1)) for b in range(4)]
            for a in range(4)
        ]
        total = [
            value + sum(chain[j] * half[a][b - j] for j in range(b + 1))
            for value, (a, b) in zip(total, PAIRS)
        ]
        chain = [sum(part[k - m] * chain[m] for m in range(k + 1)) for k in range(4)]
    return chain + total


def maps_kernel(classes, rates, _, wx, wy, wz, mx, my, my_all, mz, by_x, turned):
    def by_layer(z, _):
        here = classes[z]
        for f in range(2):
            wz[f, z] = picked(rates, 4 + f, here)
        return 0

    lax.fori_loop(0, STEPS, by_layer, 0, unroll=4)

    def by_row(z, _):
        by_x[pl.ds(z, STEPS, stride=STEPS), :] = classes[z].astype(F32)
        return 0

    lax.fori_loop(0, STEPS, by_row, 0, unroll=4)

    def x_weights(i, _):
        here = by_x[pl.ds(pl.multiple_of(i * STEPS, 8), STEPS)]
        for f in range(2):
            wx[f, i] = picked(rates, f, here)
        return 0

    lax.fori_loop(0, STEPS, x_weights, 0, unroll=4)
    for h in range(2):
        turned[h] = by_x[128 * h : 128 * h + 128].T

    def y_weights(i, _):
        rows = pl.ds(pl.multiple_of(i * 8, 8), 8)
        for h in range(2):
            here = turned[h, rows]
            for f in range(2):
                wy[2 * f + h, rows] = picked(rates, 2 + f, here)
        return 0

    lax.fori_loop(0, STEPS, y_weights, 0, unroll=4)
    for g in range(4):
        part = pl.ds(8 * (g % 2), 8)
        weights = (
            lambda i, g=g: wx[g // 2, i, part],
            lambda i, g=g: wz[g // 2, i, part],
            lambda i, g=g: wy[g, pl.ds(i, 8, stride=STEPS)],
        )
        for out, maps in zip((mx, mz, my), block_maps(weights)):
            for v in range(14):
                out[v, pl.ds(8 * g, 8)] = maps[v]
    blocks = [[my[v, pl.ds(s, 4, stride=8)] for v in range(14)] for s in range(8)]
    for v, value in enumerate(merged_maps(blocks)):
        my_all[pl.ds(4 * v, 4)] = value


def sweep_kernel(
    place, units, strips, z_even, z_odd, x_even, x_odd, corner_even, corner_odd, observed, wx, mx,
    predicted, increment, message,
    grid, side, even, odd, passed, ends,
):
    inside = slice(8, 8 + STEPS)

    def own(z, _):
        for unit in range(6):
            grid[unit, z + DEEP, inside] = units[unit, z]
        grid[6, z + DEEP, inside] = strips[z]
        for unit, offset, count in face_rows()[0]:
            rows = pl.ds(offset, count)
            low, high = sides(place, 0, x_even[z, rows], x_odd[z, rows])
            grid[unit, z + DEEP, pl.ds(8 - count, count)] = low
            grid[unit, z + DEEP, pl.ds(8 + STEPS, count)] = high
        return 0

    lax.fori_loop(0, STEPS, own, 0)
    for d in range(DEEP):
        for unit in range(7 if d < NEAR else 2):
            at = unit * NEAR + d if d < NEAR else 7 * NEAR + unit
            low, high = sides(place, 2, z_even[at], z_odd[at])
            grid[unit, DEEP - 1 - d, inside] = low
            grid[unit, DEEP + STEPS + d, inside] = high
    for unit, d, offset, count in corner_rows()[0]:
        rows = pl.ds(offset, count)
        for x_side, start in enumerate((8 - count, 8 + STEPS)):
            low, high = sides(place, 2, corner_even[x_side, rows], corner_odd[x_side, rows])
            grid[unit, DEEP - 1 - d, pl.ds(start, count)] = low
            grid[unit, DEEP + STEPS + d, pl.ds(start, count)] = high

    def unpack(z, _):
        packed = grid[6, z]
        for unit in range(6):
            side[unit, z] = pltpu.roll(packed, 128 - 14 * unit, 1) if unit else packed
        return 0

    lax.fori_loop(0, PLANES, unpack, 0, unroll=5)

    def sweep(main_from, side_from, write):
        def layer(z, _):
            main = [main_from(f, z) for f in range(2)]
            edge = [side_from(f, z) for f in range(2)]
            lane = lanes(main[0].shape)
            new_main, new_edge = ([], [])
            for f in range(2):
                below = (pltpu.roll(main[f], 1, 1), pltpu.roll(edge[f], 1, 1))
                above = (pltpu.roll(main[f], 127, 1), pltpu.roll(edge[f], 127, 1))
                for i, (here, source) in enumerate(((main[f], main_from), (edge[f], side_from))):
                    total = source(f, z - 1) + source(f, z + 1)
                    total = total + (pltpu.roll(here, 1, 0) + pltpu.roll(here, 31, 0))
                    total = total + jnp.where(lane == 0, below[1 - i], below[i])
                    total = total + jnp.where(lane == 127, above[1 - i], above[i])
                    ref = side if i else grid
                    other = edge[1 - f] if i else main[1 - f]
                    new = ref[f, z] + ref[2 + f, z] * total + ref[4 + f, z] * other
                    (new_edge if i else new_main).append(new)
            write(z, new_main, new_edge)
            return 0

        return layer

    buffers = (even, odd)
    for s in range(2, SWEEPS + 1):
        reach = SWEEPS - s
        if s == 2:
            main_from, side_from = (lambda f, z: grid[f, z], lambda f, z: side[f, z])
        else:
            old = buffers[s % 2]
            main_from = lambda f, z, old=old: old[f, z]
            side_from = lambda f, z, old=old: old[2 + f, z]
        if s < SWEEPS:
            new = buffers[(s + 1) % 2]

            def write(z, new_main, new_edge, new=new):
                for f in range(2):
                    new[f, z] = new_main[f]
                    new[2 + f, z] = new_edge[f]
        else:

            def write(z, new_main, new_edge):
                for f in range(2):
                    value = new_main[f][inside]
                    predicted[f, z - DEEP] = value
                    change = observed[f, z - DEEP] - value
                    increment[f, pl.ds(z - DEEP, STEPS, stride=STEPS), :] = change

        lax.fori_loop(DEEP - reach, DEEP + STEPS + reach, sweep(main_from, side_from, write), 0, unroll=8)

    def weight(i, g):
        return wx[g // 2, i, pl.ds(8 * (g % 2), 8)]

    def put(i, g, value):
        passed[i, pl.ds(8 * g, 8)] = value

    def value(i, g):
        return increment[g // 2, pl.ds(STEPS * i + 8 * (g % 2), 8)]

    low = forward(value, weight, zeros(), put)
    high = backward(lambda i, g: passed[i, pl.ds(8 * g, 8)], weight, zeros(), lambda i, g, value: None)
    for g in range(4):
        for k in range(4):
            ends[k, pl.ds(8 * g, 8)] = low[g][k]
            ends[4 + k, pl.ds(8 * g, 8)] = high[g][k]
    for j in range(8):
        for v in range(22):
            rows = pl.ds(4 * j, 4)
            message[j, pl.ds(4 * v, 4)] = ends[v, rows] if v < 8 else mx[v - 8, rows]


def solve_kernel(gathered, inflow):
    parts = [[gathered[s, pl.ds(4 * v, 4)] for v in range(22)] for s in range(8)]
    zero = [jnp.zeros((4, 128), F32)] * 4
    lows, highs = chained([p[8:] for p in parts], [p[:8] for p in parts], zero, zero)
    for s in range(8):
        for k in range(4):
            inflow[s, pl.ds(4 * k, 4)] = lows[s][k]
            inflow[s, pl.ds(16 + 4 * k, 4)] = highs[s + 1][k]


def y_value(ref):
    return lambda i, g: ref[g, pl.ds(i, 8, stride=STEPS)]


def x_finish_kernel(increment, wx, inflow, wy, my, my_all, lines, ends, message, passed, start):
    for k in range(8):
        for j in range(8):
            start[k, pl.ds(4 * j, 4)] = inflow[j, pl.ds(4 * k, 4)]

    def weight(i, g):
        return wx[g // 2, i, pl.ds(8 * (g % 2), 8)]

    def value(i, g):
        return increment[g // 2, pl.ds(STEPS * i + 8 * (g % 2), 8)]

    def put(i, g, value):
        passed[g // 2, pl.ds(STEPS * i + 8 * (g % 2), 8)] = value

    def passed_value(i, g):
        return passed[g // 2, pl.ds(STEPS * i + 8 * (g % 2), 8)]

    low = [[start[k, pl.ds(8 * g, 8)] for k in range(4)] for g in range(4)]
    high = [[start[4 + k, pl.ds(8 * g, 8)] for k in range(4)] for g in range(4)]
    forward(value, weight, low, put)
    backward(passed_value, weight, high, put)
    for f in range(2):
        for h in range(2):
            lines[2 * f + h] = passed[f, pl.ds(128 * h, 128)].T

    def y_put(i, g, value):
        passed[g // 2, pl.ds(128 * (g % 2) + 8 * i, 8)] = value

    def y_passed(i, g):
        return passed[g // 2, pl.ds(128 * (g % 2) + 8 * i, 8)]

    low = forward(y_value(lines), y_value(wy), zeros(), y_put)
    high = backward(y_passed, y_value(wy), zeros(), lambda i, g, value: None)
    for g in range(4):
        for k in range(4):
            ends[k, pl.ds(8 * g, 8)] = low[g][k]
            ends[4 + k, pl.ds(8 * g, 8)] = high[g][k]
    maps = [[my[v, pl.ds(s, 4, stride=8)] for v in range(14)] for s in range(8)]
    block_ends = [[ends[v, pl.ds(s, 4, stride=8)] for v in range(8)] for s in range(8)]
    zero = [jnp.zeros((4, 128), F32)] * 4
    lows, highs = chained(maps, block_ends, zero, zero)
    for k in range(4):
        message[pl.ds(4 * k, 4)] = lows[8][k]
        message[pl.ds(16 + 4 * k, 4)] = highs[0][k]
    message[pl.ds(32, 56)] = my_all[...]


def own_inflow(position, count, maps, ends, zero, write):
    for p in range(count):

        @pl.when(position == p)
        def _(p=p):
            low = zero
            for j in range(p):
                low = plus(pass_map(maps(j ^ p), low), ends(j ^ p)[:4])
            inflow, lows = (low, [])
            for j in range(p, count):
                lows.append(inflow)
                if j < count - 1:
                    inflow = plus(pass_map(maps(j ^ p), inflow), ends(j ^ p)[:4])
            high = zero
            for j in range(count - 1, p, -1):
                coupled = couple(maps(j ^ p), lows[j - p])
                high = plus(plus(pass_map(maps(j ^ p), high), coupled), ends(j ^ p)[4:])
            write(low, high)


def y_finish_kernel(
    place, lines, wy, my, block_ends, own, xor_1, xor_2, xor_3, wz, unsmoothed, message,
    passed, start, done, by_row, inflow,
):
    refs = (own, xor_1, xor_2, xor_3)

    def write(low, high):
        for k in range(4):
            inflow[k, pl.ds(0, 4)] = low[k]
            inflow[4 + k, pl.ds(0, 4)] = high[k]

    own_inflow(
        place[1],
        4,
        lambda s: [refs[s][pl.ds(32 + 4 * v, 4)] for v in range(14)],
        lambda s: [refs[s][pl.ds(4 * v, 4)] for v in range(8)],
        [jnp.zeros((4, 128), F32)] * 4,
        write,
    )
    low = [inflow[k, pl.ds(0, 4)] for k in range(4)]
    high = [inflow[4 + k, pl.ds(0, 4)] for k in range(4)]
    maps = [[my[v, pl.ds(s, 4, stride=8)] for v in range(14)] for s in range(8)]
    blocks = [[block_ends[v, pl.ds(s, 4, stride=8)] for v in range(8)] for s in range(8)]
    lows, highs = chained(maps, blocks, low, high)
    for s in range(8):
        for k in range(4):
            start[k, pl.ds(s, 4, stride=8), :] = lows[s][k]
            start[4 + k, pl.ds(s, 4, stride=8), :] = highs[s + 1][k]

    def put(i, g, value):
        passed[g // 2, pl.ds(128 * (g % 2) + 8 * i, 8)] = value

    def passed_value(i, g):
        return passed[g // 2, pl.ds(128 * (g % 2) + 8 * i, 8)]

    def put_line(i, g, value):
        done[g, pl.ds(i, 8, stride=STEPS), :] = value

    low = [[start[k, pl.ds(8 * g, 8)] for k in range(4)] for g in range(4)]
    high = [[start[4 + k, pl.ds(8 * g, 8)] for k in range(4)] for g in range(4)]
    forward(y_value(lines), y_value(wy), low, put)
    backward(passed_value, y_value(wy), high, put_line)
    for g in range(4):
        by_row[g // 2, pl.ds(128 * (g % 2), 128)] = done[g].T

    def value(i, g):
        return by_row[g // 2, pl.ds(i + 128 * (g % 2), 8, stride=STEPS)]

    def weight(i, g):
        return wz[g // 2, i, pl.ds(8 * (g % 2), 8)]

    for i in range(STEPS):
        for g in range(4):
            unsmoothed[g // 2, i, pl.ds(8 * (g % 2), 8)] = value(i, g)

    low = forward(value, weight, zeros(), put)
    high = backward(passed_value, weight, zeros(), lambda i, g, value: None)
    for g in range(4):
        for k in range(4):
            message[k, pl.ds(8 * g, 8)] = low[g][k]
            message[4 + k, pl.ds(8 * g, 8)] = high[g][k]


def z_finish_kernel(
    place, unsmoothed, wz, maps_0, maps_1, maps_2, maps_3, ends_0, ends_1, ends_2, ends_3, smoothed, passed, inflow
):
    maps = (maps_0, maps_1, maps_2, maps_3)
    ends = (ends_0, ends_1, ends_2, ends_3)
    for g in range(4):
        rows = pl.ds(8 * g, 8)

        def write(low, high, rows=rows):
            for k in range(4):
                inflow[k, rows] = low[k]
                inflow[4 + k, rows] = high[k]

        own_inflow(
            place[2],
            4,
            lambda s, rows=rows: [maps[s][v, rows] for v in range(14)],
            lambda s, rows=rows: [ends[s][v, rows] for v in range(8)],
            [jnp.zeros((8, 128), F32)] * 4,
            write,
        )
    lows = [[inflow[k, pl.ds(8 * g, 8)] for k in range(4)] for g in range(4)]
    highs = [[inflow[4 + k, pl.ds(8 * g, 8)] for k in range(4)] for g in range(4)]

    def value(i, g):
        return unsmoothed[g // 2, i, pl.ds(8 * (g % 2), 8)]

    def weight(i, g):
        return wz[g // 2, i, pl.ds(8 * (g % 2), 8)]

    def put(i, g, value):
        passed[g // 2, i, pl.ds(8 * (g % 2), 8)] = value

    def put_last(i, g, value):
        smoothed[g // 2, i, pl.ds(8 * (g % 2), 8)] = value

    forward(value, weight, lows, put)
    backward(lambda i, g: passed[g // 2, i, pl.ds(8 * (g % 2), 8)], weight, highs, put_last)


def pair_swaps(axis, spare, value_even, value_odd):
    axes = tuple(sorted((axis, spare)))
    count, others = (lax.axis_size(axis), lax.axis_size(spare))

    def flat(i, k):
        return i * others + k if axis == axes[0] else k * count + i

    odd = []
    for i in range(count):
        for k in range(others):
            j = i + 1 if i % 2 else i - 1
            odd.append((flat(i, k), flat(j, k) if 0 <= j < count else flat(i, k ^ 1)))
    from_odd = lax.ppermute(value_odd, axes, odd)
    from_even = lax.ppermute(value_even, axis, [(i, i ^ 1) for i in range(count)])
    return from_even, from_odd


def xor_gather(value, axis):
    count = lax.axis_size(axis)
    return [value] + [lax.ppermute(value, axis, [(i, i ^ s) for i in range(count)]) for s in (3, 2, 1)][::-1]


def local(source, capacity, transfer, observed, classes, conductivity, filter_rates):
    axes = ("gx", "gy", "gz")
    place = jnp.stack([lax.axis_index(a) for a in axes] + [jnp.int32(lax.axis_size(a)) for a in axes])
    rates = filter_rates.reshape(6, CLASSES)
    plane = (STEPS, STEPS, 128)
    units, y_even, y_odd, classes = call(
        coefficients_kernel,
        [(6,) + plane, (8, STEPS, 128), (8, STEPS, 128), jax.ShapeDtypeStruct(plane, jnp.int32)],
        [SMEM] + [HBM] * 4 + [SMEM],
        [plane, (2,) + plane, (2,) + plane, plane],
        limit=60,
        copies=4,
    )(place, source, capacity, transfer, classes, conductivity)
    y_even, y_odd = pair_swaps("gy", "gz", y_even, y_odd)

    z_face = (7 * NEAR + 2, STEPS, 128)
    x_face = (STEPS, face_rows()[1], 128)
    corners = (2, corner_rows()[1], 128)
    strips, z_even, z_odd, x_even, x_odd = call(
        halo_kernel,
        [plane, z_face, z_face, x_face, x_face],
        [SMEM] + [VMEM] * 3,
        limit=60,
    )(place, units, y_even, y_odd)
    x_even, x_odd = pair_swaps("gx", "gy", x_even, x_odd)
    z_even, z_odd = pair_swaps("gz", "gy", z_even, z_odd)

    rows = (32, 128)
    wx, wy, wz, mx, my, my_all, mz, _, _ = call(
        maps_kernel,
        [(2,) + plane, (4, 128, 128), (2,) + plane, (14,) + rows, (14,) + rows, (56, 128), (14,) + rows,
         (256, 128), (2, 128, 128)],
        [VMEM, SMEM, VMEM],
        limit=60,
    )(classes, rates, strips)
    x_even, wx = lax.optimization_barrier((x_even, wx))
    corner_even, corner_odd = call(corner_kernel, [corners, corners], [SMEM] + [VMEM] * 2, limit=60)(place, x_even, x_odd)
    corner_even, corner_odd = pair_swaps("gz", "gy", corner_even, corner_odd)
    z_maps = xor_gather(mz, "gz")

    padded = (PLANES, 32, 128)
    predicted, increment, message = call(
        sweep_kernel,
        [(2,) + plane, (2, 256, 128), (8, 88, 128)],
        [SMEM] + [VMEM] * 11,
        [(7,) + padded, (6,) + padded, (4,) + padded, (4,) + padded, (STEPS,) + rows, (8,) + rows],
        flops=100000000,
        limit=60,
    )(place, units, strips, z_even, z_odd, x_even, x_odd, corner_even, corner_odd,
      observed, wx, mx)
    gathered = lax.all_to_all(message, "gx", 0, 0, tiled=True)
    inflow, = call(solve_kernel, [(8, 32, 128)], [VMEM])(gathered)
    inflow = lax.all_to_all(inflow, "gx", 0, 0, tiled=True)
    inflow, z_maps = lax.optimization_barrier((inflow, z_maps))
    lines, block_ends, y_ends = call(
        x_finish_kernel,
        [(4, 128, 128), (8,) + rows, (88, 128)],
        [VMEM] * 6,
        [(2, 256, 128), (8,) + rows],
    )(increment, wx, inflow, wy, my, my_all)
    y_all = xor_gather(y_ends, "gy")
    unsmoothed, z_ends = call(
        y_finish_kernel,
        [(2,) + plane, (8,) + rows],
        [SMEM] + [VMEM] * 9,
        [(2, 256, 128), (8,) + rows, (4, 128, 128), (2, 256, 128), (8, 8, 128)],
    )(place, lines, wy, my, block_ends, *y_all, wz)
    z_all = xor_gather(z_ends, "gz")
    smoothed, = call(z_finish_kernel, [(2,) + plane], [SMEM] + [VMEM] * 10, [(2,) + plane, (8,) + rows])(
        place, unsmoothed, wz, *z_maps, *z_all
    )
    return (predicted, smoothed)


def solution(mesh):
    cells = P(None, "gz", "gx", "gy")
    return jax.shard_map(
        local,
        mesh=mesh,
        in_specs=(cells, cells, P("gz", "gx", "gy"), cells, P("gz", "gx", "gy"), P(), P()),
        out_specs=(cells, cells),
        check_vma=False,
    )
```

```python
import jax
import jax.numpy as jnp
from jax import lax
from jax.experimental import pallas as pl
from jax.experimental.pallas import tpu as pltpu
from jax.sharding import PartitionSpec as P

SWEEPS = 8
DEEP = SWEEPS - 1
NEAR = DEEP - 1
CLASSES = 12
STEPS = 16
PLANES = STEPS + 2 * DEEP
F32 = jnp.float32
VMEM = pl.BlockSpec(memory_space=pltpu.VMEM)
SMEM = pl.BlockSpec(memory_space=pltpu.SMEM)
HBM = pl.BlockSpec(memory_space=pltpu.HBM)


def call(body, outs, specs, scratch=(), flops=1000000, limit=4, copies=0):
    return pl.pallas_call(
        body,
        out_shape=[shape if hasattr(shape, "dtype") else jax.ShapeDtypeStruct(shape, F32) for shape in outs],
        in_specs=specs,
        out_specs=[VMEM] * len(outs),
        scratch_shapes=[
            pltpu.VMEM(shape, F32) for shape in scratch
        ]
        + [pltpu.SemaphoreType.DMA((copies,))] * (copies > 0),
        compiler_params=pltpu.CompilerParams(vmem_limit_bytes=limit * 1024 * 1024),
        cost_estimate=pl.CostEstimate(flops=flops, bytes_accessed=1000000, transcendentals=0),
    )


def picked(table, row, classes):
    value = jnp.full(classes.shape, table[row, 0], F32)
    for entry in range(1, CLASSES):
        value = jnp.where(classes == entry, table[row, entry], value)
    return value


def lanes(shape):
    return lax.broadcasted_iota(jnp.int32, shape, len(shape) - 1)


def first_mask(lane):
    return (lane % 14 < 7) & (lane < 84)


def last_mask(lane):
    return ((lane % 14 >= 7) & (lane < 70)) | (lane >= 121)


def by_pairs(place, axis, low, high):
    is_even = place[axis] % 2 == 0
    return jnp.where(is_even, high, low), jnp.where(is_even, low, high)


def sides(place, axis, even, odd):
    high, low = by_pairs(place, axis, odd, even)
    return (
        jnp.where(place[axis] > 0, low, 0.0),
        jnp.where(place[axis] < place[axis + 3] - 1, high, 0.0),
    )


def brought(pairs, sems):
    copies = [pltpu.make_async_copy(a, b, sems.at[i]) for i, (a, b) in enumerate(pairs)]
    for copy in copies:
        copy.start()
    for copy in copies:
        copy.wait()


def coefficients_kernel(
    source_in, capacity_in, transfer_in, classes_in, conductivity,
    units, even, odd, classes,
    edges, source, capacity, transfer, sems,
):
    place = {1: lax.axis_index("gy")}
    brought(((source_in, source), (capacity_in, capacity), (transfer_in, transfer), (classes_in, classes)), sems)

    def layer(z, _):
        transfer_z = transfer[z]
        classes_z = classes[z]
        lane = lanes(classes_z.shape)
        packed = jnp.zeros(classes_z.shape, F32)
        for f in range(2):
            conduct = picked(conductivity, f, classes_z)
            inverse = 1.0 / (capacity[f, z] + 6.0 * conduct + transfer_z)
            for unit, value in (
                (f, source[f, z] * inverse),
                (2 + f, conduct * inverse),
                (4 + f, transfer_z * inverse),
            ):
                units[unit, z] = value
                turned = pltpu.roll(value, 14 * unit, 1) if unit else value
                packed = jnp.where((lane - 14 * unit + 7 + 128) % 128 < 14, turned, packed)
        edges[z] = packed
        return 0

    lax.fori_loop(0, STEPS, layer, 0, unroll=4)

    def pair(z, _):
        upper, lower = (edges[z], edges[z + 8])
        lane = lanes(upper.shape)
        to_low = jnp.where(first_mask(lane), upper, pltpu.roll(lower, 121, 1))
        to_high = jnp.where(last_mask(lane), upper, pltpu.roll(lower, 7, 1))
        even[z], odd[z] = by_pairs(place, 1, to_low, to_high)
        return 0

    lax.fori_loop(0, 8, pair, 0, unroll=4)


def face_rows():
    offset, rows = (0, [])
    for unit in range(7):
        count = DEEP if unit < 2 else NEAR
        rows.append((unit, offset, count))
        offset += count
    return rows, offset


def corner_rows():
    offset, rows = (0, [])
    for unit in range(7):
        for d in range(NEAR):
            count = NEAR - d if unit < 2 else NEAR - d - 1
            if count > 0:
                rows.append((unit, d, offset, count))
                offset += count
    return rows, -(-offset // 8) * 8


def face_kernel(place, units, z_even, z_odd, x_even, x_odd):
    for d in range(DEEP):
        for unit in range(6 if d < NEAR else 2):
            at = unit * NEAR + d if d < NEAR else 6 * NEAR + unit
            z_even[at], z_odd[at] = by_pairs(place, 2, units[unit, d], units[unit, STEPS - 1 - d])

    def layer(z, _):
        for unit, offset, count in face_rows()[0][:6]:
            low, high = (units[unit, z, pl.ds(0, count)], units[unit, z, pl.ds(STEPS - count, count)])
            even, odd = by_pairs(place, 0, low, high)
            x_even[z, pl.ds(offset, count)] = even
            x_odd[z, pl.ds(offset, count)] = odd
        return 0

    lax.fori_loop(0, STEPS, layer, 0, unroll=2)


def halo_kernel(
    place, y_odd, y_even, z_even_in, z_odd_in, x_even_in, x_odd_in, strips, z_even, z_odd, x_even, x_odd
):
    def pair(z, _):
        low, high = sides(place, 1, y_even[z], y_odd[z])
        first = first_mask(lanes(high.shape))
        strips[z] = jnp.where(first, high, low)
        strips[z + 8] = jnp.where(first, pltpu.roll(high, 7, 1), pltpu.roll(low, 121, 1))
        return 0

    lax.fori_loop(0, 8, pair, 0, unroll=4)
    for out, value in ((z_even, z_even_in), (z_odd, z_odd_in)):
        out[pl.ds(0, 6 * NEAR + 2)] = value[...]
    for d in range(NEAR):
        z_even[6 * NEAR + 2 + d], z_odd[6 * NEAR + 2 + d] = by_pairs(
            place, 2, strips[d], strips[STEPS - 1 - d]
        )

    def layer(z, _):
        _, offset, count = face_rows()[0][6]
        x_even[z, pl.ds(0, offset)] = x_even_in[z, pl.ds(0, offset)]
        x_odd[z, pl.ds(0, offset)] = x_odd_in[z, pl.ds(0, offset)]
        low, high = (strips[z, pl.ds(0, count)], strips[z, pl.ds(STEPS - count, count)])
        even, odd = by_pairs(place, 0, low, high)
        x_even[z, pl.ds(offset, count)] = even
        x_odd[z, pl.ds(offset, count)] = odd
        return 0

    lax.fori_loop(0, STEPS, layer, 0, unroll=4)


def corner_kernel(place, x_odd, x_even, _, even, odd):
    spans = {unit: (offset, count) for unit, offset, count in face_rows()[0]}
    for unit, d, offset, count in corner_rows()[0]:
        first, span = spans[unit]
        ends = []
        for z in (d, STEPS - 1 - d):
            low = sides(place, 0, x_even[z, pl.ds(first + span - count, count)], x_odd[z, pl.ds(first + span - count, count)])[0]
            high = sides(place, 0, x_even[z, pl.ds(first, count)], x_odd[z, pl.ds(first, count)])[1]
            ends.append((low, high))
        for x_side in range(2):
            to_even, to_odd = by_pairs(place, 2, ends[0][x_side], ends[1][x_side])
            even[x_side, pl.ds(offset, count)] = to_even
            odd[x_side, pl.ds(offset, count)] = to_odd


def forward(read_value, read_weight, state, write, count=4):
    for i in range(STEPS):
        for g in range(count):
            weight = read_weight(i, g)
            value = read_value(i, g)
            keep = 1.0 - weight
            for k in range(4):
                value = keep * state[g][k] + weight * value
                state[g][k] = value
            write(i, g, value)
    return state


def backward(read_value, read_weight, state, write, count=4):
    return forward(
        lambda i, g: read_value(STEPS - 1 - i, g),
        lambda i, g: read_weight(STEPS - 1 - i, g),
        state,
        lambda i, g, value: write(STEPS - 1 - i, g, value),
        count,
    )


def zeros(count=4):
    return [[jnp.zeros((8, 128), F32) for _ in range(4)] for _ in range(count)]


PAIRS = [(a, b) for a in range(4) for b in range(a, 4)]


def block_maps(read_weights):
    def step(i, carries):
        out = []
        for read_weight, carry in zip(read_weights, carries):
            chain, sums = (list(carry[:4]), list(carry[4:]))
            weight = read_weight(i)
            keep = 1.0 - weight
            for k in range(1, 4):
                chain[k] = chain[k] + weight * chain[k - 1]
            scaled = [weight * value for value in chain]
            chain = [keep * value for value in chain]
            sums = [total + scaled[a] * chain[b] for total, (a, b) in zip(sums, PAIRS)]
            out.append(tuple(chain + sums))
        return tuple(out)

    zero = jnp.zeros((8, 128), F32)
    start = (zero + 1.0,) + (zero,) * 13
    return lax.fori_loop(0, STEPS, step, (start,) * len(read_weights), unroll=4)


def pass_map(maps, state):
    return [sum(maps[k - m] * state[m] for m in range(k + 1)) for k in range(4)]


def coupling(maps, a, b):
    return maps[4 + PAIRS.index((min(a, b), max(a, b)))]


def couple(maps, state):
    return [sum(coupling(maps, k, 3 - m) * state[m] for m in range(4)) for k in range(4)]


def plus(left, right):
    return [a + b for a, b in zip(left, right)]


def chained(maps, ends, low, high):
    count = len(maps)
    lows = [low]
    for s in range(count):
        lows.append(plus(pass_map(maps[s], lows[s]), ends[s][:4]))
    highs = [high]
    for s in reversed(range(count)):
        highs.insert(0, plus(plus(pass_map(maps[s], highs[0]), couple(maps[s], lows[s])), ends[s][4:]))
    return lows, highs


def merged_maps(maps):
    chain, total = (list(maps[0][:4]), list(maps[0][4:]))
    for s in range(1, len(maps)):
        part = maps[s]
        half = [
            [sum(chain[i] * coupling(part, a - i, b) for i in range(a + 1)) for b in range(4)]
            for a in range(4)
        ]
        total = [
            value + sum(chain[j] * half[a][b - j] for j in range(b + 1))
            for value, (a, b) in zip(total, PAIRS)
        ]
        chain = [sum(part[k - m] * chain[m] for m in range(k + 1)) for k in range(4)]
    return chain + total


def maps_kernel(classes, rates, _, wx, wy, wz, mx, my, my_all, mz, by_x, turned):
    def by_layer(z, _):
        here = classes[z]
        for f in range(2):
            wz[f, z] = picked(rates, 4 + f, here)
        return 0

    lax.fori_loop(0, STEPS, by_layer, 0, unroll=4)

    def by_row(z, _):
        by_x[pl.ds(z, STEPS, stride=STEPS), :] = classes[z].astype(F32)
        return 0

    lax.fori_loop(0, STEPS, by_row, 0, unroll=4)

    def x_weights(i, _):
        here = by_x[pl.ds(pl.multiple_of(i * STEPS, 8), STEPS)]
        for f in range(2):
            wx[f, i] = picked(rates, f, here)
        return 0

    lax.fori_loop(0, STEPS, x_weights, 0, unroll=4)
    for h in range(2):
        turned[h] = by_x[128 * h : 128 * h + 128].T

    def y_weights(i, _):
        rows = pl.ds(pl.multiple_of(i * 8, 8), 8)
        for h in range(2):
            here = turned[h, rows]
            for f in range(2):
                wy[2 * f + h, rows] = picked(rates, 2 + f, here)
        return 0

    lax.fori_loop(0, STEPS, y_weights, 0, unroll=4)
    for g in range(4):
        part = pl.ds(8 * (g % 2), 8)
        weights = (
            lambda i, g=g: wx[g // 2, i, part],
            lambda i, g=g: wz[g // 2, i, part],
            lambda i, g=g: wy[g, pl.ds(i, 8, stride=STEPS)],
        )
        for out, maps in zip((mx, mz, my), block_maps(weights)):
            for v in range(14):
                out[v, pl.ds(8 * g, 8)] = maps[v]
    blocks = [[my[v, pl.ds(s, 4, stride=8)] for v in range(14)] for s in range(8)]
    for v, value in enumerate(merged_maps(blocks)):
        my_all[pl.ds(4 * v, 4)] = value


def sweep_kernel(
    place, units, strips, z_even, z_odd, x_even, x_odd, corner_even, corner_odd, observed, wx, mx,
    predicted, increment, message,
    grid, side, even, odd, passed, ends,
):
    inside = slice(8, 8 + STEPS)

    def own(z, _):
        for unit in range(6):
            grid[unit, z + DEEP, inside] = units[unit, z]
        grid[6, z + DEEP, inside] = strips[z]
        for unit, offset, count in face_rows()[0]:
            rows = pl.ds(offset, count)
            low, high = sides(place, 0, x_even[z, rows], x_odd[z, rows])
            grid[unit, z + DEEP, pl.ds(8 - count, count)] = low
            grid[unit, z + DEEP, pl.ds(8 + STEPS, count)] = high
        return 0

    lax.fori_loop(0, STEPS, own, 0)
    for d in range(DEEP):
        for unit in range(7 if d < NEAR else 2):
            at = unit * NEAR + d if d < NEAR else 6 * NEAR + unit
            at = 6 * NEAR + 2 + d if unit == 6 else at
            low, high = sides(place, 2, z_even[at], z_odd[at])
            grid[unit, DEEP - 1 - d, inside] = low
            grid[unit, DEEP + STEPS + d, inside] = high
    for unit, d, offset, count in corner_rows()[0]:
        rows = pl.ds(offset, count)
        for x_side, start in enumerate((8 - count, 8 + STEPS)):
            low, high = sides(place, 2, corner_even[x_side, rows], corner_odd[x_side, rows])
            grid[unit, DEEP - 1 - d, pl.ds(start, count)] = low
            grid[unit, DEEP + STEPS + d, pl.ds(start, count)] = high

    def unpack(z, _):
        packed = grid[6, z]
        for unit in range(6):
            side[unit, z] = pltpu.roll(packed, 128 - 14 * unit, 1) if unit else packed
        return 0

    lax.fori_loop(0, PLANES, unpack, 0, unroll=5)

    everywhere = slice(0, 32)

    def sweep(main_from, side_from, main_to, side_to, rows, side_rows):
        def new_value(f, z, part, coefficients, source, here, other, below, above):
            total = source(f, z - 1, part) + source(f, z + 1, part)
            if part == everywhere:
                total = total + (pltpu.roll(here, 1, 0) + pltpu.roll(here, 31, 0))
            else:
                low, high = (slice(part.start - 1, part.stop - 1), slice(part.start + 1, part.stop + 1))
                total = total + (source(f, z, low) + source(f, z, high))
            total = total + (below + above)
            return coefficients[f, z, part] + coefficients[2 + f, z, part] * total + coefficients[4 + f, z, part] * other

        def layer(z, _):
            main = [main_from(f, z, rows) for f in range(2)]
            edge = [side_from(f, z, rows) for f in range(2)]
            lane = lanes(main[0].shape)
            for f in range(2):
                below = (pltpu.roll(main[f], 1, 1), pltpu.roll(edge[f], 1, 1))
                above = (pltpu.roll(main[f], 127, 1), pltpu.roll(edge[f], 127, 1))
                beside = [
                    (jnp.where(lane == 0, below[1 - i], below[i]), jnp.where(lane == 127, above[1 - i], above[i]))
                    for i in range(2)
                ]
                main_to(f, z, rows, new_value(f, z, rows, grid, main_from, main[f], main[1 - f], *beside[0]))
                if side_rows is not None:
                    side_to(f, z, rows, new_value(f, z, rows, side, side_from, edge[f], edge[1 - f], *beside[1]))
            return 0

        return layer

    buffers = (even, odd)
    for s in range(2, SWEEPS + 1):
        reach = SWEEPS - s
        if s == 2:
            main_from, side_from = (lambda f, z, part: grid[f, z, part], lambda f, z, part: side[f, z, part])
        else:
            old = buffers[s % 2]
            main_from = lambda f, z, part, old=old: old[f, z, part]
            side_from = lambda f, z, part, old=old: old[2 + f, z, part]
        new = buffers[(s + 1) % 2]

        def main_to(f, z, part, value, new=new):
            new[f, z, part] = value

        def side_to(f, z, part, value, new=new):
            new[2 + f, z, part] = value

        def last_to(f, z, part, value):
            predicted[f, z - DEEP] = value
            increment[f, pl.ds(z - DEEP, STEPS, stride=STEPS), :] = observed[f, z - DEEP] - value

        first, last = (DEEP - reach, DEEP + STEPS + reach - 1)
        if reach == 0:
            layer = sweep(main_from, side_from, last_to, None, inside, None)
            lax.fori_loop(first, last + 1, layer, 0, unroll=8)
        else:
            outermost = sweep(main_from, side_from, main_to, None, inside, None)
            outermost(first, 0)
            outermost(last, 0)
            layer = sweep(main_from, side_from, main_to, side_to, everywhere, everywhere)
            lax.fori_loop(first + 1, last, layer, 0, unroll=8)

    def weight(i, g):
        return wx[g // 2, i, pl.ds(8 * (g % 2), 8)]

    def put(i, g, value):
        passed[i, pl.ds(8 * g, 8)] = value

    def value(i, g):
        return increment[g // 2, pl.ds(STEPS * i + 8 * (g % 2), 8)]

    low = forward(value, weight, zeros(), put)
    high = backward(lambda i, g: passed[i, pl.ds(8 * g, 8)], weight, zeros(), lambda i, g, value: None)
    for g in range(4):
        for k in range(4):
            ends[k, pl.ds(8 * g, 8)] = low[g][k]
            ends[4 + k, pl.ds(8 * g, 8)] = high[g][k]
    for j in range(8):
        for v in range(22):
            rows = pl.ds(4 * j, 4)
            message[j, pl.ds(4 * v, 4)] = ends[v, rows] if v < 8 else mx[v - 8, rows]


def solve_kernel(gathered, _, inflow):
    parts = [[gathered[s, pl.ds(4 * v, 4)] for v in range(22)] for s in range(8)]
    zero = [jnp.zeros((4, 128), F32)] * 4
    lows, highs = chained([p[8:] for p in parts], [p[:8] for p in parts], zero, zero)
    for s in range(8):
        for k in range(4):
            inflow[s, pl.ds(4 * k, 4)] = lows[s][k]
            inflow[s, pl.ds(16 + 4 * k, 4)] = highs[s + 1][k]


def y_value(ref):
    return lambda i, g: ref[g, pl.ds(i, 8, stride=STEPS)]


def x_finish_kernel(increment, wx, inflow, wy, my, my_all, lines, ends, message, passed, start):
    for k in range(8):
        for j in range(8):
            start[k, pl.ds(4 * j, 4)] = inflow[j, pl.ds(4 * k, 4)]

    def weight(i, g):
        return wx[g // 2, i, pl.ds(8 * (g % 2), 8)]

    def value(i, g):
        return increment[g // 2, pl.ds(STEPS * i + 8 * (g % 2), 8)]

    def put(i, g, value):
        passed[g // 2, pl.ds(STEPS * i + 8 * (g % 2), 8)] = value

    def passed_value(i, g):
        return passed[g // 2, pl.ds(STEPS * i + 8 * (g % 2), 8)]

    low = [[start[k, pl.ds(8 * g, 8)] for k in range(4)] for g in range(4)]
    high = [[start[4 + k, pl.ds(8 * g, 8)] for k in range(4)] for g in range(4)]
    forward(value, weight, low, put)
    backward(passed_value, weight, high, put)
    for f in range(2):
        for h in range(2):
            lines[2 * f + h] = passed[f, pl.ds(128 * h, 128)].T

    def y_put(i, g, value):
        passed[g // 2, pl.ds(128 * (g % 2) + 8 * i, 8)] = value

    def y_passed(i, g):
        return passed[g // 2, pl.ds(128 * (g % 2) + 8 * i, 8)]

    low = forward(y_value(lines), y_value(wy), zeros(), y_put)
    high = backward(y_passed, y_value(wy), zeros(), lambda i, g, value: None)
    for g in range(4):
        for k in range(4):
            ends[k, pl.ds(8 * g, 8)] = low[g][k]
            ends[4 + k, pl.ds(8 * g, 8)] = high[g][k]
    maps = [[my[v, pl.ds(s, 4, stride=8)] for v in range(14)] for s in range(8)]
    block_ends = [[ends[v, pl.ds(s, 4, stride=8)] for v in range(8)] for s in range(8)]
    zero = [jnp.zeros((4, 128), F32)] * 4
    lows, highs = chained(maps, block_ends, zero, zero)
    for k in range(4):
        message[pl.ds(4 * k, 4)] = lows[8][k]
        message[pl.ds(16 + 4 * k, 4)] = highs[0][k]
    message[pl.ds(32, 56)] = my_all[...]


def own_inflow(position, count, maps, ends, zero, write):
    for p in range(count):

        @pl.when(position == p)
        def _(p=p):
            low = zero
            for j in range(p):
                low = plus(pass_map(maps(j ^ p), low), ends(j ^ p)[:4])
            inflow, lows = (low, [])
            for j in range(p, count):
                lows.append(inflow)
                if j < count - 1:
                    inflow = plus(pass_map(maps(j ^ p), inflow), ends(j ^ p)[:4])
            high = zero
            for j in range(count - 1, p, -1):
                coupled = couple(maps(j ^ p), lows[j - p])
                high = plus(plus(pass_map(maps(j ^ p), high), coupled), ends(j ^ p)[4:])
            write(low, high)


def y_finish_kernel(
    place, lines, wy, my, block_ends, own, xor_3, xor_2, xor_1, wz, unsmoothed, message,
    passed, start, done, by_row, inflow,
):
    refs = (own, xor_1, xor_2, xor_3)

    def write(low, high):
        for k in range(4):
            inflow[k, pl.ds(0, 4)] = low[k]
            inflow[4 + k, pl.ds(0, 4)] = high[k]

    own_inflow(
        place[1],
        4,
        lambda s: [refs[s][pl.ds(32 + 4 * v, 4)] for v in range(14)],
        lambda s: [refs[s][pl.ds(4 * v, 4)] for v in range(8)],
        [jnp.zeros((4, 128), F32)] * 4,
        write,
    )
    low = [inflow[k, pl.ds(0, 4)] for k in range(4)]
    high = [inflow[4 + k, pl.ds(0, 4)] for k in range(4)]
    maps = [[my[v, pl.ds(s, 4, stride=8)] for v in range(14)] for s in range(8)]
    blocks = [[block_ends[v, pl.ds(s, 4, stride=8)] for v in range(8)] for s in range(8)]
    lows, highs = chained(maps, blocks, low, high)
    for s in range(8):
        for k in range(4):
            start[k, pl.ds(s, 4, stride=8), :] = lows[s][k]
            start[4 + k, pl.ds(s, 4, stride=8), :] = highs[s + 1][k]

    def put(i, g, value):
        passed[g // 2, pl.ds(128 * (g % 2) + 8 * i, 8)] = value

    def passed_value(i, g):
        return passed[g // 2, pl.ds(128 * (g % 2) + 8 * i, 8)]

    def put_line(i, g, value):
        done[g, pl.ds(i, 8, stride=STEPS), :] = value

    low = [[start[k, pl.ds(8 * g, 8)] for k in range(4)] for g in range(4)]
    high = [[start[4 + k, pl.ds(8 * g, 8)] for k in range(4)] for g in range(4)]
    forward(y_value(lines), y_value(wy), low, put)
    backward(passed_value, y_value(wy), high, put_line)
    for g in range(4):
        by_row[g // 2, pl.ds(128 * (g % 2), 128)] = done[g].T

    def value(i, g):
        return by_row[g // 2, pl.ds(i + 128 * (g % 2), 8, stride=STEPS)]

    def weight(i, g):
        return wz[g // 2, i, pl.ds(8 * (g % 2), 8)]

    for i in range(STEPS):
        for g in range(4):
            unsmoothed[g // 2, i, pl.ds(8 * (g % 2), 8)] = value(i, g)

    low = forward(value, weight, zeros(), put)
    high = backward(passed_value, weight, zeros(), lambda i, g, value: None)
    for g in range(4):
        for k in range(4):
            message[k, pl.ds(8 * g, 8)] = low[g][k]
            message[4 + k, pl.ds(8 * g, 8)] = high[g][k]


def z_finish_kernel(
    place, unsmoothed, wz, maps_0, maps_1, maps_2, maps_3, ends_0, ends_3, ends_2, ends_1, smoothed, passed, inflow
):
    maps = (maps_0, maps_1, maps_2, maps_3)
    ends = (ends_0, ends_1, ends_2, ends_3)
    for g in range(4):
        rows = pl.ds(8 * g, 8)

        def write(low, high, rows=rows):
            for k in range(4):
                inflow[k, rows] = low[k]
                inflow[4 + k, rows] = high[k]

        own_inflow(
            place[2],
            4,
            lambda s, rows=rows: [maps[s][v, rows] for v in range(14)],
            lambda s, rows=rows: [ends[s][v, rows] for v in range(8)],
            [jnp.zeros((8, 128), F32)] * 4,
            write,
        )
    lows = [[inflow[k, pl.ds(8 * g, 8)] for k in range(4)] for g in range(4)]
    highs = [[inflow[4 + k, pl.ds(8 * g, 8)] for k in range(4)] for g in range(4)]

    def value(i, g):
        return unsmoothed[g // 2, i, pl.ds(8 * (g % 2), 8)]

    def weight(i, g):
        return wz[g // 2, i, pl.ds(8 * (g % 2), 8)]

    def put(i, g, value):
        passed[g // 2, i, pl.ds(8 * (g % 2), 8)] = value

    def put_last(i, g, value):
        smoothed[g // 2, i, pl.ds(8 * (g % 2), 8)] = value

    forward(value, weight, lows, put)
    backward(lambda i, g: passed[g // 2, i, pl.ds(8 * (g % 2), 8)], weight, highs, put_last)


def pair_swaps(axis, spare, value_even, value_odd):
    axes = tuple(sorted((axis, spare)))
    count, others = (lax.axis_size(axis), lax.axis_size(spare))

    def flat(i, k):
        return i * others + k if axis == axes[0] else k * count + i

    odd = []
    for i in range(count):
        for k in range(others):
            j = i + 1 if i % 2 else i - 1
            odd.append((flat(i, k), flat(j, k) if 0 <= j < count else flat(i, k ^ 1)))
    from_even = lax.ppermute(value_even, axis, [(i, i ^ 1) for i in range(count)])
    from_odd = lax.ppermute(value_odd, axes, odd)
    return from_even, from_odd


def xor_gather(value, axis):
    count = lax.axis_size(axis)
    return [value] + [lax.ppermute(value, axis, [(i, i ^ s) for i in range(count)]) for s in (1, 2, 3)]


def local(source, capacity, transfer, observed, classes, conductivity, filter_rates):
    axes = ("gx", "gy", "gz")
    place = jnp.stack([lax.axis_index(a) for a in axes] + [jnp.int32(lax.axis_size(a)) for a in axes])
    rates = filter_rates.reshape(6, CLASSES)
    plane = (STEPS, STEPS, 128)
    units, y_even, y_odd, classes = call(
        coefficients_kernel,
        [(6,) + plane, (8, STEPS, 128), (8, STEPS, 128), jax.ShapeDtypeStruct(plane, jnp.int32)],
        [HBM] * 4 + [SMEM],
        [plane, (2,) + plane, (2,) + plane, plane],
        limit=60,
        copies=4,
    )(source, capacity, transfer, classes, conductivity)
    y_even, y_odd = pair_swaps("gy", "gz", y_even, y_odd)

    z_face = (7 * NEAR + 2, STEPS, 128)
    x_face = (STEPS, face_rows()[1], 128)
    corners = (2, corner_rows()[1], 128)
    z_own = (6 * NEAR + 2, STEPS, 128)
    x_own = (STEPS, face_rows()[0][6][1], 128)
    faces = call(face_kernel, [z_own, z_own, x_own, x_own], [SMEM, VMEM])(place, units)
    strips, z_even, z_odd, x_even, x_odd = call(
        halo_kernel, [plane, z_face, z_face, x_face, x_face], [SMEM] + [VMEM] * 6
    )(place, y_odd, y_even, *faces)
    x_even, x_odd = pair_swaps("gx", "gy", x_even, x_odd)
    z_even, z_odd = pair_swaps("gz", "gy", z_even, z_odd)

    rows = (32, 128)
    wx, wy, wz, mx, my, my_all, mz, _, _ = call(
        maps_kernel,
        [(2,) + plane, (4, 128, 128), (2,) + plane, (14,) + rows, (14,) + rows, (56, 128), (14,) + rows,
         (256, 128), (2, 128, 128)],
        [VMEM, SMEM, VMEM],
    )(classes, rates, strips)
    x_odd, wx = lax.optimization_barrier((x_odd, wx))
    corner_even, corner_odd = call(corner_kernel, [corners, corners], [SMEM] + [VMEM] * 3)(place, x_odd, x_even, observed)
    corner_even, corner_odd = pair_swaps("gz", "gy", corner_even, corner_odd)
    z_maps = xor_gather(mz, "gz")

    padded = (PLANES, 32, 128)
    predicted, increment, message = call(
        sweep_kernel,
        [(2,) + plane, (2, 256, 128), (8, 88, 128)],
        [SMEM] + [VMEM] * 11,
        [(7,) + padded, (6,) + padded, (4,) + padded, (4,) + padded, (STEPS,) + rows, (8,) + rows],
        flops=100000000,
        limit=16,
    )(place, units, strips, z_even, z_odd, x_even, x_odd, corner_even, corner_odd,
      observed, wx, mx)
    gathered = lax.all_to_all(message, "gx", 0, 0, tiled=True)
    inflow, = call(solve_kernel, [(8, 32, 128)], [VMEM] * 2)(gathered, increment)
    inflow = lax.all_to_all(inflow, "gx", 0, 0, tiled=True)
    inflow, z_maps = lax.optimization_barrier((inflow, z_maps))
    lines, block_ends, y_ends = call(
        x_finish_kernel,
        [(4, 128, 128), (8,) + rows, (88, 128)],
        [VMEM] * 6,
        [(2, 256, 128), (8,) + rows],
    )(increment, wx, inflow, wy, my, my_all)
    y_all = xor_gather(y_ends, "gy")
    unsmoothed, z_ends = call(
        y_finish_kernel,
        [(2,) + plane, (8,) + rows],
        [SMEM] + [VMEM] * 9,
        [(2, 256, 128), (8,) + rows, (4, 128, 128), (2, 256, 128), (8, 8, 128)],
    )(place, lines, wy, my, block_ends, y_all[0], *y_all[:0:-1], wz)
    z_all = xor_gather(z_ends, "gz")
    smoothed, = call(z_finish_kernel, [(2,) + plane], [SMEM] + [VMEM] * 10, [(2,) + plane, (8,) + rows])(
        place, unsmoothed, wz, *z_maps, z_all[0], *z_all[:0:-1]
    )
    return (predicted, smoothed)


def solution(mesh):
    cells = P(None, "gz", "gx", "gy")
    return jax.shard_map(
        local,
        mesh=mesh,
        in_specs=(cells, cells, P("gz", "gx", "gy"), cells, P("gz", "gx", "gy"), P(), P()),
        out_specs=(cells, cells),
        check_vma=False,
    )
```

```python
import jax
import jax.numpy as jnp
from jax import lax
from jax.experimental import pallas as pl
from jax.experimental.pallas import tpu as pltpu
from jax.sharding import PartitionSpec as P

SWEEPS = 8
DEEP = SWEEPS - 1
NEAR = DEEP - 1
CLASSES = 12
STEPS = 16
PLANES = STEPS + 2 * DEEP
F32 = jnp.float32
VMEM = pl.BlockSpec(memory_space=pltpu.VMEM)
SMEM = pl.BlockSpec(memory_space=pltpu.SMEM)
HBM = pl.BlockSpec(memory_space=pltpu.HBM)
ANY = pl.BlockSpec(memory_space=pl.ANY)


def call(body, outs, specs, scratch=(), flops=1000000, limit=4, copies=0, out_specs=None, aliases=None):
    return pl.pallas_call(
        body,
        out_shape=[shape if hasattr(shape, "dtype") else jax.ShapeDtypeStruct(shape, F32) for shape in outs],
        in_specs=specs,
        out_specs=out_specs or [VMEM] * len(outs),
        input_output_aliases=aliases or {},
        scratch_shapes=[
            pltpu.VMEM(*((shape.shape, shape.dtype) if hasattr(shape, "dtype") else (shape, F32)))
            for shape in scratch
        ]
        + [pltpu.SemaphoreType.DMA((copies,))] * (copies > 0),
        compiler_params=pltpu.CompilerParams(vmem_limit_bytes=limit * 1024 * 1024),
        cost_estimate=pl.CostEstimate(flops=flops, bytes_accessed=1000000, transcendentals=0),
    )


def picked(table, row, classes):
    value = jnp.full(classes.shape, table[row, 0], F32)
    for entry in range(1, CLASSES):
        value = jnp.where(classes == entry, table[row, entry], value)
    return value


def lanes(shape):
    return lax.broadcasted_iota(jnp.int32, shape, len(shape) - 1)


def first_mask(lane):
    return (lane % 14 < 7) & (lane < 84)


def last_mask(lane):
    return ((lane % 14 >= 7) & (lane < 70)) | (lane >= 121)


def by_pairs(place, axis, low, high):
    is_even = place[axis] % 2 == 0
    return jnp.where(is_even, high, low), jnp.where(is_even, low, high)


def sides(place, axis, even, odd):
    high, low = by_pairs(place, axis, odd, even)
    return (
        jnp.where(place[axis] > 0, low, 0.0),
        jnp.where(place[axis] < place[axis + 3] - 1, high, 0.0),
    )


def brought(pairs, sems):
    copies = [pltpu.make_async_copy(a, b, sems.at[i]) for i, (a, b) in enumerate(pairs)]
    for copy in copies:
        copy.start()
    for copy in copies:
        copy.wait()


def coefficients_kernel(
    source_in, capacity_in, transfer_in, classes_in, conductivity,
    units, even, odd,
    edges, source, capacity, transfer, classes, sems,
):
    place = {1: lax.axis_index("gy")}
    brought(((source_in, source), (capacity_in, capacity), (transfer_in, transfer), (classes_in, classes)), sems)

    def layer(z, _):
        transfer_z = transfer[z]
        classes_z = classes[z]
        lane = lanes(classes_z.shape)
        packed = jnp.zeros(classes_z.shape, F32)
        for f in range(2):
            conduct = picked(conductivity, f, classes_z)
            inverse = 1.0 / (capacity[f, z] + 6.0 * conduct + transfer_z)
            for unit, value in (
                (f, source[f, z] * inverse),
                (2 + f, conduct * inverse),
                (4 + f, transfer_z * inverse),
            ):
                units[unit, z] = value
                turned = pltpu.roll(value, 14 * unit, 1) if unit else value
                packed = jnp.where((lane - 14 * unit + 7 + 128) % 128 < 14, turned, packed)
        edges[z] = packed
        return 0

    lax.fori_loop(0, STEPS, layer, 0, unroll=8)

    def pair(z, _):
        upper, lower = (edges[z], edges[z + 8])
        lane = lanes(upper.shape)
        to_low = jnp.where(first_mask(lane), upper, pltpu.roll(lower, 121, 1))
        to_high = jnp.where(last_mask(lane), upper, pltpu.roll(lower, 7, 1))
        even[z], odd[z] = by_pairs(place, 1, to_low, to_high)
        return 0

    lax.fori_loop(0, 8, pair, 0, unroll=4)


def counts(unit):
    return DEEP if unit < 2 else NEAR


X_MAIN = sum(counts(unit) for unit in range(6))
X_ROWS = STEPS * (X_MAIN + NEAR)


def face_row(unit, z):
    if unit == 6:
        return STEPS * X_MAIN + z * NEAR
    return z * X_MAIN + sum(counts(u) for u in range(unit))


def corner_rows():
    offset, rows = (0, [])
    for unit in range(7):
        for d in range(NEAR):
            count = NEAR - d if unit < 2 else NEAR - d - 1
            if count > 0:
                rows.append((unit, d, offset, count))
                offset += count
    return rows, -(-offset // 8) * 8


def face_kernel(place, units, z_even, z_odd, x_even, x_odd):
    for d in range(DEEP):
        for unit in range(6 if d < NEAR else 2):
            at = unit * NEAR + d if d < NEAR else 6 * NEAR + unit
            z_even[at], z_odd[at] = by_pairs(place, 2, units[unit, d], units[unit, STEPS - 1 - d])

    for z in range(STEPS):
        for unit in range(6):
            count = counts(unit)
            low, high = (units[unit, z, pl.ds(0, count)], units[unit, z, pl.ds(STEPS - count, count)])
            even, odd = by_pairs(place, 0, low, high)
            x_even[pl.ds(face_row(unit, z), count)] = even
            x_odd[pl.ds(face_row(unit, z), count)] = odd


def halo_kernel(
    place, y_odd, y_even, _z_even, _z_odd, _x_even, _x_odd, strips, z_even, z_odd, x_even, x_odd,
    to_z_even, to_z_odd, to_x_even, to_x_odd, sems,
):
    def pair(z, _):
        low, high = sides(place, 1, y_even[z], y_odd[z])
        first = first_mask(lanes(high.shape))
        strips[z] = jnp.where(first, high, low)
        strips[z + 8] = jnp.where(first, pltpu.roll(high, 7, 1), pltpu.roll(low, 121, 1))
        return 0

    lax.fori_loop(0, 8, pair, 0, unroll=4)
    for d in range(NEAR):
        to_z_even[d], to_z_odd[d] = by_pairs(place, 2, strips[d], strips[STEPS - 1 - d])
    for z in range(STEPS):
        low, high = (strips[z, pl.ds(0, NEAR)], strips[z, pl.ds(STEPS - NEAR, NEAR)])
        even, odd = by_pairs(place, 0, low, high)
        to_x_even[pl.ds(NEAR * z, NEAR)] = even
        to_x_odd[pl.ds(NEAR * z, NEAR)] = odd
    z_part = pl.ds(6 * NEAR + 2, NEAR)
    x_part = pl.ds(STEPS * X_MAIN, STEPS * NEAR)
    brought(
        (
            (to_z_even, z_even.at[z_part]),
            (to_z_odd, z_odd.at[z_part]),
            (to_x_even, x_even.at[x_part]),
            (to_x_odd, x_odd.at[x_part]),
        ),
        sems,
    )


def corner_kernel(place, x_odd, x_even, _z_even, _observed, even, odd):
    for unit, d, offset, count in corner_rows()[0]:
        ends = []
        for z in (d, STEPS - 1 - d):
            first = face_row(unit, z)
            last = first + counts(unit) - count
            low = sides(place, 0, x_even[pl.ds(last, count)], x_odd[pl.ds(last, count)])[0]
            high = sides(place, 0, x_even[pl.ds(first, count)], x_odd[pl.ds(first, count)])[1]
            ends.append((low, high))
        for x_side in range(2):
            to_even, to_odd = by_pairs(place, 2, ends[0][x_side], ends[1][x_side])
            even[x_side, pl.ds(offset, count)] = to_even
            odd[x_side, pl.ds(offset, count)] = to_odd


def forward(read_value, read_weight, state, write, count=4):
    for i in range(STEPS):
        for g in range(count):
            weight = read_weight(i, g)
            value = read_value(i, g)
            keep = 1.0 - weight
            for k in range(4):
                value = keep * state[g][k] + weight * value
                state[g][k] = value
            write(i, g, value)
    return state


def backward(read_value, read_weight, state, write, count=4):
    return forward(
        lambda i, g: read_value(STEPS - 1 - i, g),
        lambda i, g: read_weight(STEPS - 1 - i, g),
        state,
        lambda i, g, value: write(STEPS - 1 - i, g, value),
        count,
    )


def zeros(count=4):
    return [[jnp.zeros((8, 128), F32) for _ in range(4)] for _ in range(count)]


PAIRS = [(a, b) for a in range(4) for b in range(a, 4)]


def block_maps(read_weights):
    def step(i, carries):
        out = []
        for read_weight, carry in zip(read_weights, carries):
            chain, sums = (list(carry[:4]), list(carry[4:]))
            weight = read_weight(i)
            keep = 1.0 - weight
            for k in range(1, 4):
                chain[k] = chain[k] + weight * chain[k - 1]
            scaled = [weight * value for value in chain]
            chain = [keep * value for value in chain]
            sums = [total + scaled[a] * chain[b] for total, (a, b) in zip(sums, PAIRS)]
            out.append(tuple(chain + sums))
        return tuple(out)

    zero = jnp.zeros((8, 128), F32)
    start = (zero + 1.0,) + (zero,) * 13
    return lax.fori_loop(0, STEPS, step, (start,) * len(read_weights), unroll=4)


def pass_map(maps, state):
    return [sum(maps[k - m] * state[m] for m in range(k + 1)) for k in range(4)]


def coupling(maps, a, b):
    return maps[4 + PAIRS.index((min(a, b), max(a, b)))]


def couple(maps, state):
    return [sum(coupling(maps, k, 3 - m) * state[m] for m in range(4)) for k in range(4)]


def plus(left, right):
    return [a + b for a, b in zip(left, right)]


def chained(maps, ends, low, high):
    count = len(maps)
    lows = [low]
    for s in range(count):
        lows.append(plus(pass_map(maps[s], lows[s]), ends[s][:4]))
    highs = [high]
    for s in reversed(range(count)):
        highs.insert(0, plus(plus(pass_map(maps[s], highs[0]), couple(maps[s], lows[s])), ends[s][4:]))
    return lows, highs


def merged_maps(maps):
    chain, total = (list(maps[0][:4]), list(maps[0][4:]))
    for s in range(1, len(maps)):
        part = maps[s]
        half = [
            [sum(chain[i] * coupling(part, a - i, b) for i in range(a + 1)) for b in range(4)]
            for a in range(4)
        ]
        total = [
            value + sum(chain[j] * half[a][b - j] for j in range(b + 1))
            for value, (a, b) in zip(total, PAIRS)
        ]
        chain = [sum(part[k - m] * chain[m] for m in range(k + 1)) for k in range(4)]
    return chain + total


def maps_kernel(classes, rates, _, wx, wy, wz, mx, my, my_all, mz, by_x, turned):
    def by_layer(z, _):
        here = classes[z]
        for f in range(2):
            wz[f, z] = picked(rates, 4 + f, here)
        return 0

    lax.fori_loop(0, STEPS, by_layer, 0, unroll=4)

    def by_row(z, _):
        by_x[pl.ds(z, STEPS, stride=STEPS), :] = classes[z].astype(F32)
        return 0

    lax.fori_loop(0, STEPS, by_row, 0, unroll=4)

    def x_weights(i, _):
        here = by_x[pl.ds(pl.multiple_of(i * STEPS, 8), STEPS)]
        for f in range(2):
            wx[f, i] = picked(rates, f, here)
        return 0

    lax.fori_loop(0, STEPS, x_weights, 0, unroll=4)
    for h in range(2):
        turned[h] = by_x[128 * h : 128 * h + 128].T

    def y_weights(i, _):
        rows = pl.ds(pl.multiple_of(i * 8, 8), 8)
        for h in range(2):
            here = turned[h, rows]
            for f in range(2):
                wy[2 * f + h, rows] = picked(rates, 2 + f, here)
        return 0

    lax.fori_loop(0, STEPS, y_weights, 0, unroll=4)
    for g in range(4):
        part = pl.ds(8 * (g % 2), 8)
        weights = (
            lambda i, g=g: wx[g // 2, i, part],
            lambda i, g=g: wz[g // 2, i, part],
            lambda i, g=g: wy[g, pl.ds(i, 8, stride=STEPS)],
        )
        for out, maps in zip((mx, mz, my), block_maps(weights)):
            for v in range(14):
                out[v, pl.ds(8 * g, 8)] = maps[v]
    blocks = [[my[v, pl.ds(s, 4, stride=8)] for v in range(14)] for s in range(8)]
    for v, value in enumerate(merged_maps(blocks)):
        my_all[pl.ds(4 * v, 4)] = value


def sweep_kernel(
    place, units, strips, z_even, z_odd, x_even, x_odd, corner_even, corner_odd, observed, wx, mx,
    predicted, increment, message_out,
    grid, side, even, odd, passed, ends, message, sems,
):
    inside = slice(8, 8 + STEPS)

    def own(z, _):
        for unit in range(6):
            grid[unit, z + DEEP, inside] = units[unit, z]
        grid[6, z + DEEP, inside] = strips[z]
        return 0

    lax.fori_loop(0, STEPS, own, 0, unroll=2)
    for z in range(STEPS):
        for unit in range(7):
            count = counts(unit)
            rows = pl.ds(face_row(unit, z), count)
            low, high = sides(place, 0, x_even[rows], x_odd[rows])
            grid[unit, z + DEEP, pl.ds(8 - count, count)] = low
            grid[unit, z + DEEP, pl.ds(8 + STEPS, count)] = high
    for d in range(DEEP):
        for unit in range(7 if d < NEAR else 2):
            at = unit * NEAR + d if d < NEAR else 6 * NEAR + unit
            at = 6 * NEAR + 2 + d if unit == 6 else at
            low, high = sides(place, 2, z_even[at], z_odd[at])
            grid[unit, DEEP - 1 - d, inside] = low
            grid[unit, DEEP + STEPS + d, inside] = high
    for unit, d, offset, count in corner_rows()[0]:
        rows = pl.ds(offset, count)
        for x_side, start in enumerate((8 - count, 8 + STEPS)):
            low, high = sides(place, 2, corner_even[x_side, rows], corner_odd[x_side, rows])
            grid[unit, DEEP - 1 - d, pl.ds(start, count)] = low
            grid[unit, DEEP + STEPS + d, pl.ds(start, count)] = high

    def unpack(z, _):
        packed = grid[6, z]
        for unit in range(6):
            side[unit, z] = pltpu.roll(packed, 128 - 14 * unit, 1) if unit else packed
        return 0

    lax.fori_loop(0, PLANES, unpack, 0, unroll=5)

    everywhere = slice(0, 32)

    def sweep(main_from, side_from, main_to, side_to, rows, side_rows):
        def new_value(f, z, part, coefficients, source, here, other, below, above):
            total = source(f, z - 1, part) + source(f, z + 1, part)
            if part == everywhere:
                total = total + (pltpu.roll(here, 1, 0) + pltpu.roll(here, 31, 0))
            else:
                low, high = (slice(part.start - 1, part.stop - 1), slice(part.start + 1, part.stop + 1))
                total = total + (source(f, z, low) + source(f, z, high))
            total = total + (below + above)
            return coefficients[f, z, part] + coefficients[2 + f, z, part] * total + coefficients[4 + f, z, part] * other

        def layer(z, _):
            main = [main_from(f, z, rows) for f in range(2)]
            edge = [side_from(f, z, rows) for f in range(2)]
            lane = lanes(main[0].shape)
            for f in range(2):
                below = (pltpu.roll(main[f], 1, 1), pltpu.roll(edge[f], 1, 1))
                above = (pltpu.roll(main[f], 127, 1), pltpu.roll(edge[f], 127, 1))
                beside = [
                    (jnp.where(lane == 0, below[1 - i], below[i]), jnp.where(lane == 127, above[1 - i], above[i]))
                    for i in range(2)
                ]
                main_to(f, z, rows, new_value(f, z, rows, grid, main_from, main[f], main[1 - f], *beside[0]))
                if side_rows is not None:
                    side_to(f, z, rows, new_value(f, z, rows, side, side_from, edge[f], edge[1 - f], *beside[1]))
            return 0

        return layer

    buffers = (even, odd)
    for s in range(2, SWEEPS + 1):
        reach = SWEEPS - s
        if s == 2:
            main_from, side_from = (lambda f, z, part: grid[f, z, part], lambda f, z, part: side[f, z, part])
        else:
            old = buffers[s % 2]
            main_from = lambda f, z, part, old=old: old[f, z, part]
            side_from = lambda f, z, part, old=old: old[2 + f, z, part]
        new = buffers[(s + 1) % 2]

        def main_to(f, z, part, value, new=new):
            new[f, z, part] = value

        def side_to(f, z, part, value, new=new):
            new[2 + f, z, part] = value

        def last_to(f, z, part, value):
            predicted[f, z - DEEP] = value
            increment[f, pl.ds(z - DEEP, STEPS, stride=STEPS), :] = observed[f, z - DEEP] - value

        first, last = (DEEP - reach, DEEP + STEPS + reach - 1)
        if reach == 0:
            layer = sweep(main_from, side_from, last_to, None, inside, None)
            lax.fori_loop(first, last + 1, layer, 0, unroll=8)
        else:
            outermost = sweep(main_from, side_from, main_to, None, inside, None)
            outermost(first, 0)
            outermost(last, 0)
            layer = sweep(main_from, side_from, main_to, side_to, everywhere, everywhere)
            lax.fori_loop(first + 1, last, layer, 0, unroll=8)

    def weight(i, g):
        return wx[g // 2, i, pl.ds(8 * (g % 2), 8)]

    def put(i, g, value):
        passed[i, pl.ds(8 * g, 8)] = value

    def value(i, g):
        return increment[g // 2, pl.ds(STEPS * i + 8 * (g % 2), 8)]

    low = forward(value, weight, zeros(), put)
    high = backward(lambda i, g: passed[i, pl.ds(8 * g, 8)], weight, zeros(), lambda i, g, value: None)
    for g in range(4):
        for k in range(4):
            ends[k, pl.ds(8 * g, 8)] = low[g][k]
            ends[4 + k, pl.ds(8 * g, 8)] = high[g][k]
    for j in range(8):
        for v in range(22):
            rows = pl.ds(4 * j, 4)
            message[j, pl.ds(4 * v, 4)] = ends[v, rows] if v < 8 else mx[v - 8, rows]
    brought(((message, message_out),), sems)


def solve_kernel(gathered, _, inflow):
    parts = [[gathered[s, pl.ds(4 * v, 4)] for v in range(22)] for s in range(8)]
    zero = [jnp.zeros((4, 128), F32)] * 4
    lows, highs = chained([p[8:] for p in parts], [p[:8] for p in parts], zero, zero)
    for s in range(8):
        for k in range(4):
            inflow[s, pl.ds(4 * k, 4)] = lows[s][k]
            inflow[s, pl.ds(16 + 4 * k, 4)] = highs[s + 1][k]


def y_value(ref):
    return lambda i, g: ref[g, pl.ds(i, 8, stride=STEPS)]


def x_finish_kernel(increment, wx, inflow, wy, my, my_all, lines, ends, message, passed, start):
    for k in range(8):
        for j in range(8):
            start[k, pl.ds(4 * j, 4)] = inflow[j, pl.ds(4 * k, 4)]

    def weight(i, g):
        return wx[g // 2, i, pl.ds(8 * (g % 2), 8)]

    def value(i, g):
        return increment[g // 2, pl.ds(STEPS * i + 8 * (g % 2), 8)]

    def put(i, g, value):
        passed[g // 2, pl.ds(STEPS * i + 8 * (g % 2), 8)] = value

    def passed_value(i, g):
        return passed[g // 2, pl.ds(STEPS * i + 8 * (g % 2), 8)]

    low = [[start[k, pl.ds(8 * g, 8)] for k in range(4)] for g in range(4)]
    high = [[start[4 + k, pl.ds(8 * g, 8)] for k in range(4)] for g in range(4)]
    forward(value, weight, low, put)
    backward(passed_value, weight, high, put)
    for f in range(2):
        for h in range(2):
            lines[2 * f + h] = passed[f, pl.ds(128 * h, 128)].T

    def y_put(i, g, value):
        passed[g // 2, pl.ds(128 * (g % 2) + 8 * i, 8)] = value

    def y_passed(i, g):
        return passed[g // 2, pl.ds(128 * (g % 2) + 8 * i, 8)]

    low = forward(y_value(lines), y_value(wy), zeros(), y_put)
    high = backward(y_passed, y_value(wy), zeros(), lambda i, g, value: None)
    for g in range(4):
        for k in range(4):
            ends[k, pl.ds(8 * g, 8)] = low[g][k]
            ends[4 + k, pl.ds(8 * g, 8)] = high[g][k]
    maps = [[my[v, pl.ds(s, 4, stride=8)] for v in range(14)] for s in range(8)]
    block_ends = [[ends[v, pl.ds(s, 4, stride=8)] for v in range(8)] for s in range(8)]
    zero = [jnp.zeros((4, 128), F32)] * 4
    lows, highs = chained(maps, block_ends, zero, zero)
    for k in range(4):
        message[pl.ds(4 * k, 4)] = lows[8][k]
        message[pl.ds(16 + 4 * k, 4)] = highs[0][k]
    message[pl.ds(32, 56)] = my_all[...]


def own_inflow(position, count, maps, ends, zero, write):
    for p in range(count):

        @pl.when(position == p)
        def _(p=p):
            low = zero
            for j in range(p):
                low = plus(pass_map(maps(j ^ p), low), ends(j ^ p)[:4])
            inflow, lows = (low, [])
            for j in range(p, count):
                lows.append(inflow)
                if j < count - 1:
                    inflow = plus(pass_map(maps(j ^ p), inflow), ends(j ^ p)[:4])
            high = zero
            for j in range(count - 1, p, -1):
                coupled = couple(maps(j ^ p), lows[j - p])
                high = plus(plus(pass_map(maps(j ^ p), high), coupled), ends(j ^ p)[4:])
            write(low, high)


def y_finish_kernel(
    place, lines, wy, my, block_ends, own, xor_3, xor_2, xor_1, wz, unsmoothed, message,
    passed, start, done, by_row, inflow,
):
    refs = (own, xor_1, xor_2, xor_3)

    def write(low, high):
        for k in range(4):
            inflow[k, pl.ds(0, 4)] = low[k]
            inflow[4 + k, pl.ds(0, 4)] = high[k]

    own_inflow(
        place[1],
        4,
        lambda s: [refs[s][pl.ds(32 + 4 * v, 4)] for v in range(14)],
        lambda s: [refs[s][pl.ds(4 * v, 4)] for v in range(8)],
        [jnp.zeros((4, 128), F32)] * 4,
        write,
    )
    low = [inflow[k, pl.ds(0, 4)] for k in range(4)]
    high = [inflow[4 + k, pl.ds(0, 4)] for k in range(4)]
    maps = [[my[v, pl.ds(s, 4, stride=8)] for v in range(14)] for s in range(8)]
    blocks = [[block_ends[v, pl.ds(s, 4, stride=8)] for v in range(8)] for s in range(8)]
    lows, highs = chained(maps, blocks, low, high)
    for s in range(8):
        for k in range(4):
            start[k, pl.ds(s, 4, stride=8), :] = lows[s][k]
            start[4 + k, pl.ds(s, 4, stride=8), :] = highs[s + 1][k]

    def put(i, g, value):
        passed[g // 2, pl.ds(128 * (g % 2) + 8 * i, 8)] = value

    def passed_value(i, g):
        return passed[g // 2, pl.ds(128 * (g % 2) + 8 * i, 8)]

    def put_line(i, g, value):
        done[g, pl.ds(i, 8, stride=STEPS), :] = value

    low = [[start[k, pl.ds(8 * g, 8)] for k in range(4)] for g in range(4)]
    high = [[start[4 + k, pl.ds(8 * g, 8)] for k in range(4)] for g in range(4)]
    forward(y_value(lines), y_value(wy), low, put)
    backward(passed_value, y_value(wy), high, put_line)
    for g in range(4):
        by_row[g // 2, pl.ds(128 * (g % 2), 128)] = done[g].T

    def value(i, g):
        return by_row[g // 2, pl.ds(i + 128 * (g % 2), 8, stride=STEPS)]

    def weight(i, g):
        return wz[g // 2, i, pl.ds(8 * (g % 2), 8)]

    for i in range(STEPS):
        for g in range(4):
            unsmoothed[g // 2, i, pl.ds(8 * (g % 2), 8)] = value(i, g)

    low = forward(value, weight, zeros(), put)
    high = backward(passed_value, weight, zeros(), lambda i, g, value: None)
    for g in range(4):
        for k in range(4):
            message[k, pl.ds(8 * g, 8)] = low[g][k]
            message[4 + k, pl.ds(8 * g, 8)] = high[g][k]


def z_finish_kernel(
    place, unsmoothed, wz, maps_0, maps_1, maps_2, maps_3, ends_0, ends_3, ends_2, ends_1, smoothed, passed, inflow
):
    maps = (maps_0, maps_1, maps_2, maps_3)
    ends = (ends_0, ends_1, ends_2, ends_3)
    for g in range(4):
        rows = pl.ds(8 * g, 8)

        def write(low, high, rows=rows):
            for k in range(4):
                inflow[k, rows] = low[k]
                inflow[4 + k, rows] = high[k]

        own_inflow(
            place[2],
            4,
            lambda s, rows=rows: [maps[s][v, rows] for v in range(14)],
            lambda s, rows=rows: [ends[s][v, rows] for v in range(8)],
            [jnp.zeros((8, 128), F32)] * 4,
            write,
        )
    lows = [[inflow[k, pl.ds(8 * g, 8)] for k in range(4)] for g in range(4)]
    highs = [[inflow[4 + k, pl.ds(8 * g, 8)] for k in range(4)] for g in range(4)]

    def value(i, g):
        return unsmoothed[g // 2, i, pl.ds(8 * (g % 2), 8)]

    def weight(i, g):
        return wz[g // 2, i, pl.ds(8 * (g % 2), 8)]

    def put(i, g, value):
        passed[g // 2, i, pl.ds(8 * (g % 2), 8)] = value

    def put_last(i, g, value):
        smoothed[g // 2, i, pl.ds(8 * (g % 2), 8)] = value

    forward(value, weight, lows, put)
    backward(lambda i, g: passed[g // 2, i, pl.ds(8 * (g % 2), 8)], weight, highs, put_last)


def pair_swaps(axis, spare, value_even, value_odd):
    axes = tuple(sorted((axis, spare)))
    count, others = (lax.axis_size(axis), lax.axis_size(spare))

    def flat(i, k):
        return i * others + k if axis == axes[0] else k * count + i

    odd = []
    for i in range(count):
        for k in range(others):
            j = i + 1 if i % 2 else i - 1
            odd.append((flat(i, k), flat(j, k) if 0 <= j < count else flat(i, k ^ 1)))
    from_even = lax.ppermute(value_even, axis, [(i, i ^ 1) for i in range(count)])
    from_odd = lax.ppermute(value_odd, axes, odd)
    return from_even, from_odd


def xor_gather(value, axis):
    count = lax.axis_size(axis)
    return [value] + [lax.ppermute(value, axis, [(i, i ^ s) for i in range(count)]) for s in (1, 2, 3)]


def local(source, capacity, transfer, observed, classes, conductivity, filter_rates):
    axes = ("gx", "gy", "gz")
    place = jnp.stack([lax.axis_index(a) for a in axes] + [jnp.int32(lax.axis_size(a)) for a in axes])
    rates = filter_rates.reshape(6, CLASSES)
    plane = (STEPS, STEPS, 128)
    units, y_even, y_odd = call(
        coefficients_kernel,
        [(6,) + plane, (8, STEPS, 128), (8, STEPS, 128)],
        [HBM] * 4 + [SMEM],
        [plane, (2,) + plane, (2,) + plane, plane, jax.ShapeDtypeStruct(plane, jnp.int32)],
        limit=60,
        copies=4,
    )(source, capacity, transfer, classes, conductivity)
    y_even, y_odd = pair_swaps("gy", "gz", y_even, y_odd)

    z_face = (7 * NEAR + 2, STEPS, 128)
    x_face = (X_ROWS, 128)
    corners = (2, corner_rows()[1], 128)
    faces = call(face_kernel, [z_face, z_face, x_face, x_face], [SMEM, VMEM])(place, units)
    strips, z_even, z_odd, x_even, x_odd = call(
        halo_kernel,
        [plane, z_face, z_face, x_face, x_face],
        [SMEM] + [VMEM] * 2 + [ANY] * 4,
        [(NEAR,) + plane[1:]] * 2 + [(STEPS * NEAR, 128)] * 2,
        out_specs=[VMEM] + [ANY] * 4,
        aliases={3: 1, 4: 2, 5: 3, 6: 4},
        copies=4,
    )(place, y_odd, y_even, *faces)
    x_even, x_odd = pair_swaps("gx", "gy", x_even, x_odd)
    z_even, z_odd = pair_swaps("gz", "gy", z_even, z_odd)

    rows = (32, 128)
    wx, wy, wz, mx, my, my_all, mz, _, _ = call(
        maps_kernel,
        [(2,) + plane, (4, 128, 128), (2,) + plane, (14,) + rows, (14,) + rows, (56, 128), (14,) + rows,
         (256, 128), (2, 128, 128)],
        [VMEM, SMEM, VMEM],
    )(classes, rates, strips)
    x_odd, wx = lax.optimization_barrier((x_odd, wx))
    corner_even, corner_odd = call(corner_kernel, [corners, corners], [SMEM] + [VMEM] * 4)(
        place, x_odd, x_even, z_even, observed
    )
    corner_even, corner_odd = pair_swaps("gz", "gy", corner_even, corner_odd)

    z_maps = xor_gather(mz, "gz")

    padded = (PLANES, 32, 128)
    predicted, increment, message = call(
        sweep_kernel,
        [(2,) + plane, (2, 256, 128), (8, 88, 128)],
        [SMEM] + [VMEM] * 11,
        [(7,) + padded, (6,) + padded, (4,) + padded, (4,) + padded, (STEPS,) + rows, (8,) + rows, (8, 88, 128)],
        out_specs=[VMEM, VMEM, HBM],
        copies=1,
        flops=100000000,
        limit=16,
    )(place, units, strips, z_even, z_odd, x_even, x_odd, corner_even, corner_odd,
      observed, wx, mx)
    gathered = lax.all_to_all(message, "gx", 0, 0, tiled=True)
    inflow, = call(solve_kernel, [(8, 32, 128)], [VMEM] * 2)(gathered, increment)
    inflow = lax.all_to_all(inflow, "gx", 0, 0, tiled=True)
    inflow, z_maps = lax.optimization_barrier((inflow, z_maps))
    lines, block_ends, y_ends = call(
        x_finish_kernel,
        [(4, 128, 128), (8,) + rows, (88, 128)],
        [VMEM] * 6,
        [(2, 256, 128), (8,) + rows],
    )(increment, wx, inflow, wy, my, my_all)
    y_all = xor_gather(y_ends, "gy")
    unsmoothed, z_ends = call(
        y_finish_kernel,
        [(2,) + plane, (8,) + rows],
        [SMEM] + [VMEM] * 9,
        [(2, 256, 128), (8,) + rows, (4, 128, 128), (2, 256, 128), (8, 8, 128)],
    )(place, lines, wy, my, block_ends, y_all[0], *y_all[:0:-1], wz)
    z_all = xor_gather(z_ends, "gz")
    smoothed, = call(z_finish_kernel, [(2,) + plane], [SMEM] + [VMEM] * 10, [(2,) + plane, (8,) + rows])(
        place, unsmoothed, wz, *z_maps, z_all[0], *z_all[:0:-1]
    )
    return (predicted, smoothed)


def solution(mesh):
    cells = P(None, "gz", "gx", "gy")
    return jax.shard_map(
        local,
        mesh=mesh,
        in_specs=(cells, cells, P("gz", "gx", "gy"), cells, P("gz", "gx", "gy"), P(), P()),
        out_specs=(cells, cells),
        check_vma=False,
    )
```

```python
import jax
import jax.numpy as jnp
from jax import lax
from jax.experimental import pallas as pl
from jax.experimental.pallas import tpu as pltpu
from jax.sharding import PartitionSpec as P

SWEEPS = 8
DEEP = SWEEPS - 1
NEAR = DEEP - 1
CLASSES = 12
STEPS = 16
PLANES = STEPS + 2 * DEEP
F32 = jnp.float32
VMEM = pl.BlockSpec(memory_space=pltpu.VMEM)
SMEM = pl.BlockSpec(memory_space=pltpu.SMEM)
HBM = pl.BlockSpec(memory_space=pltpu.HBM)
ANY = pl.BlockSpec(memory_space=pl.ANY)


def call(body, outs, specs, scratch=(), flops=1000000, limit=4, copies=0, out_specs=None, aliases=None):
    return pl.pallas_call(
        body,
        out_shape=[shape if hasattr(shape, "dtype") else jax.ShapeDtypeStruct(shape, F32) for shape in outs],
        in_specs=specs,
        out_specs=out_specs or [VMEM] * len(outs),
        input_output_aliases=aliases or {},
        scratch_shapes=[
            pltpu.VMEM(*((shape.shape, shape.dtype) if hasattr(shape, "dtype") else (shape, F32)))
            for shape in scratch
        ]
        + [pltpu.SemaphoreType.DMA((copies,))] * (copies > 0),
        compiler_params=pltpu.CompilerParams(vmem_limit_bytes=limit * 1024 * 1024),
        cost_estimate=pl.CostEstimate(flops=flops, bytes_accessed=1000000, transcendentals=0),
    )


def picked(table, row, classes):
    value = jnp.full(classes.shape, table[row, 0], F32)
    for entry in range(1, CLASSES):
        value = jnp.where(classes == entry, table[row, entry], value)
    return value


def lanes(shape):
    return lax.broadcasted_iota(jnp.int32, shape, len(shape) - 1)


def first_mask(lane):
    return (lane % 14 < 7) & (lane < 84)


def last_mask(lane):
    return ((lane % 14 >= 7) & (lane < 70)) | (lane >= 121)


def by_pairs(place, axis, low, high):
    is_even = place[axis] % 2 == 0
    return jnp.where(is_even, high, low), jnp.where(is_even, low, high)


def sides(place, axis, even, odd):
    high, low = by_pairs(place, axis, odd, even)
    return (
        jnp.where(place[axis] > 0, low, 0.0),
        jnp.where(place[axis] < place[axis + 3] - 1, high, 0.0),
    )


def brought(pairs, sems):
    copies = [pltpu.make_async_copy(a, b, sems.at[i]) for i, (a, b) in enumerate(pairs)]
    for copy in copies:
        copy.start()
    for copy in copies:
        copy.wait()


def coefficients_kernel(
    source_in, capacity_in, transfer_in, classes_in, conductivity,
    units, even, odd,
    edges, source, capacity, transfer, classes, sems,
):
    place = {1: lax.axis_index("gy")}
    brought(((source_in, source), (capacity_in, capacity), (transfer_in, transfer), (classes_in, classes)), sems)

    def layer(z, _):
        transfer_z = transfer[z]
        classes_z = classes[z]
        lane = lanes(classes_z.shape)
        packed = jnp.zeros(classes_z.shape, F32)
        for f in range(2):
            conduct = picked(conductivity, f, classes_z)
            inverse = 1.0 / (capacity[f, z] + 6.0 * conduct + transfer_z)
            for unit, value in (
                (f, source[f, z] * inverse),
                (2 + f, conduct * inverse),
                (4 + f, transfer_z * inverse),
            ):
                units[unit, z] = value
                turned = pltpu.roll(value, 14 * unit, 1) if unit else value
                packed = jnp.where((lane - 14 * unit + 7 + 128) % 128 < 14, turned, packed)
        edges[z] = packed
        return 0

    lax.fori_loop(0, STEPS, layer, 0, unroll=8)

    def pair(z, _):
        upper, lower = (edges[z], edges[z + 8])
        lane = lanes(upper.shape)
        to_low = jnp.where(first_mask(lane), upper, pltpu.roll(lower, 121, 1))
        to_high = jnp.where(last_mask(lane), upper, pltpu.roll(lower, 7, 1))
        even[z], odd[z] = by_pairs(place, 1, to_low, to_high)
        return 0

    lax.fori_loop(0, 8, pair, 0, unroll=4)


def counts(unit):
    return DEEP if unit < 2 else NEAR


X_MAIN = sum(counts(unit) for unit in range(6))
X_ROWS = STEPS * (X_MAIN + NEAR)


def face_row(unit, z):
    if unit == 6:
        return STEPS * X_MAIN + z * NEAR
    return z * X_MAIN + sum(counts(u) for u in range(unit))


def corner_rows():
    offset, rows = (0, [])
    for unit in range(7):
        for d in range(NEAR):
            count = NEAR - d if unit < 2 else NEAR - d - 1
            if count > 0:
                rows.append((unit, d, offset, count))
                offset += count
    return rows, -(-offset // 8) * 8


def face_kernel(place, units, z_even, z_odd, x_even, x_odd):
    for d in range(DEEP):
        for unit in range(6 if d < NEAR else 2):
            at = unit * NEAR + d if d < NEAR else 6 * NEAR + unit
            z_even[at], z_odd[at] = by_pairs(place, 2, units[unit, d], units[unit, STEPS - 1 - d])

    for z in range(STEPS):
        for unit in range(6):
            count = counts(unit)
            low, high = (units[unit, z, pl.ds(0, count)], units[unit, z, pl.ds(STEPS - count, count)])
            even, odd = by_pairs(place, 0, low, high)
            x_even[pl.ds(face_row(unit, z), count)] = even
            x_odd[pl.ds(face_row(unit, z), count)] = odd


def halo_kernel(
    place, y_odd, y_even, _z_even, _z_odd, _x_even, _x_odd, strips, z_even, z_odd, x_even, x_odd,
    to_z_even, to_z_odd, to_x_even, to_x_odd, sems,
):
    def pair(z, _):
        low, high = sides(place, 1, y_even[z], y_odd[z])
        first = first_mask(lanes(high.shape))
        strips[z] = jnp.where(first, high, low)
        strips[z + 8] = jnp.where(first, pltpu.roll(high, 7, 1), pltpu.roll(low, 121, 1))
        return 0

    lax.fori_loop(0, 8, pair, 0, unroll=4)
    for d in range(NEAR):
        to_z_even[d], to_z_odd[d] = by_pairs(place, 2, strips[d], strips[STEPS - 1 - d])
    for z in range(STEPS):
        low, high = (strips[z, pl.ds(0, NEAR)], strips[z, pl.ds(STEPS - NEAR, NEAR)])
        even, odd = by_pairs(place, 0, low, high)
        to_x_even[pl.ds(NEAR * z, NEAR)] = even
        to_x_odd[pl.ds(NEAR * z, NEAR)] = odd
    z_part = pl.ds(6 * NEAR + 2, NEAR)
    x_part = pl.ds(STEPS * X_MAIN, STEPS * NEAR)
    brought(
        (
            (to_z_even, z_even.at[z_part]),
            (to_z_odd, z_odd.at[z_part]),
            (to_x_even, x_even.at[x_part]),
            (to_x_odd, x_odd.at[x_part]),
        ),
        sems,
    )


def corner_kernel(place, x_odd, x_even, _z_even, _observed, even, odd):
    for unit, d, offset, count in corner_rows()[0]:
        ends = []
        for z in (d, STEPS - 1 - d):
            first = face_row(unit, z)
            last = first + counts(unit) - count
            low = sides(place, 0, x_even[pl.ds(last, count)], x_odd[pl.ds(last, count)])[0]
            high = sides(place, 0, x_even[pl.ds(first, count)], x_odd[pl.ds(first, count)])[1]
            ends.append((low, high))
        for x_side in range(2):
            to_even, to_odd = by_pairs(place, 2, ends[0][x_side], ends[1][x_side])
            even[x_side, pl.ds(offset, count)] = to_even
            odd[x_side, pl.ds(offset, count)] = to_odd


def forward(read_value, read_weight, state, write, count=4):
    for i in range(STEPS):
        for g in range(count):
            weight = read_weight(i, g)
            value = read_value(i, g)
            keep = 1.0 - weight
            for k in range(4):
                value = keep * state[g][k] + weight * value
                state[g][k] = value
            write(i, g, value)
    return state


def backward(read_value, read_weight, state, write, count=4):
    return forward(
        lambda i, g: read_value(STEPS - 1 - i, g),
        lambda i, g: read_weight(STEPS - 1 - i, g),
        state,
        lambda i, g, value: write(STEPS - 1 - i, g, value),
        count,
    )


def zeros(count=4):
    return [[jnp.zeros((8, 128), F32) for _ in range(4)] for _ in range(count)]


PAIRS = [(a, b) for a in range(4) for b in range(a, 4)]


def block_maps(read_weights):
    def step(i, carries):
        out = []
        for read_weight, carry in zip(read_weights, carries):
            chain, sums = (list(carry[:4]), list(carry[4:]))
            weight = read_weight(i)
            keep = 1.0 - weight
            for k in range(1, 4):
                chain[k] = chain[k] + weight * chain[k - 1]
            scaled = [weight * value for value in chain]
            chain = [keep * value for value in chain]
            sums = [total + scaled[a] * chain[b] for total, (a, b) in zip(sums, PAIRS)]
            out.append(tuple(chain + sums))
        return tuple(out)

    zero = jnp.zeros((8, 128), F32)
    start = (zero + 1.0,) + (zero,) * 13
    return lax.fori_loop(0, STEPS, step, (start,) * len(read_weights), unroll=4)


def pass_map(maps, state):
    return [sum(maps[k - m] * state[m] for m in range(k + 1)) for k in range(4)]


def coupling(maps, a, b):
    return maps[4 + PAIRS.index((min(a, b), max(a, b)))]


def couple(maps, state):
    return [sum(coupling(maps, k, 3 - m) * state[m] for m in range(4)) for k in range(4)]


def plus(left, right):
    return [a + b for a, b in zip(left, right)]


def chained(maps, ends, low, high):
    count = len(maps)
    lows = [low]
    for s in range(count):
        lows.append(plus(pass_map(maps[s], lows[s]), ends[s][:4]))
    highs = [high]
    for s in reversed(range(count)):
        highs.insert(0, plus(plus(pass_map(maps[s], highs[0]), couple(maps[s], lows[s])), ends[s][4:]))
    return lows, highs


def merged_maps(maps):
    chain, total = (list(maps[0][:4]), list(maps[0][4:]))
    for s in range(1, len(maps)):
        part = maps[s]
        half = [
            [sum(chain[i] * coupling(part, a - i, b) for i in range(a + 1)) for b in range(4)]
            for a in range(4)
        ]
        total = [
            value + sum(chain[j] * half[a][b - j] for j in range(b + 1))
            for value, (a, b) in zip(total, PAIRS)
        ]
        chain = [sum(part[k - m] * chain[m] for m in range(k + 1)) for k in range(4)]
    return chain + total


def maps_kernel(classes, rates, _, wx, wy, wz, mx, my, my_all, mz, by_x, turned):
    def by_layer(z, _):
        here = classes[z]
        for f in range(2):
            wz[f, z] = picked(rates, 4 + f, here)
        return 0

    lax.fori_loop(0, STEPS, by_layer, 0, unroll=4)

    def by_row(z, _):
        by_x[pl.ds(z, STEPS, stride=STEPS), :] = classes[z].astype(F32)
        return 0

    lax.fori_loop(0, STEPS, by_row, 0, unroll=4)

    def x_weights(i, _):
        here = by_x[pl.ds(pl.multiple_of(i * STEPS, 8), STEPS)]
        for f in range(2):
            wx[f, i] = picked(rates, f, here)
        return 0

    lax.fori_loop(0, STEPS, x_weights, 0, unroll=4)
    for h in range(2):
        turned[h] = by_x[128 * h : 128 * h + 128].T

    def y_weights(i, _):
        rows = pl.ds(pl.multiple_of(i * 8, 8), 8)
        for h in range(2):
            here = turned[h, rows]
            for f in range(2):
                wy[2 * f + h, rows] = picked(rates, 2 + f, here)
        return 0

    lax.fori_loop(0, STEPS, y_weights, 0, unroll=4)
    for g in range(4):
        part = pl.ds(8 * (g % 2), 8)
        weights = (
            lambda i, g=g: wx[g // 2, i, part],
            lambda i, g=g: wz[g // 2, i, part],
            lambda i, g=g: wy[g, pl.ds(i, 8, stride=STEPS)],
        )
        for out, maps in zip((mx, mz, my), block_maps(weights)):
            for v in range(14):
                out[v, pl.ds(8 * g, 8)] = maps[v]
    blocks = [[my[v, pl.ds(s, 4, stride=8)] for v in range(14)] for s in range(8)]
    for v, value in enumerate(merged_maps(blocks)):
        my_all[pl.ds(4 * v, 4)] = value


def sweep_kernel(
    place, units, strips, z_even, z_odd, x_even, x_odd, corner_even, corner_odd, observed, wx,
    predicted, increment, ends,
    grid, side, even, odd, passed,
):
    inside = slice(8, 8 + STEPS)

    def own(z, _):
        for unit in range(6):
            grid[unit, z + DEEP, inside] = units[unit, z]
        grid[6, z + DEEP, inside] = strips[z]
        return 0

    lax.fori_loop(0, STEPS, own, 0, unroll=2)
    for z in range(STEPS):
        for unit in range(7):
            count = counts(unit)
            rows = pl.ds(face_row(unit, z), count)
            low, high = sides(place, 0, x_even[rows], x_odd[rows])
            grid[unit, z + DEEP, pl.ds(8 - count, count)] = low
            grid[unit, z + DEEP, pl.ds(8 + STEPS, count)] = high
    for d in range(DEEP):
        for unit in range(7 if d < NEAR else 2):
            at = unit * NEAR + d if d < NEAR else 6 * NEAR + unit
            at = 6 * NEAR + 2 + d if unit == 6 else at
            low, high = sides(place, 2, z_even[at], z_odd[at])
            grid[unit, DEEP - 1 - d, inside] = low
            grid[unit, DEEP + STEPS + d, inside] = high
    for unit, d, offset, count in corner_rows()[0]:
        rows = pl.ds(offset, count)
        for x_side, start in enumerate((8 - count, 8 + STEPS)):
            low, high = sides(place, 2, corner_even[x_side, rows], corner_odd[x_side, rows])
            grid[unit, DEEP - 1 - d, pl.ds(start, count)] = low
            grid[unit, DEEP + STEPS + d, pl.ds(start, count)] = high

    def unpack(z, _):
        packed = grid[6, z]
        for unit in range(6):
            side[unit, z] = pltpu.roll(packed, 128 - 14 * unit, 1) if unit else packed
        return 0

    lax.fori_loop(0, PLANES, unpack, 0, unroll=5)

    everywhere = slice(0, 32)

    def sweep(main_from, side_from, main_to, side_to, rows, side_rows):
        def new_value(f, z, part, coefficients, source, here, other, below, above):
            total = source(f, z - 1, part) + source(f, z + 1, part)
            if part == everywhere:
                total = total + (pltpu.roll(here, 1, 0) + pltpu.roll(here, 31, 0))
            else:
                low, high = (slice(part.start - 1, part.stop - 1), slice(part.start + 1, part.stop + 1))
                total = total + (source(f, z, low) + source(f, z, high))
            total = total + (below + above)
            return coefficients[f, z, part] + coefficients[2 + f, z, part] * total + coefficients[4 + f, z, part] * other

        def layer(z, _):
            main = [main_from(f, z, rows) for f in range(2)]
            edge = [side_from(f, z, rows) for f in range(2)]
            lane = lanes(main[0].shape)
            for f in range(2):
                below = (pltpu.roll(main[f], 1, 1), pltpu.roll(edge[f], 1, 1))
                above = (pltpu.roll(main[f], 127, 1), pltpu.roll(edge[f], 127, 1))
                beside = [
                    (jnp.where(lane == 0, below[1 - i], below[i]), jnp.where(lane == 127, above[1 - i], above[i]))
                    for i in range(2)
                ]
                main_to(f, z, rows, new_value(f, z, rows, grid, main_from, main[f], main[1 - f], *beside[0]))
                if side_rows is not None:
                    side_to(f, z, rows, new_value(f, z, rows, side, side_from, edge[f], edge[1 - f], *beside[1]))
            return 0

        return layer

    buffers = (even, odd)
    for s in range(2, SWEEPS + 1):
        reach = SWEEPS - s
        if s == 2:
            main_from, side_from = (lambda f, z, part: grid[f, z, part], lambda f, z, part: side[f, z, part])
        else:
            old = buffers[s % 2]
            main_from = lambda f, z, part, old=old: old[f, z, part]
            side_from = lambda f, z, part, old=old: old[2 + f, z, part]
        new = buffers[(s + 1) % 2]

        def main_to(f, z, part, value, new=new):
            new[f, z, part] = value

        def side_to(f, z, part, value, new=new):
            new[2 + f, z, part] = value

        def last_to(f, z, part, value):
            predicted[f, z - DEEP] = value
            increment[f, pl.ds(z - DEEP, STEPS, stride=STEPS), :] = observed[f, z - DEEP] - value

        first, last = (DEEP - reach, DEEP + STEPS + reach - 1)
        if reach == 0:
            layer = sweep(main_from, side_from, last_to, None, inside, None)
            lax.fori_loop(first, last + 1, layer, 0, unroll=8)
        else:
            outermost = sweep(main_from, side_from, main_to, None, inside, None)
            outermost(first, 0)
            outermost(last, 0)
            layer = sweep(main_from, side_from, main_to, side_to, everywhere, everywhere)
            lax.fori_loop(first + 1, last, layer, 0, unroll=8)

    def weight(i, g):
        return wx[g // 2, i, pl.ds(8 * (g % 2), 8)]

    def put(i, g, value):
        passed[i, pl.ds(8 * g, 8)] = value

    def value(i, g):
        return increment[g // 2, pl.ds(STEPS * i + 8 * (g % 2), 8)]

    low = forward(value, weight, zeros(), put)
    high = backward(lambda i, g: passed[i, pl.ds(8 * g, 8)], weight, zeros(), lambda i, g, value: None)
    for g in range(4):
        for k in range(4):
            ends[k, pl.ds(8 * g, 8)] = low[g][k]
            ends[4 + k, pl.ds(8 * g, 8)] = high[g][k]


GROUPS = [pl.ds(8 * g, 8) for g in range(4)]


def values_of(ref, rows, count):
    return [ref[v, rows] for v in range(count)]


def no_state(rows=8):
    return [jnp.zeros((rows, 128), F32)] * 4


def laid_end_to_end(first, second):
    return [sum(first[k - m] * second[m] for m in range(k + 1)) for k in range(4)]


def run_maps_kernel(place, maps_0, maps_1, maps_2, maps_3, joint, around):
    maps = (maps_0, maps_1, maps_2, maps_3)
    for p in range(4):

        @pl.when(place[0] % 4 == p)
        def _(p=p):
            for rows in GROUPS:
                run = [values_of(maps[j ^ p], rows, 14) for j in range(4)]
                zero = jnp.zeros((8, 128), F32)
                unit = [zero + 1.0] + [zero] * 3
                before = unit
                for j in range(p):
                    before = laid_end_to_end(before, run[j][:4])
                through = laid_end_to_end(before, run[p][:4])
                after = merged_maps(run[p + 1 :]) if p < 3 else unit + [zero] * 10
                for v, value in enumerate(merged_maps(run)[4:]):
                    joint[v, rows] = value
                for v, value in enumerate(before + through + after):
                    around[v, rows] = value


def run_ends_kernel(place, maps_0, maps_1, maps_2, maps_3, ends_0, ends_3, ends_2, ends_1, _, joint, inner):
    maps, ends = ((maps_0, maps_1, maps_2, maps_3), (ends_0, ends_1, ends_2, ends_3))
    for p in range(4):

        @pl.when(place[0] % 4 == p)
        def _(p=p):
            for rows in GROUPS:
                lows, highs = chained(
                    [values_of(maps[j ^ p], rows, 14) for j in range(4)],
                    [values_of(ends[j ^ p], rows, 8) for j in range(4)],
                    no_state(),
                    no_state(),
                )
                for k in range(4):
                    joint[k, rows] = lows[4][k]
                    joint[4 + k, rows] = highs[0][k]
                    inner[k, rows] = lows[p][k]
                    inner[4 + k, rows] = highs[p + 1][k]


def outer_inflow(is_high, own_ends, other_ends, other_coupling):
    low = [jnp.where(is_high, value, 0.0) for value in other_ends[:4]]
    back = plus(couple([None] * 4 + other_coupling, own_ends[:4]), other_ends[4:])
    return low, [jnp.where(is_high, 0.0, value) for value in back]


def y_value(ref):
    return lambda i, g: ref[g, pl.ds(i, 8, stride=STEPS)]


def x_finish_kernel(
    place, increment, wx, around, inner, joint, other_joint, other_coupling, wy, my, my_all,
    lines, ends, message, passed, start,
):
    for rows in GROUPS:
        outer_low, outer_high = outer_inflow(
            place[0] >= 4,
            values_of(joint, rows, 8),
            values_of(other_joint, rows, 8),
            values_of(other_coupling, rows, 10),
        )
        maps, inside = (values_of(around, rows, 22), values_of(inner, rows, 8))
        low = plus(inside[:4], pass_map(maps[:4], outer_low))
        back = couple(maps[8:], pass_map(maps[4:8], outer_low))
        high = plus(plus(inside[4:], pass_map(maps[8:], outer_high)), back)
        inflow_writer(start, rows)(low, high)

    def weight(i, g):
        return wx[g // 2, i, pl.ds(8 * (g % 2), 8)]

    def value(i, g):
        return increment[g // 2, pl.ds(STEPS * i + 8 * (g % 2), 8)]

    def put(i, g, value):
        passed[g // 2, pl.ds(STEPS * i + 8 * (g % 2), 8)] = value

    def passed_value(i, g):
        return passed[g // 2, pl.ds(STEPS * i + 8 * (g % 2), 8)]

    low = [[start[k, pl.ds(8 * g, 8)] for k in range(4)] for g in range(4)]
    high = [[start[4 + k, pl.ds(8 * g, 8)] for k in range(4)] for g in range(4)]
    forward(value, weight, low, put)
    backward(passed_value, weight, high, put)
    for f in range(2):
        for h in range(2):
            lines[2 * f + h] = passed[f, pl.ds(128 * h, 128)].T

    def y_put(i, g, value):
        passed[g // 2, pl.ds(128 * (g % 2) + 8 * i, 8)] = value

    def y_passed(i, g):
        return passed[g // 2, pl.ds(128 * (g % 2) + 8 * i, 8)]

    low = forward(y_value(lines), y_value(wy), zeros(), y_put)
    high = backward(y_passed, y_value(wy), zeros(), lambda i, g, value: None)
    for g in range(4):
        for k in range(4):
            ends[k, pl.ds(8 * g, 8)] = low[g][k]
            ends[4 + k, pl.ds(8 * g, 8)] = high[g][k]
    maps = [[my[v, pl.ds(s, 4, stride=8)] for v in range(14)] for s in range(8)]
    block_ends = [[ends[v, pl.ds(s, 4, stride=8)] for v in range(8)] for s in range(8)]
    zero = [jnp.zeros((4, 128), F32)] * 4
    lows, highs = chained(maps, block_ends, zero, zero)
    for k in range(4):
        message[pl.ds(4 * k, 4)] = lows[8][k]
        message[pl.ds(16 + 4 * k, 4)] = highs[0][k]
    message[pl.ds(32, 56)] = my_all[...]


def own_inflow(position, lines):
    count = 4
    for p in range(count):

        @pl.when(position == p)
        def _(p=p):
            for maps, ends, outer_low, outer_high, write in lines:
                low = outer_low
                for j in range(p):
                    low = plus(pass_map(maps(j ^ p), low), ends(j ^ p)[:4])
                inflow, lows = (low, [])
                for j in range(p, count):
                    lows.append(inflow)
                    if j < count - 1:
                        inflow = plus(pass_map(maps(j ^ p), inflow), ends(j ^ p)[:4])
                high = outer_high
                for j in range(count - 1, p, -1):
                    coupled = couple(maps(j ^ p), lows[j - p])
                    high = plus(plus(pass_map(maps(j ^ p), high), coupled), ends(j ^ p)[4:])
                write(low, high)


def inflow_writer(ref, rows):
    def write(low, high):
        for k in range(4):
            ref[k, rows] = low[k]
            ref[4 + k, rows] = high[k]

    return write


def pair_blocks(place, own, partner):
    is_low = place[1] % 2 == 0
    rows = [pl.ds(4 * v, 4) for v in range(22)]
    blocks = (
        [jnp.where(is_low, own[r], partner[r]) for r in rows],
        [jnp.where(is_low, partner[r], own[r]) for r in rows],
    )
    return [b[8:] for b in blocks], [b[:8] for b in blocks]


def y_pair_kernel(place, own, partner, joint):
    maps, ends = pair_blocks(place, own, partner)
    lows, highs = chained(maps, ends, no_state(4), no_state(4))
    for v, value in enumerate(lows[2] + highs[0] + merged_maps(maps)):
        joint[pl.ds(4 * v, 4)] = value


def y_finish_kernel(
    place, lines, wy, my, block_ends, own, partner, joint, other_joint, wz, unsmoothed, message,
    passed, start, done, by_row,
):
    own_joint, other = ([ref[pl.ds(4 * v, 4)] for v in range(22)] for ref in (joint, other_joint))
    outer = outer_inflow(place[1] >= 2, own_joint[:8], other[:8], other[12:])
    pair_lows, pair_highs = chained(*pair_blocks(place, own, partner), *outer)
    is_low = place[1] % 2 == 0
    low = [jnp.where(is_low, a, b) for a, b in zip(pair_lows[0], pair_lows[1])]
    high = [jnp.where(is_low, a, b) for a, b in zip(pair_highs[1], pair_highs[2])]
    maps = [[my[v, pl.ds(s, 4, stride=8)] for v in range(14)] for s in range(8)]
    blocks = [[block_ends[v, pl.ds(s, 4, stride=8)] for v in range(8)] for s in range(8)]
    lows, highs = chained(maps, blocks, low, high)
    for s in range(8):
        for k in range(4):
            start[k, pl.ds(s, 4, stride=8), :] = lows[s][k]
            start[4 + k, pl.ds(s, 4, stride=8), :] = highs[s + 1][k]

    def put(i, g, value):
        passed[g // 2, pl.ds(128 * (g % 2) + 8 * i, 8)] = value

    def passed_value(i, g):
        return passed[g // 2, pl.ds(128 * (g % 2) + 8 * i, 8)]

    def put_line(i, g, value):
        done[g, pl.ds(i, 8, stride=STEPS), :] = value

    low = [[start[k, pl.ds(8 * g, 8)] for k in range(4)] for g in range(4)]
    high = [[start[4 + k, pl.ds(8 * g, 8)] for k in range(4)] for g in range(4)]
    forward(y_value(lines), y_value(wy), low, put)
    backward(passed_value, y_value(wy), high, put_line)
    for g in range(4):
        by_row[g // 2, pl.ds(128 * (g % 2), 128)] = done[g].T

    def value(i, g):
        return by_row[g // 2, pl.ds(i + 128 * (g % 2), 8, stride=STEPS)]

    def weight(i, g):
        return wz[g // 2, i, pl.ds(8 * (g % 2), 8)]

    for i in range(STEPS):
        for g in range(4):
            unsmoothed[g // 2, i, pl.ds(8 * (g % 2), 8)] = value(i, g)

    low = forward(value, weight, zeros(), put)
    high = backward(passed_value, weight, zeros(), lambda i, g, value: None)
    for g in range(4):
        for k in range(4):
            message[k, pl.ds(8 * g, 8)] = low[g][k]
            message[4 + k, pl.ds(8 * g, 8)] = high[g][k]


def z_finish_kernel(
    place, unsmoothed, wz, maps_0, maps_1, maps_2, maps_3, ends_0, ends_3, ends_2, ends_1, smoothed, passed, inflow
):
    maps = (maps_0, maps_1, maps_2, maps_3)
    ends = (ends_0, ends_1, ends_2, ends_3)
    own_inflow(
        place[2],
        [
            (
                lambda s, rows=rows: values_of(maps[s], rows, 14),
                lambda s, rows=rows: values_of(ends[s], rows, 8),
                no_state(),
                no_state(),
                inflow_writer(inflow, rows),
            )
            for rows in GROUPS
        ],
    )
    lows = [[inflow[k, pl.ds(8 * g, 8)] for k in range(4)] for g in range(4)]
    highs = [[inflow[4 + k, pl.ds(8 * g, 8)] for k in range(4)] for g in range(4)]

    def value(i, g):
        return unsmoothed[g // 2, i, pl.ds(8 * (g % 2), 8)]

    def weight(i, g):
        return wz[g // 2, i, pl.ds(8 * (g % 2), 8)]

    def put(i, g, value):
        passed[g // 2, i, pl.ds(8 * (g % 2), 8)] = value

    def put_last(i, g, value):
        smoothed[g // 2, i, pl.ds(8 * (g % 2), 8)] = value

    forward(value, weight, lows, put)
    backward(lambda i, g: passed[g // 2, i, pl.ds(8 * (g % 2), 8)], weight, highs, put_last)


def pair_swaps(axis, spare, value_even, value_odd):
    axes = tuple(sorted((axis, spare)))
    count, others = (lax.axis_size(axis), lax.axis_size(spare))

    def flat(i, k):
        return i * others + k if axis == axes[0] else k * count + i

    odd = []
    for i in range(count):
        for k in range(others):
            j = i + 1 if i % 2 else i - 1
            odd.append((flat(i, k), flat(j, k) if 0 <= j < count else flat(i, k ^ 1)))
    from_even = lax.ppermute(value_even, axis, [(i, i ^ 1) for i in range(count)])
    from_odd = lax.ppermute(value_odd, axes, odd)
    return from_even, from_odd


def xor_swap(value, axis, s):
    return lax.ppermute(value, axis, [(i, i ^ s) for i in range(lax.axis_size(axis))])


def xor_gather(value, axis):
    return [value] + [xor_swap(value, axis, s) for s in (1, 2, 3)]


def local(source, capacity, transfer, observed, classes, conductivity, filter_rates):
    axes = ("gx", "gy", "gz")
    place = jnp.stack([lax.axis_index(a) for a in axes] + [jnp.int32(lax.axis_size(a)) for a in axes])
    rates = filter_rates.reshape(6, CLASSES)
    plane = (STEPS, STEPS, 128)
    units, y_even, y_odd = call(
        coefficients_kernel,
        [(6,) + plane, (8, STEPS, 128), (8, STEPS, 128)],
        [HBM] * 4 + [SMEM],
        [plane, (2,) + plane, (2,) + plane, plane, jax.ShapeDtypeStruct(plane, jnp.int32)],
        limit=60,
        copies=4,
    )(source, capacity, transfer, classes, conductivity)
    y_even, y_odd = pair_swaps("gy", "gz", y_even, y_odd)

    z_face = (7 * NEAR + 2, STEPS, 128)
    x_face = (X_ROWS, 128)
    corners = (2, corner_rows()[1], 128)
    faces = call(face_kernel, [z_face, z_face, x_face, x_face], [SMEM, VMEM])(place, units)
    strips, z_even, z_odd, x_even, x_odd = call(
        halo_kernel,
        [plane, z_face, z_face, x_face, x_face],
        [SMEM] + [VMEM] * 2 + [ANY] * 4,
        [(NEAR,) + plane[1:]] * 2 + [(STEPS * NEAR, 128)] * 2,
        out_specs=[VMEM] + [ANY] * 4,
        aliases={3: 1, 4: 2, 5: 3, 6: 4},
        copies=4,
    )(place, y_odd, y_even, *faces)
    x_even, x_odd = pair_swaps("gx", "gy", x_even, x_odd)
    z_even, z_odd = pair_swaps("gz", "gy", z_even, z_odd)

    rows = (32, 128)
    wx, wy, wz, mx, my, my_all, mz, _, _ = call(
        maps_kernel,
        [(2,) + plane, (4, 128, 128), (2,) + plane, (14,) + rows, (14,) + rows, (56, 128), (14,) + rows,
         (256, 128), (2, 128, 128)],
        [VMEM, SMEM, VMEM],
    )(classes, rates, strips)
    x_odd, wx, mx = lax.optimization_barrier((x_odd, wx, mx))
    x_maps = [mx] + [xor_swap(mx, "gx", s) for s in (1, 2)]
    corner_even, corner_odd = call(corner_kernel, [corners, corners], [SMEM] + [VMEM] * 4)(
        place, x_odd, x_even, z_even, observed
    )
    mx, corner_even, z_odd = lax.optimization_barrier((mx, corner_even, z_odd))
    corner_even, corner_odd = pair_swaps("gz", "gy", corner_even, corner_odd)
    x_maps.append(xor_swap(mx, "gx", 3))

    padded = (PLANES, 32, 128)
    predicted, increment, x_ends = call(
        sweep_kernel,
        [(2,) + plane, (2, 256, 128), (8,) + rows],
        [SMEM] + [VMEM] * 10,
        [(7,) + padded, (6,) + padded, (4,) + padded, (4,) + padded, (STEPS,) + rows],
        limit=16,
    )(place, units, strips, z_even, z_odd, x_even, x_odd, corner_even, corner_odd, observed, wx)
    x_all = xor_gather(x_ends, "gx")
    coupling_x, around = call(run_maps_kernel, [(10,) + rows, (22,) + rows], [SMEM] + [VMEM] * 4)(place, *x_maps)
    other_coupling = xor_swap(coupling_x, "gx", 4)
    x_run = x_maps + [x_all[0]] + x_all[:0:-1]
    joint, inner = call(run_ends_kernel, [(8,) + rows] * 2, [SMEM] + [VMEM] * 9)(place, *x_run, increment)
    other_joint = xor_swap(joint, "gx", 4)
    mz, joint = lax.optimization_barrier((mz, joint))
    z_maps = xor_gather(mz, "gz")
    lines, block_ends, y_ends = call(
        x_finish_kernel,
        [(4, 128, 128), (8,) + rows, (88, 128)],
        [SMEM] + [VMEM] * 10,
        [(2, 256, 128), (8,) + rows],
    )(place, increment, wx, around, inner, joint, other_joint, other_coupling, wy, my, my_all)
    y_partner = xor_swap(y_ends, "gy", 1)
    y_joint, = call(y_pair_kernel, [(88, 128)], [SMEM] + [VMEM] * 2)(place, y_ends, y_partner)
    y_other = xor_swap(y_joint, "gy", 2)
    unsmoothed, z_ends = call(
        y_finish_kernel,
        [(2,) + plane, (8,) + rows],
        [SMEM] + [VMEM] * 9,
        [(2, 256, 128), (8,) + rows, (4, 128, 128), (2, 256, 128)],
    )(place, lines, wy, my, block_ends, y_ends, y_partner, y_joint, y_other, wz)
    z_all = xor_gather(z_ends, "gz")
    smoothed, = call(z_finish_kernel, [(2,) + plane], [SMEM] + [VMEM] * 10, [(2,) + plane, (8,) + rows])(
        place, unsmoothed, wz, *z_maps, z_all[0], *z_all[:0:-1]
    )
    return (predicted, smoothed)


def solution(mesh):
    cells = P(None, "gz", "gx", "gy")
    return jax.shard_map(
        local,
        mesh=mesh,
        in_specs=(cells, cells, P("gz", "gx", "gy"), cells, P("gz", "gx", "gy"), P(), P()),
        out_specs=(cells, cells),
        check_vma=False,
    )
```

```python
import jax
import jax.numpy as jnp
from jax import lax
from jax.experimental import pallas as pl
from jax.experimental.pallas import tpu as pltpu
from jax.sharding import PartitionSpec as P

SWEEPS = 8
DEEP = SWEEPS - 1
NEAR = DEEP - 1
CLASSES = 12
STEPS = 16
PLANES = STEPS + 2 * DEEP
F32 = jnp.float32
VMEM = pl.BlockSpec(memory_space=pltpu.VMEM)
SMEM = pl.BlockSpec(memory_space=pltpu.SMEM)
HBM = pl.BlockSpec(memory_space=pltpu.HBM)
ANY = pl.BlockSpec(memory_space=pl.ANY)


def call(body, outs, specs, scratch=(), flops=1000000, limit=4, copies=0, out_specs=None, aliases=None):
    return pl.pallas_call(
        body,
        out_shape=[shape if hasattr(shape, "dtype") else jax.ShapeDtypeStruct(shape, F32) for shape in outs],
        in_specs=specs,
        out_specs=out_specs or [VMEM] * len(outs),
        input_output_aliases=aliases or {},
        scratch_shapes=[
            pltpu.VMEM(*((shape.shape, shape.dtype) if hasattr(shape, "dtype") else (shape, F32)))
            for shape in scratch
        ]
        + [pltpu.SemaphoreType.DMA((copies,))] * (copies > 0),
        compiler_params=pltpu.CompilerParams(vmem_limit_bytes=limit * 1024 * 1024),
        cost_estimate=pl.CostEstimate(flops=flops, bytes_accessed=1000000, transcendentals=0),
    )


def picked(table, row, classes):
    value = jnp.full(classes.shape, table[row, 0], F32)
    for entry in range(1, CLASSES):
        value = jnp.where(classes == entry, table[row, entry], value)
    return value


def lanes(shape):
    return lax.broadcasted_iota(jnp.int32, shape, len(shape) - 1)


def first_mask(lane):
    return (lane % 14 < 7) & (lane < 84)


def last_mask(lane):
    return ((lane % 14 >= 7) & (lane < 70)) | (lane >= 121)


def by_pairs(place, axis, low, high):
    is_even = place[axis] % 2 == 0
    return jnp.where(is_even, high, low), jnp.where(is_even, low, high)


def sides(place, axis, even, odd):
    high, low = by_pairs(place, axis, odd, even)
    return (
        jnp.where(place[axis] > 0, low, 0.0),
        jnp.where(place[axis] < place[axis + 3] - 1, high, 0.0),
    )


def brought(pairs, sems):
    copies = [pltpu.make_async_copy(a, b, sems.at[i]) for i, (a, b) in enumerate(pairs)]
    for copy in copies:
        copy.start()
    for copy in copies:
        copy.wait()


def coefficients_kernel(
    source_in, capacity_in, transfer_in, classes_in, conductivity,
    units, even, odd,
    edges, source, capacity, transfer, classes, sems,
):
    place = {1: lax.axis_index("gy")}
    brought(((source_in, source), (capacity_in, capacity), (transfer_in, transfer), (classes_in, classes)), sems)

    def layer(z, _):
        transfer_z = transfer[z]
        classes_z = classes[z]
        lane = lanes(classes_z.shape)
        packed = jnp.zeros(classes_z.shape, F32)
        for f in range(2):
            conduct = picked(conductivity, f, classes_z)
            inverse = 1.0 / (capacity[f, z] + 6.0 * conduct + transfer_z)
            for unit, value in (
                (f, source[f, z] * inverse),
                (2 + f, conduct * inverse),
                (4 + f, transfer_z * inverse),
            ):
                units[unit, z] = value
                turned = pltpu.roll(value, 14 * unit, 1) if unit else value
                packed = jnp.where((lane - 14 * unit + 7 + 128) % 128 < 14, turned, packed)
        edges[z] = packed
        return 0

    lax.fori_loop(0, STEPS, layer, 0, unroll=8)

    def pair(z, _):
        upper, lower = (edges[z], edges[z + 8])
        lane = lanes(upper.shape)
        to_low = jnp.where(first_mask(lane), upper, pltpu.roll(lower, 121, 1))
        to_high = jnp.where(last_mask(lane), upper, pltpu.roll(lower, 7, 1))
        even[z], odd[z] = by_pairs(place, 1, to_low, to_high)
        return 0

    lax.fori_loop(0, 8, pair, 0, unroll=4)


def counts(unit):
    return DEEP if unit < 2 else NEAR


X_MAIN = sum(counts(unit) for unit in range(6))
X_ROWS = STEPS * (X_MAIN + NEAR)


def face_row(unit, z):
    if unit == 6:
        return STEPS * X_MAIN + z * NEAR
    return z * X_MAIN + sum(counts(u) for u in range(unit))


def corner_rows():
    offset, rows = (0, [])
    for unit in range(7):
        for d in range(NEAR):
            count = NEAR - d if unit < 2 else NEAR - d - 1
            if count > 0:
                rows.append((unit, d, offset, count))
                offset += count
    return rows, -(-offset // 8) * 8


def face_kernel(place, units, z_even, z_odd, x_even, x_odd):
    for d in range(DEEP):
        for unit in range(6 if d < NEAR else 2):
            at = unit * NEAR + d if d < NEAR else 6 * NEAR + unit
            z_even[at], z_odd[at] = by_pairs(place, 2, units[unit, d], units[unit, STEPS - 1 - d])

    for z in range(STEPS):
        for unit in range(6):
            count = counts(unit)
            low, high = (units[unit, z, pl.ds(0, count)], units[unit, z, pl.ds(STEPS - count, count)])
            even, odd = by_pairs(place, 0, low, high)
            x_even[pl.ds(face_row(unit, z), count)] = even
            x_odd[pl.ds(face_row(unit, z), count)] = odd


def halo_kernel(
    place, y_odd, y_even, _z_even, _z_odd, _x_even, _x_odd, strips, z_even, z_odd, x_even, x_odd,
    to_z_even, to_z_odd, to_x_even, to_x_odd, sems,
):
    def pair(z, _):
        low, high = sides(place, 1, y_even[z], y_odd[z])
        first = first_mask(lanes(high.shape))
        strips[z] = jnp.where(first, high, low)
        strips[z + 8] = jnp.where(first, pltpu.roll(high, 7, 1), pltpu.roll(low, 121, 1))
        return 0

    lax.fori_loop(0, 8, pair, 0, unroll=4)
    for d in range(NEAR):
        to_z_even[d], to_z_odd[d] = by_pairs(place, 2, strips[d], strips[STEPS - 1 - d])
    for z in range(STEPS):
        low, high = (strips[z, pl.ds(0, NEAR)], strips[z, pl.ds(STEPS - NEAR, NEAR)])
        even, odd = by_pairs(place, 0, low, high)
        to_x_even[pl.ds(NEAR * z, NEAR)] = even
        to_x_odd[pl.ds(NEAR * z, NEAR)] = odd
    z_part = pl.ds(6 * NEAR + 2, NEAR)
    x_part = pl.ds(STEPS * X_MAIN, STEPS * NEAR)
    brought(
        (
            (to_z_even, z_even.at[z_part]),
            (to_z_odd, z_odd.at[z_part]),
            (to_x_even, x_even.at[x_part]),
            (to_x_odd, x_odd.at[x_part]),
        ),
        sems,
    )


def corner_kernel(place, x_odd, x_even, _z_even, _observed, even, odd):
    for unit, d, offset, count in corner_rows()[0]:
        ends = []
        for z in (d, STEPS - 1 - d):
            first = face_row(unit, z)
            last = first + counts(unit) - count
            low = sides(place, 0, x_even[pl.ds(last, count)], x_odd[pl.ds(last, count)])[0]
            high = sides(place, 0, x_even[pl.ds(first, count)], x_odd[pl.ds(first, count)])[1]
            ends.append((low, high))
        for x_side in range(2):
            to_even, to_odd = by_pairs(place, 2, ends[0][x_side], ends[1][x_side])
            even[x_side, pl.ds(offset, count)] = to_even
            odd[x_side, pl.ds(offset, count)] = to_odd


def forward(read_value, read_weight, state, write, count=4):
    for i in range(STEPS):
        for g in range(count):
            weight = read_weight(i, g)
            value = read_value(i, g)
            keep = 1.0 - weight
            for k in range(4):
                value = keep * state[g][k] + weight * value
                state[g][k] = value
            write(i, g, value)
    return state


def backward(read_value, read_weight, state, write, count=4):
    return forward(
        lambda i, g: read_value(STEPS - 1 - i, g),
        lambda i, g: read_weight(STEPS - 1 - i, g),
        state,
        lambda i, g, value: write(STEPS - 1 - i, g, value),
        count,
    )


def zeros(count=4):
    return [[jnp.zeros((8, 128), F32) for _ in range(4)] for _ in range(count)]


PAIRS = [(a, b) for a in range(4) for b in range(a, 4)]


def block_maps(read_weights):
    def step(i, carries):
        out = []
        for read_weight, carry in zip(read_weights, carries):
            chain, sums = (list(carry[:4]), list(carry[4:]))
            weight = read_weight(i)
            keep = 1.0 - weight
            for k in range(1, 4):
                chain[k] = chain[k] + weight * chain[k - 1]
            scaled = [weight * value for value in chain]
            chain = [keep * value for value in chain]
            sums = [total + scaled[a] * chain[b] for total, (a, b) in zip(sums, PAIRS)]
            out.append(tuple(chain + sums))
        return tuple(out)

    zero = jnp.zeros((8, 128), F32)
    start = (zero + 1.0,) + (zero,) * 13
    return lax.fori_loop(0, STEPS, step, (start,) * len(read_weights), unroll=4)


def pass_map(maps, state):
    return [sum(maps[k - m] * state[m] for m in range(k + 1)) for k in range(4)]


def coupling(maps, a, b):
    return maps[4 + PAIRS.index((min(a, b), max(a, b)))]


def couple(maps, state):
    return [sum(coupling(maps, k, 3 - m) * state[m] for m in range(4)) for k in range(4)]


def plus(left, right):
    return [a + b for a, b in zip(left, right)]


def chained(maps, ends, low, high):
    count = len(maps)
    lows = [low]
    for s in range(count):
        lows.append(plus(pass_map(maps[s], lows[s]), ends[s][:4]))
    highs = [high]
    for s in reversed(range(count)):
        highs.insert(0, plus(plus(pass_map(maps[s], highs[0]), couple(maps[s], lows[s])), ends[s][4:]))
    return lows, highs


def merged_maps(maps):
    chain, total = (list(maps[0][:4]), list(maps[0][4:]))
    for s in range(1, len(maps)):
        part = maps[s]
        half = [
            [sum(chain[i] * coupling(part, a - i, b) for i in range(a + 1)) for b in range(4)]
            for a in range(4)
        ]
        total = [
            value + sum(chain[j] * half[a][b - j] for j in range(b + 1))
            for value, (a, b) in zip(total, PAIRS)
        ]
        chain = [sum(part[k - m] * chain[m] for m in range(k + 1)) for k in range(4)]
    return chain + total


def maps_kernel(classes, rates, _, wx, wy, wz, mx, my, my_all, mz, by_x, turned):
    def by_layer(z, _):
        here = classes[z]
        for f in range(2):
            wz[f, z] = picked(rates, 4 + f, here)
        return 0

    lax.fori_loop(0, STEPS, by_layer, 0, unroll=4)

    def by_row(z, _):
        by_x[pl.ds(z, STEPS, stride=STEPS), :] = classes[z].astype(F32)
        return 0

    lax.fori_loop(0, STEPS, by_row, 0, unroll=4)

    def x_weights(i, _):
        here = by_x[pl.ds(pl.multiple_of(i * STEPS, 8), STEPS)]
        for f in range(2):
            wx[f, i] = picked(rates, f, here)
        return 0

    lax.fori_loop(0, STEPS, x_weights, 0, unroll=4)
    for h in range(2):
        turned[h] = by_x[128 * h : 128 * h + 128].T

    def y_weights(i, _):
        rows = pl.ds(pl.multiple_of(i * 8, 8), 8)
        for h in range(2):
            here = turned[h, rows]
            for f in range(2):
                wy[2 * f + h, rows] = picked(rates, 2 + f, here)
        return 0

    lax.fori_loop(0, STEPS, y_weights, 0, unroll=4)
    for g in range(4):
        part = pl.ds(8 * (g % 2), 8)
        weights = (
            lambda i, g=g: wx[g // 2, i, part],
            lambda i, g=g: wz[g // 2, i, part],
            lambda i, g=g: wy[g, pl.ds(i, 8, stride=STEPS)],
        )
        for out, maps in zip((mx, mz, my), block_maps(weights)):
            for v in range(14):
                out[v, pl.ds(8 * g, 8)] = maps[v]
    blocks = [[my[v, pl.ds(s, 4, stride=8)] for v in range(14)] for s in range(8)]
    for v, value in enumerate(merged_maps(blocks)):
        my_all[pl.ds(4 * v, 4)] = value


def sweep_kernel(
    place, units, strips, z_even, z_odd, x_even, x_odd, corner_even, corner_odd, observed, wx,
    predicted, increment, ends,
    grid, side, even, odd, passed,
):
    inside = slice(8, 8 + STEPS)

    def own(z, _):
        for unit in range(6):
            grid[unit, z + DEEP, inside] = units[unit, z]
        grid[6, z + DEEP, inside] = strips[z]
        return 0

    lax.fori_loop(0, STEPS, own, 0, unroll=2)
    for z in range(STEPS):
        for unit in range(7):
            count = counts(unit)
            rows = pl.ds(face_row(unit, z), count)
            low, high = sides(place, 0, x_even[rows], x_odd[rows])
            grid[unit, z + DEEP, pl.ds(8 - count, count)] = low
            grid[unit, z + DEEP, pl.ds(8 + STEPS, count)] = high
    for d in range(DEEP):
        for unit in range(7 if d < NEAR else 2):
            at = unit * NEAR + d if d < NEAR else 6 * NEAR + unit
            at = 6 * NEAR + 2 + d if unit == 6 else at
            low, high = sides(place, 2, z_even[at], z_odd[at])
            grid[unit, DEEP - 1 - d, inside] = low
            grid[unit, DEEP + STEPS + d, inside] = high
    for unit, d, offset, count in corner_rows()[0]:
        rows = pl.ds(offset, count)
        for x_side, start in enumerate((8 - count, 8 + STEPS)):
            low, high = sides(place, 2, corner_even[x_side, rows], corner_odd[x_side, rows])
            grid[unit, DEEP - 1 - d, pl.ds(start, count)] = low
            grid[unit, DEEP + STEPS + d, pl.ds(start, count)] = high

    def unpack(z, _):
        packed = grid[6, z]
        for unit in range(6):
            side[unit, z] = pltpu.roll(packed, 128 - 14 * unit, 1) if unit else packed
        return 0

    lax.fori_loop(0, PLANES, unpack, 0, unroll=5)

    everywhere = slice(0, 32)

    def sweep(main_from, side_from, main_to, side_to, rows, side_rows):
        def new_value(f, z, part, coefficients, source, here, other, below, above):
            total = source(f, z - 1, part) + source(f, z + 1, part)
            if part == everywhere:
                total = total + (pltpu.roll(here, 1, 0) + pltpu.roll(here, 31, 0))
            else:
                low, high = (slice(part.start - 1, part.stop - 1), slice(part.start + 1, part.stop + 1))
                total = total + (source(f, z, low) + source(f, z, high))
            total = total + (below + above)
            return coefficients[f, z, part] + coefficients[2 + f, z, part] * total + coefficients[4 + f, z, part] * other

        def layer(z, _):
            main = [main_from(f, z, rows) for f in range(2)]
            edge = [side_from(f, z, rows) for f in range(2)]
            lane = lanes(main[0].shape)
            for f in range(2):
                below = (pltpu.roll(main[f], 1, 1), pltpu.roll(edge[f], 1, 1))
                above = (pltpu.roll(main[f], 127, 1), pltpu.roll(edge[f], 127, 1))
                beside = [
                    (jnp.where(lane == 0, below[1 - i], below[i]), jnp.where(lane == 127, above[1 - i], above[i]))
                    for i in range(2)
                ]
                main_to(f, z, rows, new_value(f, z, rows, grid, main_from, main[f], main[1 - f], *beside[0]))
                if side_rows is not None:
                    side_to(f, z, rows, new_value(f, z, rows, side, side_from, edge[f], edge[1 - f], *beside[1]))
            return 0

        return layer

    buffers = (even, odd)
    for s in range(2, SWEEPS + 1):
        reach = SWEEPS - s
        if s == 2:
            main_from, side_from = (lambda f, z, part: grid[f, z, part], lambda f, z, part: side[f, z, part])
        else:
            old = buffers[s % 2]
            main_from = lambda f, z, part, old=old: old[f, z, part]
            side_from = lambda f, z, part, old=old: old[2 + f, z, part]
        new = buffers[(s + 1) % 2]

        def main_to(f, z, part, value, new=new):
            new[f, z, part] = value

        def side_to(f, z, part, value, new=new):
            new[2 + f, z, part] = value

        def last_to(f, z, part, value):
            predicted[f, z - DEEP] = value
            increment[f, pl.ds(z - DEEP, STEPS, stride=STEPS), :] = observed[f, z - DEEP] - value

        first, last = (DEEP - reach, DEEP + STEPS + reach - 1)
        if reach == 0:
            layer = sweep(main_from, side_from, last_to, None, inside, None)
            lax.fori_loop(first, last + 1, layer, 0, unroll=8)
        else:
            outermost = sweep(main_from, side_from, main_to, None, inside, None)
            outermost(first, 0)
            outermost(last, 0)
            layer = sweep(main_from, side_from, main_to, side_to, everywhere, everywhere)
            lax.fori_loop(first + 1, last, layer, 0, unroll=8)

    def weight(i, g):
        return wx[g // 2, i, pl.ds(8 * (g % 2), 8)]

    def put(i, g, value):
        passed[i, pl.ds(8 * g, 8)] = value

    def value(i, g):
        return increment[g // 2, pl.ds(STEPS * i + 8 * (g % 2), 8)]

    low = forward(value, weight, zeros(), put)
    high = backward(lambda i, g: passed[i, pl.ds(8 * g, 8)], weight, zeros(), lambda i, g, value: None)
    for g in range(4):
        for k in range(4):
            ends[k, pl.ds(8 * g, 8)] = low[g][k]
            ends[4 + k, pl.ds(8 * g, 8)] = high[g][k]


GROUPS = [pl.ds(8 * g, 8) for g in range(4)]


def values_of(ref, rows, count):
    return [ref[v, rows] for v in range(count)]


def no_state(rows=8):
    return [jnp.zeros((rows, 128), F32)] * 4


def laid_end_to_end(first, second):
    return [sum(first[k - m] * second[m] for m in range(k + 1)) for k in range(4)]


def run_maps_kernel(place, maps_0, maps_1, maps_2, maps_3, joint, around):
    maps = (maps_0, maps_1, maps_2, maps_3)
    for p in range(4):

        @pl.when(place[0] % 4 == p)
        def _(p=p):
            for rows in GROUPS:
                run = [values_of(maps[j ^ p], rows, 14) for j in range(4)]
                zero = jnp.zeros((8, 128), F32)
                unit = [zero + 1.0] + [zero] * 3
                before = unit
                for j in range(p):
                    before = laid_end_to_end(before, run[j][:4])
                through = laid_end_to_end(before, run[p][:4])
                after = merged_maps(run[p + 1 :]) if p < 3 else unit + [zero] * 10
                for v, value in enumerate(merged_maps(run)[4:]):
                    joint[v, rows] = value
                for v, value in enumerate(before + through + after):
                    around[v, rows] = value


def run_ends_kernel(place, maps_0, maps_1, maps_2, maps_3, ends_0, ends_3, ends_2, ends_1, _, joint, inner):
    maps, ends = ((maps_0, maps_1, maps_2, maps_3), (ends_0, ends_1, ends_2, ends_3))
    for p in range(4):

        @pl.when(place[0] % 4 == p)
        def _(p=p):
            for rows in GROUPS:
                lows, highs = chained(
                    [values_of(maps[j ^ p], rows, 14) for j in range(4)],
                    [values_of(ends[j ^ p], rows, 8) for j in range(4)],
                    no_state(),
                    no_state(),
                )
                for k in range(4):
                    joint[k, rows] = lows[4][k]
                    joint[4 + k, rows] = highs[0][k]
                    inner[k, rows] = lows[p][k]
                    inner[4 + k, rows] = highs[p + 1][k]


def outer_inflow(is_high, own_ends, other_ends, other_coupling):
    low = [jnp.where(is_high, value, 0.0) for value in other_ends[:4]]
    back = plus(couple([None] * 4 + other_coupling, own_ends[:4]), other_ends[4:])
    return low, [jnp.where(is_high, 0.0, value) for value in back]


def y_value(ref):
    return lambda i, g: ref[g, pl.ds(i, 8, stride=STEPS)]


def x_finish_kernel(
    place, increment, wx, around, inner, joint, other_joint, other_coupling, wy, my, my_all,
    lines, ends, message, passed, start,
):
    for rows in GROUPS:
        outer_low, outer_high = outer_inflow(
            place[0] >= 4,
            values_of(joint, rows, 8),
            values_of(other_joint, rows, 8),
            values_of(other_coupling, rows, 10),
        )
        maps, inside = (values_of(around, rows, 22), values_of(inner, rows, 8))
        low = plus(inside[:4], pass_map(maps[:4], outer_low))
        back = couple(maps[8:], pass_map(maps[4:8], outer_low))
        high = plus(plus(inside[4:], pass_map(maps[8:], outer_high)), back)
        inflow_writer(start, rows)(low, high)

    def weight(i, g):
        return wx[g // 2, i, pl.ds(8 * (g % 2), 8)]

    def value(i, g):
        return increment[g // 2, pl.ds(STEPS * i + 8 * (g % 2), 8)]

    def put(i, g, value):
        passed[g // 2, pl.ds(STEPS * i + 8 * (g % 2), 8)] = value

    def passed_value(i, g):
        return passed[g // 2, pl.ds(STEPS * i + 8 * (g % 2), 8)]

    low = [[start[k, pl.ds(8 * g, 8)] for k in range(4)] for g in range(4)]
    high = [[start[4 + k, pl.ds(8 * g, 8)] for k in range(4)] for g in range(4)]
    forward(value, weight, low, put)
    backward(passed_value, weight, high, put)
    for f in range(2):
        for h in range(2):
            lines[2 * f + h] = passed[f, pl.ds(128 * h, 128)].T

    def y_put(i, g, value):
        passed[g // 2, pl.ds(128 * (g % 2) + 8 * i, 8)] = value

    def y_passed(i, g):
        return passed[g // 2, pl.ds(128 * (g % 2) + 8 * i, 8)]

    low = forward(y_value(lines), y_value(wy), zeros(), y_put)
    high = backward(y_passed, y_value(wy), zeros(), lambda i, g, value: None)
    for g in range(4):
        for k in range(4):
            ends[k, pl.ds(8 * g, 8)] = low[g][k]
            ends[4 + k, pl.ds(8 * g, 8)] = high[g][k]
    maps = [[my[v, pl.ds(s, 4, stride=8)] for v in range(14)] for s in range(8)]
    block_ends = [[ends[v, pl.ds(s, 4, stride=8)] for v in range(8)] for s in range(8)]
    zero = [jnp.zeros((4, 128), F32)] * 4
    lows, highs = chained(maps, block_ends, zero, zero)
    for k in range(4):
        message[pl.ds(4 * k, 4)] = lows[8][k]
        message[pl.ds(16 + 4 * k, 4)] = highs[0][k]
    message[pl.ds(32, 56)] = my_all[...]


def own_inflow(position, lines):
    count = 4
    for p in range(count):

        @pl.when(position == p)
        def _(p=p):
            for maps, ends, outer_low, outer_high, write in lines:
                low = outer_low
                for j in range(p):
                    low = plus(pass_map(maps(j ^ p), low), ends(j ^ p)[:4])
                inflow, lows = (low, [])
                for j in range(p, count):
                    lows.append(inflow)
                    if j < count - 1:
                        inflow = plus(pass_map(maps(j ^ p), inflow), ends(j ^ p)[:4])
                high = outer_high
                for j in range(count - 1, p, -1):
                    coupled = couple(maps(j ^ p), lows[j - p])
                    high = plus(plus(pass_map(maps(j ^ p), high), coupled), ends(j ^ p)[4:])
                write(low, high)


def inflow_writer(ref, rows):
    def write(low, high):
        for k in range(4):
            ref[k, rows] = low[k]
            ref[4 + k, rows] = high[k]

    return write


def pair_blocks(place, own, partner):
    is_low = place[1] % 2 == 0
    rows = [pl.ds(4 * v, 4) for v in range(22)]
    blocks = (
        [jnp.where(is_low, own[r], partner[r]) for r in rows],
        [jnp.where(is_low, partner[r], own[r]) for r in rows],
    )
    return [b[8:] for b in blocks], [b[:8] for b in blocks]


def y_pair_kernel(place, own, partner, joint):
    maps, ends = pair_blocks(place, own, partner)
    lows, highs = chained(maps, ends, no_state(4), no_state(4))
    for v, value in enumerate(lows[2] + highs[0] + merged_maps(maps)):
        joint[pl.ds(4 * v, 4)] = value


def y_finish_kernel(
    place, lines, wy, my, block_ends, own, partner, joint, other_joint, wz, unsmoothed, message,
    passed, start, done, by_row,
):
    own_joint, other = ([ref[pl.ds(4 * v, 4)] for v in range(22)] for ref in (joint, other_joint))
    outer = outer_inflow(place[1] >= 2, own_joint[:8], other[:8], other[12:])
    pair_lows, pair_highs = chained(*pair_blocks(place, own, partner), *outer)
    is_low = place[1] % 2 == 0
    low = [jnp.where(is_low, a, b) for a, b in zip(pair_lows[0], pair_lows[1])]
    high = [jnp.where(is_low, a, b) for a, b in zip(pair_highs[1], pair_highs[2])]
    maps = [[my[v, pl.ds(s, 4, stride=8)] for v in range(14)] for s in range(8)]
    blocks = [[block_ends[v, pl.ds(s, 4, stride=8)] for v in range(8)] for s in range(8)]
    lows, highs = chained(maps, blocks, low, high)
    for s in range(8):
        for k in range(4):
            start[k, pl.ds(s, 4, stride=8), :] = lows[s][k]
            start[4 + k, pl.ds(s, 4, stride=8), :] = highs[s + 1][k]

    def put(i, g, value):
        passed[g // 2, pl.ds(128 * (g % 2) + 8 * i, 8)] = value

    def passed_value(i, g):
        return passed[g // 2, pl.ds(128 * (g % 2) + 8 * i, 8)]

    def put_line(i, g, value):
        done[g, pl.ds(i, 8, stride=STEPS), :] = value

    low = [[start[k, pl.ds(8 * g, 8)] for k in range(4)] for g in range(4)]
    high = [[start[4 + k, pl.ds(8 * g, 8)] for k in range(4)] for g in range(4)]
    forward(y_value(lines), y_value(wy), low, put)
    backward(passed_value, y_value(wy), high, put_line)
    for g in range(4):
        by_row[g // 2, pl.ds(128 * (g % 2), 128)] = done[g].T

    def value(i, g):
        return by_row[g // 2, pl.ds(i + 128 * (g % 2), 8, stride=STEPS)]

    def weight(i, g):
        return wz[g // 2, i, pl.ds(8 * (g % 2), 8)]

    for i in range(STEPS):
        for g in range(4):
            unsmoothed[g // 2, i, pl.ds(8 * (g % 2), 8)] = value(i, g)

    low = forward(value, weight, zeros(), put)
    high = backward(passed_value, weight, zeros(), lambda i, g, value: None)
    for g in range(4):
        for k in range(4):
            message[k, pl.ds(8 * g, 8)] = low[g][k]
            message[4 + k, pl.ds(8 * g, 8)] = high[g][k]


def z_finish_kernel(
    place, unsmoothed, wz, maps_0, maps_1, maps_2, maps_3, ends_0, ends_3, ends_2, ends_1, smoothed, passed, inflow
):
    maps = (maps_0, maps_1, maps_2, maps_3)
    ends = (ends_0, ends_1, ends_2, ends_3)
    own_inflow(
        place[2],
        [
            (
                lambda s, rows=rows: values_of(maps[s], rows, 14),
                lambda s, rows=rows: values_of(ends[s], rows, 8),
                no_state(),
                no_state(),
                inflow_writer(inflow, rows),
            )
            for rows in GROUPS
        ],
    )
    lows = [[inflow[k, pl.ds(8 * g, 8)] for k in range(4)] for g in range(4)]
    highs = [[inflow[4 + k, pl.ds(8 * g, 8)] for k in range(4)] for g in range(4)]

    def value(i, g):
        return unsmoothed[g // 2, i, pl.ds(8 * (g % 2), 8)]

    def weight(i, g):
        return wz[g // 2, i, pl.ds(8 * (g % 2), 8)]

    def put(i, g, value):
        passed[g // 2, i, pl.ds(8 * (g % 2), 8)] = value

    def put_last(i, g, value):
        smoothed[g // 2, i, pl.ds(8 * (g % 2), 8)] = value

    forward(value, weight, lows, put)
    backward(lambda i, g: passed[g // 2, i, pl.ds(8 * (g % 2), 8)], weight, highs, put_last)


def pair_swaps(axis, spare, value_even, value_odd):
    axes = tuple(sorted((axis, spare)))
    count, others = (lax.axis_size(axis), lax.axis_size(spare))

    def flat(i, k):
        return i * others + k if axis == axes[0] else k * count + i

    odd = []
    for i in range(count):
        for k in range(others):
            j = i + 1 if i % 2 else i - 1
            odd.append((flat(i, k), flat(j, k) if 0 <= j < count else flat(i, k ^ 1)))
    from_even = lax.ppermute(value_even, axis, [(i, i ^ 1) for i in range(count)])
    from_odd = lax.ppermute(value_odd, axes, odd)
    return from_even, from_odd


def xor_swap(value, axis, s):
    return lax.ppermute(value, axis, [(i, i ^ s) for i in range(lax.axis_size(axis))])


def xor_gather(value, axis):
    return [value] + [xor_swap(value, axis, s) for s in (1, 2, 3)]


def local(source, capacity, transfer, observed, classes, conductivity, filter_rates):
    axes = ("gx", "gy", "gz")
    place = jnp.stack([lax.axis_index(a) for a in axes] + [jnp.int32(lax.axis_size(a)) for a in axes])
    rates = filter_rates.reshape(6, CLASSES)
    plane = (STEPS, STEPS, 128)
    units, y_even, y_odd = call(
        coefficients_kernel,
        [(6,) + plane, (8, STEPS, 128), (8, STEPS, 128)],
        [HBM] * 4 + [SMEM],
        [plane, (2,) + plane, (2,) + plane, plane, jax.ShapeDtypeStruct(plane, jnp.int32)],
        limit=60,
        copies=4,
    )(source, capacity, transfer, classes, conductivity)
    y_even, y_odd = pair_swaps("gy", "gz", y_even, y_odd)

    z_face = (7 * NEAR + 2, STEPS, 128)
    x_face = (X_ROWS, 128)
    corners = (2, corner_rows()[1], 128)
    faces = call(face_kernel, [z_face, z_face, x_face, x_face], [SMEM, VMEM])(place, units)
    strips, z_even, z_odd, x_even, x_odd = call(
        halo_kernel,
        [plane, z_face, z_face, x_face, x_face],
        [SMEM] + [VMEM] * 2 + [ANY] * 4,
        [(NEAR,) + plane[1:]] * 2 + [(STEPS * NEAR, 128)] * 2,
        out_specs=[VMEM] + [ANY] * 4,
        aliases={3: 1, 4: 2, 5: 3, 6: 4},
        copies=4,
    )(place, y_odd, y_even, *faces)
    x_even, x_odd = pair_swaps("gx", "gy", x_even, x_odd)
    z_even, z_odd = pair_swaps("gz", "gy", z_even, z_odd)

    rows = (32, 128)
    wx, wy, wz, mx, my, my_all, mz, _, _ = call(
        maps_kernel,
        [(2,) + plane, (4, 128, 128), (2,) + plane, (14,) + rows, (14,) + rows, (56, 128), (14,) + rows,
         (256, 128), (2, 128, 128)],
        [VMEM, SMEM, VMEM],
    )(classes, rates, strips)
    x_odd, wx, mx = lax.optimization_barrier((x_odd, wx, mx))
    map_2 = xor_swap(mx, "gx", 2)
    x_maps = [mx, xor_swap(mx, "gx", 1), map_2]
    corner_even, corner_odd = call(corner_kernel, [corners, corners], [SMEM] + [VMEM] * 4)(
        place, x_odd, x_even, z_odd, observed
    )
    mx, corner_even, z_odd = lax.optimization_barrier((mx, corner_even, z_odd))
    corner_even, corner_odd = pair_swaps("gz", "gy", corner_even, corner_odd)
    x_maps.append(xor_swap(mx, "gx", 3))
    x_maps[1], corner_odd = lax.optimization_barrier((x_maps[1], corner_odd))

    padded = (PLANES, 32, 128)
    predicted, increment, x_ends = call(
        sweep_kernel,
        [(2,) + plane, (2, 256, 128), (8,) + rows],
        [SMEM] + [VMEM] * 10,
        [(7,) + padded, (6,) + padded, (4,) + padded, (4,) + padded, (STEPS,) + rows],
        limit=16,
    )(place, units, strips, z_even, z_odd, x_even, x_odd, corner_even, corner_odd, observed, wx)
    x_all = xor_gather(x_ends, "gx")
    coupling_x, around = call(run_maps_kernel, [(10,) + rows, (22,) + rows], [SMEM] + [VMEM] * 4)(place, *x_maps)
    other_coupling = xor_swap(coupling_x, "gx", 4)
    x_run = x_maps + [x_all[0]] + x_all[:0:-1]
    joint, inner = call(run_ends_kernel, [(8,) + rows] * 2, [SMEM] + [VMEM] * 9)(place, *x_run, increment)
    other_joint = xor_swap(joint, "gx", 4)
    mz, joint = lax.optimization_barrier((mz, joint))
    z_maps = xor_gather(mz, "gz")
    lines, block_ends, y_ends = call(
        x_finish_kernel,
        [(4, 128, 128), (8,) + rows, (88, 128)],
        [SMEM] + [VMEM] * 10,
        [(2, 256, 128), (8,) + rows],
    )(place, increment, wx, around, inner, joint, other_joint, other_coupling, wy, my, my_all)
    y_partner = xor_swap(y_ends, "gy", 1)
    y_joint, = call(y_pair_kernel, [(88, 128)], [SMEM] + [VMEM] * 2)(place, y_ends, y_partner)
    y_other = xor_swap(y_joint, "gy", 2)
    unsmoothed, z_ends = call(
        y_finish_kernel,
        [(2,) + plane, (8,) + rows],
        [SMEM] + [VMEM] * 9,
        [(2, 256, 128), (8,) + rows, (4, 128, 128), (2, 256, 128)],
    )(place, lines, wy, my, block_ends, y_ends, y_partner, y_joint, y_other, wz)
    z_all = xor_gather(z_ends, "gz")
    smoothed, = call(z_finish_kernel, [(2,) + plane], [SMEM] + [VMEM] * 10, [(2,) + plane, (8,) + rows])(
        place, unsmoothed, wz, *z_maps, z_all[0], *z_all[:0:-1]
    )
    return (predicted, smoothed)


def solution(mesh):
    cells = P(None, "gz", "gx", "gy")
    return jax.shard_map(
        local,
        mesh=mesh,
        in_specs=(cells, cells, P("gz", "gx", "gy"), cells, P("gz", "gx", "gy"), P(), P()),
        out_specs=(cells, cells),
        check_vma=False,
    )
```

```python
import jax
import jax.numpy as jnp
from jax import lax
from jax.experimental import pallas as pl
from jax.experimental.pallas import tpu as pltpu
from jax.sharding import PartitionSpec as P

SWEEPS = 8
DEEP = SWEEPS - 1
NEAR = DEEP - 1
CLASSES = 12
STEPS = 16
PLANES = STEPS + 2 * DEEP
F32 = jnp.float32
VMEM = pl.BlockSpec(memory_space=pltpu.VMEM)
SMEM = pl.BlockSpec(memory_space=pltpu.SMEM)
HBM = pl.BlockSpec(memory_space=pltpu.HBM)
ANY = pl.BlockSpec(memory_space=pl.ANY)


def call(body, outs, specs, scratch=(), flops=1000000, limit=4, copies=0, out_specs=None, aliases=None):
    return pl.pallas_call(
        body,
        out_shape=[shape if hasattr(shape, "dtype") else jax.ShapeDtypeStruct(shape, F32) for shape in outs],
        in_specs=specs,
        out_specs=out_specs or [VMEM] * len(outs),
        input_output_aliases=aliases or {},
        scratch_shapes=[
            pltpu.VMEM(*((shape.shape, shape.dtype) if hasattr(shape, "dtype") else (shape, F32)))
            for shape in scratch
        ]
        + [pltpu.SemaphoreType.DMA((copies,))] * (copies > 0),
        compiler_params=pltpu.CompilerParams(vmem_limit_bytes=limit * 1024 * 1024),
        cost_estimate=pl.CostEstimate(flops=flops, bytes_accessed=1000000, transcendentals=0),
    )


def picked(table, row, classes):
    value = jnp.full(classes.shape, table[row, 0], F32)
    for entry in range(1, CLASSES):
        value = jnp.where(classes == entry, table[row, entry], value)
    return value


def lanes(shape):
    return lax.broadcasted_iota(jnp.int32, shape, len(shape) - 1)


def first_mask(lane):
    return (lane % 14 < 7) & (lane < 84)


def last_mask(lane):
    return ((lane % 14 >= 7) & (lane < 70)) | (lane >= 121)


def by_pairs(place, axis, low, high):
    is_even = place[axis] % 2 == 0
    return jnp.where(is_even, high, low), jnp.where(is_even, low, high)


def sides(place, axis, even, odd):
    high, low = by_pairs(place, axis, odd, even)
    return (
        jnp.where(place[axis] > 0, low, 0.0),
        jnp.where(place[axis] < place[axis + 3] - 1, high, 0.0),
    )


def brought(pairs, sems):
    copies = [pltpu.make_async_copy(a, b, sems.at[i]) for i, (a, b) in enumerate(pairs)]
    for copy in copies:
        copy.start()
    for copy in copies:
        copy.wait()


def coefficients_kernel(
    source_in, capacity_in, transfer_in, classes_in, conductivity,
    units, even, odd,
    edges, source, capacity, transfer, classes, sems,
):
    place = {1: lax.axis_index("gy")}
    brought(((source_in, source), (capacity_in, capacity), (transfer_in, transfer), (classes_in, classes)), sems)

    def layer(z, _):
        transfer_z = transfer[z]
        classes_z = classes[z]
        lane = lanes(classes_z.shape)
        packed = jnp.zeros(classes_z.shape, F32)
        for f in range(2):
            conduct = picked(conductivity, f, classes_z)
            inverse = 1.0 / (capacity[f, z] + 6.0 * conduct + transfer_z)
            for unit, value in (
                (f, source[f, z] * inverse),
                (2 + f, conduct * inverse),
                (4 + f, transfer_z * inverse),
            ):
                units[unit, z] = value
                turned = pltpu.roll(value, 14 * unit, 1) if unit else value
                packed = jnp.where((lane - 14 * unit + 7 + 128) % 128 < 14, turned, packed)
        edges[z] = packed
        return 0

    lax.fori_loop(0, STEPS, layer, 0, unroll=8)

    def pair(z, _):
        upper, lower = (edges[z], edges[z + 8])
        lane = lanes(upper.shape)
        to_low = jnp.where(first_mask(lane), upper, pltpu.roll(lower, 121, 1))
        to_high = jnp.where(last_mask(lane), upper, pltpu.roll(lower, 7, 1))
        even[z], odd[z] = by_pairs(place, 1, to_low, to_high)
        return 0

    lax.fori_loop(0, 8, pair, 0, unroll=4)


def counts(unit):
    return DEEP if unit < 2 else NEAR


X_MAIN = sum(counts(unit) for unit in range(6))
X_ROWS = STEPS * (X_MAIN + NEAR)


def face_row(unit, z):
    if unit == 6:
        return STEPS * X_MAIN + z * NEAR
    return z * X_MAIN + sum(counts(u) for u in range(unit))


def corner_rows():
    offset, rows = (0, [])
    for unit in range(7):
        for d in range(NEAR):
            count = NEAR - d if unit < 2 else NEAR - d - 1
            if count > 0:
                rows.append((unit, d, offset, count))
                offset += count
    return rows, -(-offset // 8) * 8


def face_kernel(place, units, z_even, z_odd, x_even, x_odd):
    for d in range(DEEP):
        for unit in range(6 if d < NEAR else 2):
            at = unit * NEAR + d if d < NEAR else 6 * NEAR + unit
            z_even[at], z_odd[at] = by_pairs(place, 2, units[unit, d], units[unit, STEPS - 1 - d])

    for z in range(STEPS):
        for unit in range(6):
            count = counts(unit)
            low, high = (units[unit, z, pl.ds(0, count)], units[unit, z, pl.ds(STEPS - count, count)])
            even, odd = by_pairs(place, 0, low, high)
            x_even[pl.ds(face_row(unit, z), count)] = even
            x_odd[pl.ds(face_row(unit, z), count)] = odd


def halo_kernel(
    place, y_odd, y_even, _z_even, _z_odd, _x_even, _x_odd, strips, z_even, z_odd, x_even, x_odd,
    to_z_even, to_z_odd, to_x_even, to_x_odd, sems,
):
    def pair(z, _):
        low, high = sides(place, 1, y_even[z], y_odd[z])
        first = first_mask(lanes(high.shape))
        strips[z] = jnp.where(first, high, low)
        strips[z + 8] = jnp.where(first, pltpu.roll(high, 7, 1), pltpu.roll(low, 121, 1))
        return 0

    lax.fori_loop(0, 8, pair, 0, unroll=4)
    for d in range(NEAR):
        to_z_even[d], to_z_odd[d] = by_pairs(place, 2, strips[d], strips[STEPS - 1 - d])
    for z in range(STEPS):
        low, high = (strips[z, pl.ds(0, NEAR)], strips[z, pl.ds(STEPS - NEAR, NEAR)])
        even, odd = by_pairs(place, 0, low, high)
        to_x_even[pl.ds(NEAR * z, NEAR)] = even
        to_x_odd[pl.ds(NEAR * z, NEAR)] = odd
    z_part = pl.ds(6 * NEAR + 2, NEAR)
    x_part = pl.ds(STEPS * X_MAIN, STEPS * NEAR)
    brought(
        (
            (to_z_even, z_even.at[z_part]),
            (to_z_odd, z_odd.at[z_part]),
            (to_x_even, x_even.at[x_part]),
            (to_x_odd, x_odd.at[x_part]),
        ),
        sems,
    )


def corner_kernel(place, x_odd, x_even, _z_even, _observed, even, odd):
    for unit, d, offset, count in corner_rows()[0]:
        ends = []
        for z in (d, STEPS - 1 - d):
            first = face_row(unit, z)
            last = first + counts(unit) - count
            low = sides(place, 0, x_even[pl.ds(last, count)], x_odd[pl.ds(last, count)])[0]
            high = sides(place, 0, x_even[pl.ds(first, count)], x_odd[pl.ds(first, count)])[1]
            ends.append((low, high))
        for x_side in range(2):
            to_even, to_odd = by_pairs(place, 2, ends[0][x_side], ends[1][x_side])
            even[x_side, pl.ds(offset, count)] = to_even
            odd[x_side, pl.ds(offset, count)] = to_odd


def forward(read_value, read_weight, state, write, count=4):
    for i in range(STEPS):
        for g in range(count):
            weight = read_weight(i, g)
            value = read_value(i, g)
            keep = 1.0 - weight
            for k in range(4):
                value = keep * state[g][k] + weight * value
                state[g][k] = value
            write(i, g, value)
    return state


def backward(read_value, read_weight, state, write, count=4):
    return forward(
        lambda i, g: read_value(STEPS - 1 - i, g),
        lambda i, g: read_weight(STEPS - 1 - i, g),
        state,
        lambda i, g, value: write(STEPS - 1 - i, g, value),
        count,
    )


def zeros(count=4):
    return [[jnp.zeros((8, 128), F32) for _ in range(4)] for _ in range(count)]


PAIRS = [(a, b) for a in range(4) for b in range(a, 4)]


def block_maps(read_weights):
    def step(i, carries):
        out = []
        for read_weight, carry in zip(read_weights, carries):
            chain, sums = (list(carry[:4]), list(carry[4:]))
            weight = read_weight(i)
            keep = 1.0 - weight
            for k in range(1, 4):
                chain[k] = chain[k] + weight * chain[k - 1]
            scaled = [weight * value for value in chain]
            chain = [keep * value for value in chain]
            sums = [total + scaled[a] * chain[b] for total, (a, b) in zip(sums, PAIRS)]
            out.append(tuple(chain + sums))
        return tuple(out)

    zero = jnp.zeros((8, 128), F32)
    start = (zero + 1.0,) + (zero,) * 13
    return lax.fori_loop(0, STEPS, step, (start,) * len(read_weights), unroll=4)


def pass_map(maps, state):
    return [sum(maps[k - m] * state[m] for m in range(k + 1)) for k in range(4)]


def coupling(maps, a, b):
    return maps[4 + PAIRS.index((min(a, b), max(a, b)))]


def couple(maps, state):
    return [sum(coupling(maps, k, 3 - m) * state[m] for m in range(4)) for k in range(4)]


def plus(left, right):
    return [a + b for a, b in zip(left, right)]


def chained(maps, ends, low, high):
    count = len(maps)
    lows = [low]
    for s in range(count):
        lows.append(plus(pass_map(maps[s], lows[s]), ends[s][:4]))
    highs = [high]
    for s in reversed(range(count)):
        highs.insert(0, plus(plus(pass_map(maps[s], highs[0]), couple(maps[s], lows[s])), ends[s][4:]))
    return lows, highs


def merged_maps(maps):
    chain, total = (list(maps[0][:4]), list(maps[0][4:]))
    for s in range(1, len(maps)):
        part = maps[s]
        half = [
            [sum(chain[i] * coupling(part, a - i, b) for i in range(a + 1)) for b in range(4)]
            for a in range(4)
        ]
        total = [
            value + sum(chain[j] * half[a][b - j] for j in range(b + 1))
            for value, (a, b) in zip(total, PAIRS)
        ]
        chain = [sum(part[k - m] * chain[m] for m in range(k + 1)) for k in range(4)]
    return chain + total


def maps_kernel(classes, rates, _, wx, wy, wz, mx, my, my_all, mz, by_x, turned):
    def by_layer(z, _):
        here = classes[z]
        for f in range(2):
            wz[f, z] = picked(rates, 4 + f, here)
        return 0

    lax.fori_loop(0, STEPS, by_layer, 0, unroll=4)

    def by_row(z, _):
        by_x[pl.ds(z, STEPS, stride=STEPS), :] = classes[z].astype(F32)
        return 0

    lax.fori_loop(0, STEPS, by_row, 0, unroll=4)

    def x_weights(i, _):
        here = by_x[pl.ds(pl.multiple_of(i * STEPS, 8), STEPS)]
        for f in range(2):
            wx[f, i] = picked(rates, f, here)
        return 0

    lax.fori_loop(0, STEPS, x_weights, 0, unroll=4)
    for h in range(2):
        turned[h] = by_x[128 * h : 128 * h + 128].T

    def y_weights(i, _):
        rows = pl.ds(pl.multiple_of(i * 8, 8), 8)
        for h in range(2):
            here = turned[h, rows]
            for f in range(2):
                wy[2 * f + h, rows] = picked(rates, 2 + f, here)
        return 0

    lax.fori_loop(0, STEPS, y_weights, 0, unroll=4)
    for g in range(4):
        part = pl.ds(8 * (g % 2), 8)
        weights = (
            lambda i, g=g: wx[g // 2, i, part],
            lambda i, g=g: wz[g // 2, i, part],
            lambda i, g=g: wy[g, pl.ds(i, 8, stride=STEPS)],
        )
        for out, maps in zip((mx, mz, my), block_maps(weights)):
            for v in range(14):
                out[v, pl.ds(8 * g, 8)] = maps[v]
    blocks = [[my[v, pl.ds(s, 4, stride=8)] for v in range(14)] for s in range(8)]
    for v, value in enumerate(merged_maps(blocks)):
        my_all[pl.ds(4 * v, 4)] = value


def sweep_kernel(
    place, units, strips, z_even, z_odd, x_even, x_odd, corner_even, corner_odd, observed, wx,
    predicted, increment, ends,
    grid, side, even, odd, passed,
):
    inside = slice(8, 8 + STEPS)

    def own(z, _):
        for unit in range(6):
            grid[unit, z + DEEP, inside] = units[unit, z]
        grid[6, z + DEEP, inside] = strips[z]
        return 0

    lax.fori_loop(0, STEPS, own, 0, unroll=2)
    for z in range(STEPS):
        for unit in range(7):
            count = counts(unit)
            rows = pl.ds(face_row(unit, z), count)
            low, high = sides(place, 0, x_even[rows], x_odd[rows])
            grid[unit, z + DEEP, pl.ds(8 - count, count)] = low
            grid[unit, z + DEEP, pl.ds(8 + STEPS, count)] = high
    for d in range(DEEP):
        for unit in range(7 if d < NEAR else 2):
            at = unit * NEAR + d if d < NEAR else 6 * NEAR + unit
            at = 6 * NEAR + 2 + d if unit == 6 else at
            low, high = sides(place, 2, z_even[at], z_odd[at])
            grid[unit, DEEP - 1 - d, inside] = low
            grid[unit, DEEP + STEPS + d, inside] = high
    for unit, d, offset, count in corner_rows()[0]:
        rows = pl.ds(offset, count)
        for x_side, start in enumerate((8 - count, 8 + STEPS)):
            low, high = sides(place, 2, corner_even[x_side, rows], corner_odd[x_side, rows])
            grid[unit, DEEP - 1 - d, pl.ds(start, count)] = low
            grid[unit, DEEP + STEPS + d, pl.ds(start, count)] = high

    def unpack(z, _):
        packed = grid[6, z]
        for unit in range(6):
            side[unit, z] = pltpu.roll(packed, 128 - 14 * unit, 1) if unit else packed
        return 0

    lax.fori_loop(0, PLANES, unpack, 0, unroll=10)

    everywhere = slice(0, 32)

    def sweep(main_from, side_from, main_to, side_to, rows, side_rows):
        def new_value(f, z, part, coefficients, source, here, other, below, above):
            total = source(f, z - 1, part) + source(f, z + 1, part)
            if part == everywhere:
                total = total + (pltpu.roll(here, 1, 0) + pltpu.roll(here, 31, 0))
            else:
                low, high = (slice(part.start - 1, part.stop - 1), slice(part.start + 1, part.stop + 1))
                total = total + (source(f, z, low) + source(f, z, high))
            total = total + (below + above)
            return coefficients[f, z, part] + coefficients[2 + f, z, part] * total + coefficients[4 + f, z, part] * other

        def layer(z, _):
            main = [main_from(f, z, rows) for f in range(2)]
            edge = [side_from(f, z, rows) for f in range(2)]
            lane = lanes(main[0].shape)
            for f in range(2):
                below = (pltpu.roll(main[f], 1, 1), pltpu.roll(edge[f], 1, 1))
                above = (pltpu.roll(main[f], 127, 1), pltpu.roll(edge[f], 127, 1))
                beside = [
                    (jnp.where(lane == 0, below[1 - i], below[i]), jnp.where(lane == 127, above[1 - i], above[i]))
                    for i in range(2)
                ]
                main_to(f, z, rows, new_value(f, z, rows, grid, main_from, main[f], main[1 - f], *beside[0]))
                if side_rows is not None:
                    side_to(f, z, rows, new_value(f, z, rows, side, side_from, edge[f], edge[1 - f], *beside[1]))
            return 0

        return layer

    buffers = (even, odd)
    for s in range(2, SWEEPS + 1):
        reach = SWEEPS - s
        if s == 2:
            main_from, side_from = (lambda f, z, part: grid[f, z, part], lambda f, z, part: side[f, z, part])
        else:
            old = buffers[s % 2]
            main_from = lambda f, z, part, old=old: old[f, z, part]
            side_from = lambda f, z, part, old=old: old[2 + f, z, part]
        new = buffers[(s + 1) % 2]

        def main_to(f, z, part, value, new=new):
            new[f, z, part] = value

        def side_to(f, z, part, value, new=new):
            new[2 + f, z, part] = value

        def last_to(f, z, part, value):
            predicted[f, z - DEEP] = value
            increment[f, pl.ds(z - DEEP, STEPS, stride=STEPS), :] = observed[f, z - DEEP] - value

        first, last = (DEEP - reach, DEEP + STEPS + reach - 1)
        if reach == 0:
            layer = sweep(main_from, side_from, last_to, None, inside, None)
            lax.fori_loop(first, last + 1, layer, 0, unroll=8)
        else:
            outermost = sweep(main_from, side_from, main_to, None, inside, None)
            outermost(first, 0)
            outermost(last, 0)
            layer = sweep(main_from, side_from, main_to, side_to, everywhere, everywhere)
            count = last - first - 1
            even_unroll = min(u for u in range(8, count + 1) if count % u == 0)
            lax.fori_loop(first + 1, last, layer, 0, unroll=even_unroll)

    def weight(i, g):
        return wx[g // 2, i, pl.ds(8 * (g % 2), 8)]

    def put(i, g, value):
        passed[i, pl.ds(8 * g, 8)] = value

    def value(i, g):
        return increment[g // 2, pl.ds(STEPS * i + 8 * (g % 2), 8)]

    low = forward(value, weight, zeros(), put)
    high = backward(lambda i, g: passed[i, pl.ds(8 * g, 8)], weight, zeros(), lambda i, g, value: None)
    for g in range(4):
        for k in range(4):
            ends[k, pl.ds(8 * g, 8)] = low[g][k]
            ends[4 + k, pl.ds(8 * g, 8)] = high[g][k]


GROUPS = [pl.ds(8 * g, 8) for g in range(4)]


def values_of(ref, rows, count):
    return [ref[v, rows] for v in range(count)]


def no_state(rows=8):
    return [jnp.zeros((rows, 128), F32)] * 4


def laid_end_to_end(first, second):
    return [sum(first[k - m] * second[m] for m in range(k + 1)) for k in range(4)]


def run_maps_kernel(place, maps_0, maps_1, maps_2, maps_3, joint, around):
    maps = (maps_0, maps_1, maps_2, maps_3)
    for p in range(4):

        @pl.when(place[0] % 4 == p)
        def _(p=p):
            for rows in GROUPS:
                run = [values_of(maps[j ^ p], rows, 14) for j in range(4)]
                zero = jnp.zeros((8, 128), F32)
                unit = [zero + 1.0] + [zero] * 3
                before = unit
                for j in range(p):
                    before = laid_end_to_end(before, run[j][:4])
                through = laid_end_to_end(before, run[p][:4])
                after = merged_maps(run[p + 1 :]) if p < 3 else unit + [zero] * 10
                for v, value in enumerate(merged_maps(run)[4:]):
                    joint[v, rows] = value
                for v, value in enumerate(before + through + after):
                    around[v, rows] = value


def run_ends_kernel(place, maps_0, maps_1, maps_2, maps_3, ends_0, ends_3, ends_2, ends_1, _, joint, inner):
    maps, ends = ((maps_0, maps_1, maps_2, maps_3), (ends_0, ends_1, ends_2, ends_3))
    for p in range(4):

        @pl.when(place[0] % 4 == p)
        def _(p=p):
            for rows in GROUPS:
                lows, highs = chained(
                    [values_of(maps[j ^ p], rows, 14) for j in range(4)],
                    [values_of(ends[j ^ p], rows, 8) for j in range(4)],
                    no_state(),
                    no_state(),
                )
                for k in range(4):
                    joint[k, rows] = lows[4][k]
                    joint[4 + k, rows] = highs[0][k]
                    inner[k, rows] = lows[p][k]
                    inner[4 + k, rows] = highs[p + 1][k]


def outer_inflow(is_high, own_ends, other_ends, other_coupling):
    low = [jnp.where(is_high, value, 0.0) for value in other_ends[:4]]
    back = plus(couple([None] * 4 + other_coupling, own_ends[:4]), other_ends[4:])
    return low, [jnp.where(is_high, 0.0, value) for value in back]


def y_value(ref):
    return lambda i, g: ref[g, pl.ds(i, 8, stride=STEPS)]


def x_finish_kernel(
    place, increment, wx, around, inner, joint, other_joint, other_coupling, wy, my, my_all,
    lines, ends, message, passed, start,
):
    for rows in GROUPS:
        outer_low, outer_high = outer_inflow(
            place[0] >= 4,
            values_of(joint, rows, 8),
            values_of(other_joint, rows, 8),
            values_of(other_coupling, rows, 10),
        )
        maps, inside = (values_of(around, rows, 22), values_of(inner, rows, 8))
        low = plus(inside[:4], pass_map(maps[:4], outer_low))
        back = couple(maps[8:], pass_map(maps[4:8], outer_low))
        high = plus(plus(inside[4:], pass_map(maps[8:], outer_high)), back)
        inflow_writer(start, rows)(low, high)

    def weight(i, g):
        return wx[g // 2, i, pl.ds(8 * (g % 2), 8)]

    def value(i, g):
        return increment[g // 2, pl.ds(STEPS * i + 8 * (g % 2), 8)]

    def put(i, g, value):
        passed[g // 2, pl.ds(STEPS * i + 8 * (g % 2), 8)] = value

    def passed_value(i, g):
        return passed[g // 2, pl.ds(STEPS * i + 8 * (g % 2), 8)]

    low = [[start[k, pl.ds(8 * g, 8)] for k in range(4)] for g in range(4)]
    high = [[start[4 + k, pl.ds(8 * g, 8)] for k in range(4)] for g in range(4)]
    forward(value, weight, low, put)
    backward(passed_value, weight, high, put)
    for f in range(2):
        for h in range(2):
            lines[2 * f + h] = passed[f, pl.ds(128 * h, 128)].T

    def y_put(i, g, value):
        passed[g // 2, pl.ds(128 * (g % 2) + 8 * i, 8)] = value

    def y_passed(i, g):
        return passed[g // 2, pl.ds(128 * (g % 2) + 8 * i, 8)]

    low = forward(y_value(lines), y_value(wy), zeros(), y_put)
    high = backward(y_passed, y_value(wy), zeros(), lambda i, g, value: None)
    for g in range(4):
        for k in range(4):
            ends[k, pl.ds(8 * g, 8)] = low[g][k]
            ends[4 + k, pl.ds(8 * g, 8)] = high[g][k]
    maps = [[my[v, pl.ds(s, 4, stride=8)] for v in range(14)] for s in range(8)]
    block_ends = [[ends[v, pl.ds(s, 4, stride=8)] for v in range(8)] for s in range(8)]
    zero = [jnp.zeros((4, 128), F32)] * 4
    lows, highs = chained(maps, block_ends, zero, zero)
    for k in range(4):
        message[pl.ds(4 * k, 4)] = lows[8][k]
        message[pl.ds(16 + 4 * k, 4)] = highs[0][k]
    message[pl.ds(32, 56)] = my_all[...]


def own_inflow(position, lines):
    count = 4
    for p in range(count):

        @pl.when(position == p)
        def _(p=p):
            for maps, ends, outer_low, outer_high, write in lines:
                low = outer_low
                for j in range(p):
                    low = plus(pass_map(maps(j ^ p), low), ends(j ^ p)[:4])
                inflow, lows = (low, [])
                for j in range(p, count):
                    lows.append(inflow)
                    if j < count - 1:
                        inflow = plus(pass_map(maps(j ^ p), inflow), ends(j ^ p)[:4])
                high = outer_high
                for j in range(count - 1, p, -1):
                    coupled = couple(maps(j ^ p), lows[j - p])
                    high = plus(plus(pass_map(maps(j ^ p), high), coupled), ends(j ^ p)[4:])
                write(low, high)


def inflow_writer(ref, rows):
    def write(low, high):
        for k in range(4):
            ref[k, rows] = low[k]
            ref[4 + k, rows] = high[k]

    return write


def pair_blocks(place, own, partner):
    is_low = place[1] % 2 == 0
    rows = [pl.ds(4 * v, 4) for v in range(22)]
    blocks = (
        [jnp.where(is_low, own[r], partner[r]) for r in rows],
        [jnp.where(is_low, partner[r], own[r]) for r in rows],
    )
    return [b[8:] for b in blocks], [b[:8] for b in blocks]


def y_pair_kernel(place, own, partner, joint):
    maps, ends = pair_blocks(place, own, partner)
    lows, highs = chained(maps, ends, no_state(4), no_state(4))
    for v, value in enumerate(lows[2] + highs[0] + merged_maps(maps)):
        joint[pl.ds(4 * v, 4)] = value


def y_finish_kernel(
    place, lines, wy, my, block_ends, own, partner, joint, other_joint, wz, unsmoothed, message,
    passed, start, done, by_row,
):
    own_joint, other = ([ref[pl.ds(4 * v, 4)] for v in range(22)] for ref in (joint, other_joint))
    outer = outer_inflow(place[1] >= 2, own_joint[:8], other[:8], other[12:])
    pair_lows, pair_highs = chained(*pair_blocks(place, own, partner), *outer)
    is_low = place[1] % 2 == 0
    low = [jnp.where(is_low, a, b) for a, b in zip(pair_lows[0], pair_lows[1])]
    high = [jnp.where(is_low, a, b) for a, b in zip(pair_highs[1], pair_highs[2])]
    maps = [[my[v, pl.ds(s, 4, stride=8)] for v in range(14)] for s in range(8)]
    blocks = [[block_ends[v, pl.ds(s, 4, stride=8)] for v in range(8)] for s in range(8)]
    lows, highs = chained(maps, blocks, low, high)
    for s in range(8):
        for k in range(4):
            start[k, pl.ds(s, 4, stride=8), :] = lows[s][k]
            start[4 + k, pl.ds(s, 4, stride=8), :] = highs[s + 1][k]

    def put(i, g, value):
        passed[g // 2, pl.ds(128 * (g % 2) + 8 * i, 8)] = value

    def passed_value(i, g):
        return passed[g // 2, pl.ds(128 * (g % 2) + 8 * i, 8)]

    def put_line(i, g, value):
        done[g, pl.ds(i, 8, stride=STEPS), :] = value

    low = [[start[k, pl.ds(8 * g, 8)] for k in range(4)] for g in range(4)]
    high = [[start[4 + k, pl.ds(8 * g, 8)] for k in range(4)] for g in range(4)]
    forward(y_value(lines), y_value(wy), low, put)
    backward(passed_value, y_value(wy), high, put_line)
    for g in range(4):
        by_row[g // 2, pl.ds(128 * (g % 2), 128)] = done[g].T

    def value(i, g):
        return by_row[g // 2, pl.ds(i + 128 * (g % 2), 8, stride=STEPS)]

    def weight(i, g):
        return wz[g // 2, i, pl.ds(8 * (g % 2), 8)]

    for i in range(STEPS):
        for g in range(4):
            unsmoothed[g // 2, i, pl.ds(8 * (g % 2), 8)] = value(i, g)

    low = forward(value, weight, zeros(), put)
    high = backward(passed_value, weight, zeros(), lambda i, g, value: None)
    for g in range(4):
        for k in range(4):
            message[k, pl.ds(8 * g, 8)] = low[g][k]
            message[4 + k, pl.ds(8 * g, 8)] = high[g][k]


def z_finish_kernel(
    place, unsmoothed, wz, maps_0, maps_1, maps_2, maps_3, ends_0, ends_3, ends_2, ends_1, smoothed, passed, inflow
):
    maps = (maps_0, maps_1, maps_2, maps_3)
    ends = (ends_0, ends_1, ends_2, ends_3)
    own_inflow(
        place[2],
        [
            (
                lambda s, rows=rows: values_of(maps[s], rows, 14),
                lambda s, rows=rows: values_of(ends[s], rows, 8),
                no_state(),
                no_state(),
                inflow_writer(inflow, rows),
            )
            for rows in GROUPS
        ],
    )
    lows = [[inflow[k, pl.ds(8 * g, 8)] for k in range(4)] for g in range(4)]
    highs = [[inflow[4 + k, pl.ds(8 * g, 8)] for k in range(4)] for g in range(4)]

    def value(i, g):
        return unsmoothed[g // 2, i, pl.ds(8 * (g % 2), 8)]

    def weight(i, g):
        return wz[g // 2, i, pl.ds(8 * (g % 2), 8)]

    def put(i, g, value):
        passed[g // 2, i, pl.ds(8 * (g % 2), 8)] = value

    def put_last(i, g, value):
        smoothed[g // 2, i, pl.ds(8 * (g % 2), 8)] = value

    forward(value, weight, lows, put)
    backward(lambda i, g: passed[g // 2, i, pl.ds(8 * (g % 2), 8)], weight, highs, put_last)


def pair_swaps(axis, spare, value_even, value_odd):
    axes = tuple(sorted((axis, spare)))
    count, others = (lax.axis_size(axis), lax.axis_size(spare))

    def flat(i, k):
        return i * others + k if axis == axes[0] else k * count + i

    odd = []
    for i in range(count):
        for k in range(others):
            j = i + 1 if i % 2 else i - 1
            odd.append((flat(i, k), flat(j, k) if 0 <= j < count else flat(i, k ^ 1)))
    from_even = lax.ppermute(value_even, axis, [(i, i ^ 1) for i in range(count)])
    from_odd = lax.ppermute(value_odd, axes, odd)
    return from_even, from_odd


def xor_swap(value, axis, s):
    return lax.ppermute(value, axis, [(i, i ^ s) for i in range(lax.axis_size(axis))])


def xor_gather(value, axis):
    return [value] + [xor_swap(value, axis, s) for s in (1, 2, 3)]


def local(source, capacity, transfer, observed, classes, conductivity, filter_rates):
    axes = ("gx", "gy", "gz")
    place = jnp.stack([lax.axis_index(a) for a in axes] + [jnp.int32(lax.axis_size(a)) for a in axes])
    rates = filter_rates.reshape(6, CLASSES)
    plane = (STEPS, STEPS, 128)
    units, y_even, y_odd = call(
        coefficients_kernel,
        [(6,) + plane, (8, STEPS, 128), (8, STEPS, 128)],
        [HBM] * 4 + [SMEM],
        [plane, (2,) + plane, (2,) + plane, plane, jax.ShapeDtypeStruct(plane, jnp.int32)],
        limit=60,
        copies=4,
    )(source, capacity, transfer, classes, conductivity)
    y_even, y_odd = pair_swaps("gy", "gz", y_even, y_odd)

    z_face = (7 * NEAR + 2, STEPS, 128)
    x_face = (X_ROWS, 128)
    corners = (2, corner_rows()[1], 128)
    faces = call(face_kernel, [z_face, z_face, x_face, x_face], [SMEM, VMEM])(place, units)
    strips, z_even, z_odd, x_even, x_odd = call(
        halo_kernel,
        [plane, z_face, z_face, x_face, x_face],
        [SMEM] + [VMEM] * 2 + [ANY] * 4,
        [(NEAR,) + plane[1:]] * 2 + [(STEPS * NEAR, 128)] * 2,
        out_specs=[VMEM] + [ANY] * 4,
        aliases={3: 1, 4: 2, 5: 3, 6: 4},
        copies=4,
    )(place, y_odd, y_even, *faces)
    x_even, x_odd = pair_swaps("gx", "gy", x_even, x_odd)
    z_even, z_odd = pair_swaps("gz", "gy", z_even, z_odd)

    rows = (32, 128)
    wx, wy, wz, mx, my, my_all, mz, _, _ = call(
        maps_kernel,
        [(2,) + plane, (4, 128, 128), (2,) + plane, (14,) + rows, (14,) + rows, (56, 128), (14,) + rows,
         (256, 128), (2, 128, 128)],
        [VMEM, SMEM, VMEM],
    )(classes, rates, strips)
    x_odd, wx, mx = lax.optimization_barrier((x_odd, wx, mx))
    map_2 = xor_swap(mx, "gx", 2)
    x_maps = [mx, xor_swap(mx, "gx", 1), map_2]
    corner_even, corner_odd = call(corner_kernel, [corners, corners], [SMEM] + [VMEM] * 4)(
        place, x_odd, x_even, z_odd, observed
    )
    mx, corner_even, z_odd = lax.optimization_barrier((mx, corner_even, z_odd))
    corner_even, corner_odd = pair_swaps("gz", "gy", corner_even, corner_odd)
    x_maps.append(xor_swap(mx, "gx", 3))
    x_maps[1], corner_odd = lax.optimization_barrier((x_maps[1], corner_odd))

    padded = (PLANES, 32, 128)
    predicted, increment, x_ends = call(
        sweep_kernel,
        [(2,) + plane, (2, 256, 128), (8,) + rows],
        [SMEM] + [VMEM] * 10,
        [(7,) + padded, (6,) + padded, (4,) + padded, (4,) + padded, (STEPS,) + rows],
        limit=16,
    )(place, units, strips, z_even, z_odd, x_even, x_odd, corner_even, corner_odd, observed, wx)
    x_all = xor_gather(x_ends, "gx")
    coupling_x, around = call(run_maps_kernel, [(10,) + rows, (22,) + rows], [SMEM] + [VMEM] * 4)(place, *x_maps)
    other_coupling = xor_swap(coupling_x, "gx", 4)
    x_run = x_maps + [x_all[0]] + x_all[:0:-1]
    joint, inner = call(run_ends_kernel, [(8,) + rows] * 2, [SMEM] + [VMEM] * 9)(place, *x_run, increment)
    other_joint = xor_swap(joint, "gx", 4)
    mz, joint = lax.optimization_barrier((mz, joint))
    z_maps = xor_gather(mz, "gz")
    lines, block_ends, y_ends = call(
        x_finish_kernel,
        [(4, 128, 128), (8,) + rows, (88, 128)],
        [SMEM] + [VMEM] * 10,
        [(2, 256, 128), (8,) + rows],
    )(place, increment, wx, around, inner, joint, other_joint, other_coupling, wy, my, my_all)
    y_partner = xor_swap(y_ends, "gy", 1)
    y_joint, = call(y_pair_kernel, [(88, 128)], [SMEM] + [VMEM] * 2)(place, y_ends, y_partner)
    y_other = xor_swap(y_joint, "gy", 2)
    unsmoothed, z_ends = call(
        y_finish_kernel,
        [(2,) + plane, (8,) + rows],
        [SMEM] + [VMEM] * 9,
        [(2, 256, 128), (8,) + rows, (4, 128, 128), (2, 256, 128)],
    )(place, lines, wy, my, block_ends, y_ends, y_partner, y_joint, y_other, wz)
    z_all = xor_gather(z_ends, "gz")
    smoothed, = call(z_finish_kernel, [(2,) + plane], [SMEM] + [VMEM] * 10, [(2,) + plane, (8,) + rows])(
        place, unsmoothed, wz, *z_maps, z_all[0], *z_all[:0:-1]
    )
    return (predicted, smoothed)


def solution(mesh):
    cells = P(None, "gz", "gx", "gy")
    return jax.shard_map(
        local,
        mesh=mesh,
        in_specs=(cells, cells, P("gz", "gx", "gy"), cells, P("gz", "gx", "gy"), P(), P()),
        out_specs=(cells, cells),
        check_vma=False,
    )
```
